128 devices in a mesh: dp: 16 (over z, x), tensor: 8 (over y, core).
Axes of the slice: x: 4, y: 4, z: 4, core: 2. Of those that a mesh axis runs over, the one named last changes fastest.
Arguments:
- tokens_in: bfloat16 [8192, 4096], P('dp'), may hold values from -6 to 6
- teacher_hidden: bfloat16 [8192, 12288], P('dp', 'tensor'), may hold values from -6 to 6
- up_old: bfloat16 [6144, 12288], P('dp', 'tensor'), may hold values from -0.09375 to 0.09375
- gain_old: float32 [6144], replicated, may hold values from 0.25 to 1.75
- keep_chan: int32 [4096], replicated, may hold values from 0 to 6143, as said below
- keep_ff: int32 [8192], replicated, may hold values from 0 to 12287, as said below
Outputs:
- grad_up: float32 [4096, 8192], P('dp', 'tensor')
The draws below stay inside these ranges and needn't reach their ends.
Inputs may be any that keep to these rules, and one draw needn't show every extreme that they name: Distinct old hidden units. Entry j has new owner j // 1024 and old owner keep_ff[j] // 1536; at most 256 entries of one new owner have one old owner, and some pair reaches it. Each new owner takes entries from every old owner but one. Every old owner has exactly 1024 entries in all. `keep_chan`: distinct old channels. At most 320 entries lie in one aligned block of 384 old channels, and some block reaches it.
All inputs are finite; a program needn't handle non-finite values.
Results may differ from the reference program's by a relative error of at most 0.019.
Values may be sent and summed in bfloat16 or wider, within the bound.
A program may use at most 128 MiB of HBM per device.

```python
import math
import jax
import jax.numpy as jnp
from jax import lax

D_OLD = 6144
D = 4096
FFO = 12288
FF = 8192
TOK_DEV = 512
TOKENS = 8192
FFO_DEV = 1536
FF_DEV = 1024
D_OLD_DEV = 384
N_DP = 16


def offsets(key, owners, top):
    pairs = (owners - 2) // 2
    values = jax.random.randint(key, (max(pairs, 1),), 0, top)[:pairs]
    tail = jnp.stack([values, -values], axis=1).reshape(-1)
    head = jnp.array([top, -top], jnp.int32)
    return jnp.concatenate([head, tail.astype(jnp.int32)])


def draw_keep_ff(key, part):
    key = jax.random.fold_in(key, 11)
    owners = FFO // FFO_DEV
    average = FF_DEV // owners
    key_a, key_b, key_c, key_d = jax.random.split(key, 4)
    pattern = offsets(key_a, owners, average)
    shift_by = jax.random.randint(key_b, (), 0, owners)
    new_side = jnp.arange(owners)[:, None]
    old_side = jnp.arange(owners)[None, :]
    counts = average + pattern[(old_side - new_side - shift_by) % owners]
    starts = jnp.cumsum(counts, axis=0) - counts
    ends = jnp.cumsum(counts, axis=1)
    begins = ends - counts
    orders = jax.vmap(lambda k: jax.random.permutation(k, FFO_DEV))(jax.random.split(key_c, owners))
    places = jnp.arange(FF_DEV)
    source = jnp.sum(ends[:, None, :] <= places[None, :, None], axis=2)
    within = places[None, :] - jnp.take_along_axis(begins, source, axis=1)
    local = orders[source, jnp.take_along_axis(starts, source, axis=1) + within]
    picked = source * FFO_DEV + local
    mixing = jax.vmap(lambda k: jax.random.permutation(k, FF_DEV))(jax.random.split(key_d, owners))
    picked = jnp.take_along_axis(picked, mixing, axis=1)
    return picked.reshape(-1).astype(jnp.int32)


def draw_keep_chan(key, part):
    key = jax.random.fold_in(key, 23)
    shards = D_OLD // D_OLD_DEV
    average = D // shards
    key_a, key_b, key_c, key_d = jax.random.split(key, 4)
    pattern = offsets(key_a, shards, average // 4)
    shift_by = jax.random.randint(key_b, (), 0, shards)
    counts = average + pattern[(jnp.arange(shards) - shift_by) % shards]
    ends = jnp.cumsum(counts)
    begins = ends - counts
    orders = jax.vmap(lambda k: jax.random.permutation(k, D_OLD_DEV))(jax.random.split(key_c, shards))
    places = jnp.arange(D)
    source = jnp.sum(ends[None, :] <= places[:, None], axis=1)
    within = places - begins[source]
    picked = source * D_OLD_DEV + orders[source, within]
    mixing = jax.random.permutation(key_d, D)
    return picked[mixing].astype(jnp.int32)


def block_scale(stream_key, shape, cuts, low, largest):
    def one(dim, shards_of):
        heights = jax.random.uniform(jax.random.fold_in(jax.random.fold_in(stream_key, 6), dim), (shards_of,), jnp.float32, low / len(cuts), largest / len(cuts))
        return jnp.repeat(jnp.exp(heights), shape[dim] // shards_of).reshape((-1,) + (1,) * (len(shape) - dim - 1))

    level = one(*cuts[0])
    for cut in cuts[1:]:
        level = level * one(*cut)
    return level


def centred(own_key, shape, scale, reach, cuts=(), kind=jnp.bfloat16):
    entries = jax.random.normal(own_key, shape, jnp.float32) * scale
    if len(cuts) > 0:
        entries = block_scale(own_key, shape, cuts, -0.22, 0.18) * entries
    return jnp.clip(entries, min=-reach, max=reach).astype(kind)


def setup_inputs(seed: int = 0) -> dict:
    keys = jax.random.split(jax.random.key(seed), 7)
    tokens_in = centred(keys[0], (TOKENS, D), 1.0, 6.0, ((0, 16),))
    teacher_hidden = centred(keys[1], (TOKENS, FFO), 1.0, 6.0, ((0, 16), (1, 8)))
    up_old = centred(keys[2], (D_OLD, FFO), D ** -0.5, 0.09375, ((0, 16), (1, 8)))
    gain_old = jnp.clip(1.0 + 0.15 * jax.random.normal(keys[3], (D_OLD,), jnp.float32), 0.25, 1.75)
    keep_chan = draw_keep_chan(jax.random.fold_in(keys[6], 71), 0)
    keep_ff = draw_keep_ff(jax.random.fold_in(keys[6], 71), 0)
    return dict(tokens_in=tokens_in, teacher_hidden=teacher_hidden, up_old=up_old, gain_old=gain_old, keep_chan=keep_chan, keep_ff=keep_ff)


def reference(tokens_in, teacher_hidden, up_old, gain_old, keep_chan, keep_ff):
    up_new = jnp.take(jnp.take(up_old, keep_chan, axis=0), keep_ff, axis=1)
    gain = jnp.take(gain_old, keep_chan)
    scale = 1.0 / math.sqrt(TOKENS)
    blocks_x = tokens_in.reshape(N_DP, TOK_DEV, D)
    blocks_t = teacher_hidden.reshape(N_DP, TOK_DEV, FFO)

    def step(total, pair):
        block_x, block_t = pair
        values = block_x.astype(jnp.float32)
        center = lax.optimization_barrier(jnp.mean(values, axis=1, keepdims=True))
        spread = lax.optimization_barrier(jnp.mean((values - center) ** 2, axis=1, keepdims=True))
        normed = ((values - center) * lax.rsqrt(spread + 1e-05) * gain).astype(jnp.bfloat16)
        pre = jnp.dot(normed, up_new, preferred_element_type=jnp.float32)
        active = jnp.maximum(pre, 0.0)
        target = jnp.take(block_t, keep_ff, axis=1).astype(jnp.float32)
        delta = (2.0 * active * (active * active - target) * scale).astype(jnp.bfloat16)
        partial_sum = lax.dot_general(normed, delta, (((0,), (0,)), ((), ())), preferred_element_type=jnp.float32)
        partial_sum = lax.optimization_barrier(partial_sum.astype(jnp.bfloat16)).astype(jnp.float32)
        return (total + partial_sum, None)
    start = jnp.zeros((D, FF), jnp.float32)
    total, unused = lax.scan(step, start, (blocks_x, blocks_t))
    return total
```

```python
import math

import jax
import jax.numpy as jnp
from jax import lax
from jax.experimental import pallas as pl
from jax.experimental.pallas import tpu as pltpu
from jax.sharding import PartitionSpec as P

MESH = pl.DeviceIdType.MESH
SLOT_ROWS = 320
SLOT_COLS = 256
BF16 = jnp.bfloat16
F32 = jnp.float32


def ranks_of(hits):
    rows, width = hits.shape
    chunks = width // 128
    parts = hits.astype(BF16).reshape(rows * chunks, 128)
    before = (jnp.arange(128)[:, None] < jnp.arange(128)[None, :]).astype(BF16)
    within = jnp.dot(parts, before, preferred_element_type=F32).reshape(rows, chunks, 128)
    totals = jnp.sum(hits.astype(F32).reshape(rows, chunks, 128), axis=2).astype(BF16)
    ahead = (jnp.arange(chunks)[:, None] < jnp.arange(chunks)[None, :]).astype(BF16)
    starts = jnp.dot(totals, ahead, preferred_element_type=F32)
    return (within + starts[:, :, None]).reshape(rows, width).astype(jnp.int32)


def kernel(
    scale,
    tokens_hbm, teacher_hbm, up_ref, gain_ref, cols_ref, rowsel_ref, from_ref, pos_hbm,
    out_ref,
    normed, normed_t, packed_x, weights, teacher, kept_rows, weight_send, weight_recv,
    target_send, target_recv, unpack, places, pick, pre, delta, target, ring_b, ring_a,
    local_sems, ws_send, ws_recv, ts_send, ts_recv, ag_send, ag_recv, rs_send, rs_recv,
):
    dp = lax.axis_index("dp")
    owner = lax.axis_index("tensor")
    core = owner % 2
    z, x = dp // 4, dp % 4
    a = x + core * (z - x)
    b = z + core * (x - z)

    def dp_of(ao, bo):
        aa, bb = (a + ao) % 4, (b + bo) % 4
        return bb * 4 + aa + core * 3 * (aa - bb)

    def device(ao, bo):
        return (dp_of(ao, bo), owner)

    load_tokens = pltpu.make_async_copy(tokens_hbm, packed_x.at[:, pl.ds(0, 4096)], local_sems.at[0])
    load_teacher = pltpu.make_async_copy(teacher_hbm, teacher, local_sems.at[1])
    load_places = pltpu.make_async_copy(pos_hbm, places, local_sems.at[2])
    load_teacher.start()
    load_tokens.start()
    load_places.start()
    barrier = pltpu.get_barrier_semaphore()
    for ao, bo in ((1, 0), (3, 0), (0, 1), (0, 3)):
        pl.semaphore_signal(barrier, inc=1, device_id=device(ao, bo), device_id_type=MESH)
    for k in range(1, 8):
        pl.semaphore_signal(barrier, inc=1, device_id=(dp, (owner + k) % 8), device_id_type=MESH)

    rows_hot = (lax.broadcasted_iota(jnp.int32, (SLOT_ROWS, 384), 1) == rowsel_ref[...]).astype(F32).astype(BF16)
    kept_rows[...] = jnp.dot(rows_hot, up_ref[...], preferred_element_type=F32).astype(BF16)
    load_teacher.wait()

    def pack(o, carry):
        hot = (
            lax.broadcasted_iota(jnp.int32, (1536, SLOT_COLS), 0) == cols_ref[pl.ds(o, 1), :]
        ).astype(F32).astype(BF16)
        pick[pl.ds(0, 1536), :] = hot
        weight_send[o] = jnp.dot(kept_rows[...], pick[pl.ds(0, 1536), :], preferred_element_type=F32).astype(BF16)
        target_send[o] = jnp.dot(teacher[...], pick[pl.ds(0, 1536), :], preferred_element_type=F32).astype(BF16)
        return carry

    lax.fori_loop(0, 8, pack, 0)
    pl.semaphore_wait(barrier, 11)

    def weight_copy(k, h):
        peer = (owner + k) % 8
        return pltpu.make_async_remote_copy(
            src_ref=weight_send.at[peer, pl.ds(h * 160, 160), :],
            dst_ref=weight_recv.at[owner, pl.ds(h * 160, 160), :],
            send_sem=ws_send.at[h * 8 + k],
            recv_sem=ws_recv.at[h * 8 + k],
            device_id=(dp, peer),
            device_id_type=MESH,
        )

    def target_copy(k):
        peer = (owner + k) % 8
        return pltpu.make_async_remote_copy(
            src_ref=target_send.at[peer],
            dst_ref=target_recv.at[owner],
            send_sem=ts_send.at[k],
            recv_sem=ts_recv.at[k],
            device_id=(dp, peer),
            device_id_type=MESH,
        )

    for h in range(2):
        for k in (4, 3, 5, 2, 6, 1, 7):
            weight_copy(k, h).start()
    weight_recv[owner] = weight_send[owner]
    target_recv[owner] = target_send[owner]

    def make_unpack(s, carry):
        unpack[pl.ds(pl.multiple_of(s * 256, 256), 256), :] = (
            lax.broadcasted_iota(jnp.int32, (256, 1024), 0) + s * 256 == from_ref[...]
        ).astype(F32).astype(BF16)
        return carry

    lax.fori_loop(0, 8, make_unpack, 0)
    load_tokens.wait()

    def norm(r, carry):
        rows = pl.ds(pl.multiple_of(r * 16, 16), 16)
        values = packed_x[rows, pl.ds(0, 4096)].astype(F32)
        center = jnp.mean(values, axis=1, keepdims=True)
        spread = jnp.mean((values - center) ** 2, axis=1, keepdims=True)
        normed[rows, :] = ((values - center) * lax.rsqrt(spread + 1e-05) * gain_ref[...]).astype(BF16)
        return carry

    def slot_row(ao, bo, h):
        aa, bb = (a + ao) % 4, (b + bo) % 4
        return pl.multiple_of((bb * 4 + aa) * SLOT_ROWS + h * 160, 32)

    ag_started = []

    def ag_copy(ring, step, ao, bo, h):
        far = (ao if ring == 0 else bo) != 0
        role = (4 + h) if far else ((0 if step == 1 else 2) + h)
        index = role if ring == 0 else 6 + ao * 6 + role
        rows = pl.ds(slot_row(ao, bo, h), 160)
        return pltpu.make_async_remote_copy(
            src_ref=weights.at[rows, :],
            dst_ref=weights.at[rows, :],
            send_sem=ag_send.at[len(ag_started)],
            recv_sem=ag_recv.at[index],
            device_id=device(step, 0) if ring == 0 else device(0, step),
            device_id_type=MESH,
        )

    def ag_start(ring, step, ao, bo, h):
        copy = ag_copy(ring, step, ao, bo, h)
        copy.start()
        ag_started.append(copy)

    def ag_wait(ring, ao, bo, h):
        offset = ao if ring == 0 else bo
        role = {3: 0, 1: 2, 2: 4}[offset] + h
        index = role if ring == 0 else 6 + ao * 6 + role
        rows = pl.ds(slot_row(ao, bo, h), 160)
        pltpu.make_async_remote_copy(
            src_ref=weights.at[rows, :],
            dst_ref=weights.at[rows, :],
            send_sem=ag_send.at[0],
            recv_sem=ag_recv.at[index],
            device_id=device(1, 0),
            device_id_type=MESH,
        ).wait_recv()

    lax.fori_loop(0, 16, norm, 0)
    for h in range(2):
        for k in range(1, 8):
            source = (owner - k + 8) % 8
            pltpu.make_async_remote_copy(
                src_ref=weight_recv.at[source, pl.ds(h * 160, 160), :],
                dst_ref=weight_recv.at[source, pl.ds(h * 160, 160), :],
                send_sem=ws_send.at[h * 8 + k],
                recv_sem=ws_recv.at[h * 8 + k],
                device_id=(dp, (owner + k) % 8),
                device_id_type=MESH,
            ).wait_recv()
        total = jnp.zeros((160, 1024), F32)
        for s in range(8):
            total += jnp.dot(
                weight_recv[s, h * 160 : h * 160 + 160, :],
                unpack[s * 256 : s * 256 + 256, :],
                preferred_element_type=F32,
            )
        weights[pl.ds(slot_row(0, 0, h), 160), :] = total.astype(BF16)
        for ring in (0, 1):
            for step in (1, 3):
                ag_start(ring, step, 0, 0, h)
    for k in (4, 3, 5, 2, 6, 1, 7):
        target_copy(k).start()
    lax.fori_loop(16, 32, norm, 0)

    def permute(c, carry):
        start = pl.multiple_of(c * 256, 256)
        lanes = lax.broadcasted_iota(jnp.int32, (4096, 128), 1) + start
        pick[:, pl.ds(0, 128)] = (places[...] == lanes).astype(F32).astype(BF16)
        pick[:, pl.ds(128, 128)] = (places[...] == lanes + 128).astype(F32).astype(BF16)
        packed_x[:, pl.ds(start, 256)] = jnp.dot(normed[...], pick[...], preferred_element_type=F32).astype(BF16)
        return carry

    def permute_group(bo):
        first = ((b + bo) % 4) * 5
        lax.fori_loop(first, first + 5, permute, 0)

    def transpose(ao, bo):
        aa, bb = (a + ao) % 4, (b + bo) % 4
        cols = pl.ds(pl.multiple_of(dp_of(ao, bo) * 256, 256), 256)
        rows = pl.ds(pl.multiple_of((aa * 4 + bb) * 256, 256), 256)
        normed_t[rows, :] = normed[:, cols].T

    def multiply_group(bo, first):
        depth = pl.ds(pl.multiple_of(((b + bo) % 4) * 1280, 256), 1280)

        @pl.loop(0, 4)
        def _(n):
            cols = pl.ds(pl.multiple_of(n * 256, 256), 256)
            part = jnp.dot(packed_x[:, depth], weights[depth, cols], preferred_element_type=F32)
            pre[:, cols] = part if first else pre[:, cols] + part

    load_places.wait()

    for ao, h in ((3, 0), (1, 1), (3, 1), (1, 0)):
        ag_wait(0, ao, 0, h)
        if (ao, h) == (3, 0):
            ag_start(0, 1, 3, 0, 0)
        if (ao, h) == (1, 1):
            ag_start(0, 3, 1, 0, 1)
        ag_start(1, 1, ao, 0, h)
        ag_start(1, 3, ao, 0, h)
    ag_wait(1, 0, 3, 0)
    ag_start(1, 1, 0, 3, 0)
    ag_wait(1, 0, 1, 1)
    ag_start(1, 3, 0, 1, 1)
    for h in range(2):
        ag_wait(0, 2, 0, h)
        ag_start(1, 1, 2, 0, h)
        ag_start(1, 3, 2, 0, h)
    permute_group(0)
    for ao in (3, 1):
        ag_wait(1, ao, 3, 0)
        ag_start(1, 1, ao, 3, 0)
        ag_wait(1, ao, 1, 1)
        ag_start(1, 3, ao, 1, 1)
    permute_group(3)
    ag_wait(1, 2, 3, 0)
    ag_start(1, 1, 2, 3, 0)
    ag_wait(1, 2, 1, 1)
    ag_start(1, 3, 2, 1, 1)
    multiply_group(0, True)
    permute_group(1)
    permute_group(2)

    @pl.loop(0, 16)
    def _(s):
        aa, bb = s // 4, s % 4
        cols = pl.ds(pl.multiple_of((bb * 4 + aa + core * 3 * (aa - bb)) * 256, 256), 256)
        normed_t[pl.ds(pl.multiple_of(s * 256, 256), 256), :] = normed[:, cols].T

    for k in range(1, 8):
        source = (owner - k + 8) % 8
        pltpu.make_async_remote_copy(
            src_ref=target_recv.at[source],
            dst_ref=target_recv.at[source],
            send_sem=ts_send.at[k],
            recv_sem=ts_recv.at[k],
            device_id=(dp, (owner + k) % 8),
            device_id_type=MESH,
        ).wait_recv()

    @pl.loop(0, 4)
    def _(n):
        cols = pl.ds(pl.multiple_of(n * 256, 256), 256)
        total = jnp.zeros((512, 256), F32)
        for s in range(8):
            total += jnp.dot(target_recv[s], unpack[s * 256 : s * 256 + 256, cols], preferred_element_type=F32)
        target[:, cols] = total.astype(BF16)

    for ao in range(4):
        ag_wait(1, ao, 3, 1)
        ag_wait(1, ao, 1, 0)
    multiply_group(3, False)
    multiply_group(1, False)
    for ao in range(4):
        ag_wait(1, ao, 2, 0)
        ag_wait(1, ao, 2, 1)
    multiply_group(2, False)

    @pl.loop(0, 32)
    def _(r):
        rows = pl.ds(pl.multiple_of(r * 16, 16), 16)
        active = jnp.maximum(pre[rows, :], 0.0)
        delta[rows, :] = (2.0 * active * (active * active - target[rows, :].astype(F32)) * scale).astype(BF16)

    for copy in ag_started:
        copy.wait_send()
    for k in range(1, 8):
        for h in range(2):
            weight_copy(k, h).wait_send()
        target_copy(k).wait_send()

    rs_started = []

    def grad_row(ao, bo, h):
        aa, bb = (a + ao) % 4, (b + bo) % 4
        return pl.multiple_of((aa * 4 + bb) * 256 + h * 128, 128)

    def rs_start(ring, step, ao, bo, h, role):
        index = role if ring == 0 else 6 + ao * 6 + role
        place = ring_a.at[pl.ds(role * 128, 128), :] if ring == 0 else ring_b.at[pl.ds((ao * 6 + role) * 128, 128), :]
        copy = pltpu.make_async_remote_copy(
            src_ref=weights.at[pl.ds(grad_row(ao, bo, h), 128), :],
            dst_ref=place,
            send_sem=rs_send.at[len(rs_started)],
            recv_sem=rs_recv.at[index],
            device_id=device(step, 0) if ring == 0 else device(0, step),
            device_id_type=MESH,
        )
        copy.start()
        rs_started.append(copy)

    def rs_take(ring, ao, role):
        index = role if ring == 0 else 6 + ao * 6 + role
        place = ring_a.at[pl.ds(role * 128, 128), :] if ring == 0 else ring_b.at[pl.ds((ao * 6 + role) * 128, 128), :]
        pltpu.make_async_remote_copy(
            src_ref=place,
            dst_ref=place,
            send_sem=rs_send.at[0],
            recv_sem=rs_recv.at[index],
            device_id=device(1, 0),
            device_id_type=MESH,
        ).wait_recv()
        return place

    def add_into(ao, bo, h, places_in, final=False):
        base = grad_row(ao, bo, h)

        @pl.loop(0, 8)
        def _(r):
            total = weights[pl.ds(base + r * 16, 16), :].astype(F32)
            for place in places_in:
                total += place[pl.ds(pl.multiple_of(r * 16, 16), 16), :].astype(F32)
            if final:
                out_ref[pl.ds(pl.multiple_of(h * 128 + r * 16, 16), 16), :] = total
            else:
                weights[pl.ds(base + r * 16, 16), :] = total.astype(BF16)

    def products(ao):
        rows = pl.ds(pl.multiple_of(((a + ao) % 4) * 1024, 1024), 1024)

        @pl.loop(0, 4)
        def _(n):
            cols = pl.ds(pl.multiple_of(n * 256, 256), 256)
            weights[rows, cols] = jnp.dot(
                normed_t[rows, :], delta[:, cols], preferred_element_type=F32
            ).astype(BF16)

    def spread_b(ao):
        rs_start(1, 1, ao, 2, 0, 0)
        rs_start(1, 3, ao, 2, 1, 1)
        rs_start(1, 1, ao, 1, 1, 3)
        rs_start(1, 3, ao, 3, 0, 4)

    def relay_b(ao):
        add_into(ao, 1, 0, [rs_take(1, ao, 0)])
        rs_start(1, 1, ao, 1, 0, 2)
        add_into(ao, 3, 1, [rs_take(1, ao, 1)])
        rs_start(1, 3, ao, 3, 1, 5)

    def gather_b(ao):
        for h in range(2):
            add_into(ao, 0, h, [rs_take(1, ao, 2 + h), rs_take(1, ao, 4 + h)])

    products(2)
    spread_b(2)
    products(1)
    spread_b(1)
    relay_b(2)
    products(3)
    spread_b(3)
    relay_b(1)
    products(0)
    spread_b(0)
    relay_b(3)
    gather_b(2)
    rs_start(0, 1, 2, 0, 0, 0)
    rs_start(0, 3, 2, 0, 1, 1)
    relay_b(0)
    gather_b(1)
    rs_start(0, 1, 1, 0, 1, 3)
    add_into(1, 0, 0, [rs_take(0, 0, 0)])
    rs_start(0, 1, 1, 0, 0, 2)
    gather_b(3)
    rs_start(0, 3, 3, 0, 0, 4)
    add_into(3, 0, 1, [rs_take(0, 0, 1)])
    rs_start(0, 3, 3, 0, 1, 5)
    for h in range(2):
        add_into(
            0, 0, h,
            [rs_take(1, 0, 2 + h), rs_take(1, 0, 4 + h), rs_take(0, 0, 2 + h), rs_take(0, 0, 4 + h)],
            final=True,
        )
    for copy in rs_started:
        copy.wait_send()


def per_device(tokens_in, teacher_hidden, up_old, gain_old, keep_chan, keep_ff):
    dp = lax.axis_index("dp")
    owner = lax.axis_index("tensor")
    core = owner % 2
    scale = 1.0 / math.sqrt(tokens_in.shape[0] * lax.axis_size("dp"))

    blocks = keep_ff.reshape(8, 1024)
    local = blocks - owner * 1536
    mine = (local >= 0) & (local < 1536)
    slot = jnp.where(mine, ranks_of(mine), -1)
    cols = jnp.sum(
        jnp.where(slot[:, None, :] == jnp.arange(SLOT_COLS)[None, :, None], local[:, None, :] + 1, 0), axis=2
    ) - 1

    own = lax.dynamic_slice_in_dim(keep_ff, owner * 1024, 1024)
    source_hits = own[None, :] // 1536 == jnp.arange(8)[:, None]
    where_from = jnp.sum(
        jnp.where(source_hits, ranks_of(source_hits) + jnp.arange(8)[:, None] * SLOT_COLS, 0), axis=0
    )

    block = keep_chan // 384
    block_hits = block[None, :] == jnp.arange(16)[:, None]
    rank = jnp.sum(jnp.where(block_hits, ranks_of(block_hits), 0), axis=0)
    turned = (block % 4) * 4 + block // 4
    order = jnp.where(core == 0, block, turned)
    pos = order * SLOT_ROWS + rank
    pos = jnp.broadcast_to(pos[:, None], (4096, 128))
    rank_here = jnp.where(block == dp, rank, -1)
    rowsel = jnp.sum(
        jnp.where(rank_here[None, :] == jnp.arange(SLOT_ROWS)[:, None], keep_chan[None, :] - dp * 384 + 1, 0),
        axis=1, keepdims=True,
    ) - 1

    high = (keep_chan[None, :] // 128 == jnp.arange(48)[:, None]).astype(F32)
    low = keep_chan[None, :] % 128 == jnp.arange(128)[:, None]
    wide = lax.dot_general(
        gain_old.reshape(48, 128), high, (((0,), (0,)), ((), ())),
        precision=lax.Precision.HIGHEST, preferred_element_type=F32,
    )
    gain = jnp.sum(jnp.where(low, wide, 0.0), axis=0, keepdims=True)

    anywhere = pl.BlockSpec(memory_space=pl.ANY)
    vmem = pl.BlockSpec(memory_space=pltpu.VMEM)
    dma = pltpu.SemaphoreType.DMA

    def body(*refs):
        kernel(scale, *refs)

    return pl.pallas_call(
        body,
        out_shape=jax.ShapeDtypeStruct((256, 1024), F32),
        in_specs=[anywhere, anywhere, vmem, vmem, vmem, vmem, vmem, anywhere],
        out_specs=vmem,
        scratch_shapes=[
            pltpu.VMEM((512, 4096), BF16),
            pltpu.VMEM((4096, 512), BF16),
            pltpu.VMEM((512, 5120), BF16),
            pltpu.VMEM((5120, 1024), BF16),
            pltpu.VMEM((512, 1536), BF16),
            pltpu.VMEM((SLOT_ROWS, 1536), BF16),
            pltpu.VMEM((8, SLOT_ROWS, SLOT_COLS), BF16),
            pltpu.VMEM((8, SLOT_ROWS, SLOT_COLS), BF16),
            pltpu.VMEM((8, 512, SLOT_COLS), BF16),
            pltpu.VMEM((8, 512, SLOT_COLS), BF16),
            pltpu.VMEM((2048, 1024), BF16),
            pltpu.VMEM((4096, 128), jnp.int32),
            pltpu.VMEM((4096, 256), BF16),
            pltpu.VMEM((512, 1024), F32),
            pltpu.VMEM((512, 1024), BF16),
            pltpu.VMEM((512, 1024), BF16),
            pltpu.VMEM((24 * 128, 1024), BF16),
            pltpu.VMEM((6 * 128, 1024), BF16),
            dma((3,)),
            dma((16,)),
            dma((16,)),
            dma((8,)),
            dma((8,)),
            dma((30,)),
            dma((30,)),
            dma((30,)),
            dma((30,)),
        ],
        compiler_params=pltpu.CompilerParams(
            collective_id=0, has_side_effects=True, vmem_limit_bytes=62 * 1024 * 1024
        ),
        cost_estimate=pl.CostEstimate(flops=40_000_000_000, bytes_accessed=10_000_000, transcendentals=0),
    )(tokens_in, teacher_hidden, up_old, gain, cols, rowsel, where_from[None, :], pos)


def solution(mesh):
    return jax.shard_map(
        per_device,
        mesh=mesh,
        in_specs=(P("dp", None), P("dp", "tensor"), P("dp", "tensor"), P(), P(), P()),
        out_specs=P("dp", "tensor"),
        check_vma=False,
    )
```

```python
import math

import jax
import jax.numpy as jnp
from jax import lax
from jax.experimental import pallas as pl
from jax.experimental.pallas import tpu as pltpu
from jax.sharding import PartitionSpec as P

MESH = pl.DeviceIdType.MESH
SLOT_ROWS = 320
SLOT_COLS = 256
BF16 = jnp.bfloat16
F32 = jnp.float32


def strict(shape, dim, group):
    rows = lax.broadcasted_iota(jnp.int32, shape, 0)
    cols = lax.broadcasted_iota(jnp.int32, shape, 1)
    ahead = rows < cols if dim == 1 else cols < rows
    same = rows // group == cols // group
    return jnp.where(ahead & same, 1.0, 0.0).astype(BF16)


def ranks_of(hits, group):
    parts = hits.astype(BF16)
    within = jnp.dot(parts, strict((128, 128), 1, 128), preferred_element_type=F32)
    above = jnp.dot(strict((hits.shape[0],) * 2, 0, group), parts, preferred_element_type=F32)
    return within + jnp.sum(above, axis=1, keepdims=True)


def blocks_of(index, width, count):
    block = jnp.zeros_like(index)
    for edge in range(1, count):
        block += jnp.where(index >= edge * width, 1, 0)
    return block


def kernel(
    scale,
    tokens_hbm, teacher_hbm, up_hbm, gain_ref, chan_ref, ff_ref,
    out_ref,
    normed, normed_t, packed_x, weights, teacher, up, kept_rows, weight_send, weight_recv,
    target_send, target_recv, unpack, picks, pre, delta, target, ring_b, ring_a, gain, places,
    local_sems, ws_send, ws_recv, ts_send, ts_recv, ag_send, ag_recv, rs_send, rs_recv,
):
    dp = lax.axis_index("dp")
    owner = lax.axis_index("tensor")
    core = owner % 2
    z, x = dp // 4, dp % 4
    a = x + core * (z - x)
    b = z + core * (x - z)

    def dp_of(ao, bo):
        aa, bb = (a + ao) % 4, (b + bo) % 4
        return bb * 4 + aa + core * 3 * (aa - bb)

    def device(ao, bo):
        return (dp_of(ao, bo), owner)

    load_up = pltpu.make_async_copy(up_hbm, up, local_sems.at[0])
    load_teacher = pltpu.make_async_copy(teacher_hbm, teacher, local_sems.at[1])
    load_tokens = pltpu.make_async_copy(tokens_hbm, packed_x.at[:, pl.ds(0, 4096)], local_sems.at[2])
    load_up.start()
    load_teacher.start()
    load_tokens.start()
    barrier = pltpu.get_barrier_semaphore()
    for ao, bo in ((1, 0), (3, 0), (0, 1), (0, 3)):
        pl.semaphore_signal(barrier, inc=1, device_id=device(ao, bo), device_id_type=MESH)
    for k in range(1, 8):
        pl.semaphore_signal(barrier, inc=1, device_id=(dp, (owner + k) % 8), device_id_type=MESH)

    chan = chan_ref[...]
    block = blocks_of(chan, 384, 16)
    block_hits = jnp.concatenate([jnp.where(block == s, 1.0, 0.0) for s in range(16)], axis=0)
    block_ranks = ranks_of(block_hits, 32) * block_hits
    rank = block_ranks[0:32, :]
    for s in range(1, 16):
        rank += block_ranks[32 * s : 32 * s + 32, :]
    rank = rank.astype(jnp.int32)
    group = blocks_of(block, 4, 4)
    order = block + core * 3 * (block - group * 5)
    places[0:32, :] = order * SLOT_ROWS + rank
    places[32:64, :] = jnp.where(block == dp, rank, -1)

    slots = lax.broadcasted_iota(jnp.int32, (SLOT_ROWS, 128), 0)
    found = jnp.zeros((SLOT_ROWS, 128), jnp.int32)
    for r in range(32):
        found += jnp.where(places[32 + r : 33 + r, :] == slots, chan_ref[r : r + 1, :] - dp * 384 + 1, 0)
    row = jnp.sum(found.astype(F32), axis=1, keepdims=True).astype(jnp.int32) - 1
    hot = jnp.where(lax.broadcasted_iota(jnp.int32, (SLOT_ROWS, 384), 1) == row, 1.0, 0.0).astype(BF16)
    load_up.wait()
    kept_rows[...] = jnp.dot(hot, up[...], preferred_element_type=F32).astype(BF16)

    places[64:128, :] = ff_ref[...] - owner * 1536
    local = places[64:128, :]
    mine = (local >= 0) & (local < 1536)
    slot = ranks_of(jnp.where(mine, 1.0, 0.0), 8).astype(jnp.int32)
    places[128:192, :] = jnp.where(mine, slot, -1)

    def make_pick(o, carry):
        slots = lax.broadcasted_iota(jnp.int32, (SLOT_COLS, 128), 0)
        found = jnp.zeros((SLOT_COLS, 128), jnp.int32)
        for r in range(8):
            found += jnp.where(
                places[pl.ds(128 + o * 8 + r, 1), :] == slots, places[pl.ds(64 + o * 8 + r, 1), :] + 1, 0
            )
        column = jnp.sum(found.astype(F32), axis=1, keepdims=True).astype(jnp.int32) - 1
        hot = jnp.where(lax.broadcasted_iota(jnp.int32, (SLOT_COLS, 1536), 1) == column, 1.0, 0.0)
        picks[pl.ds(pl.multiple_of(o * 256, 256), 256), :] = hot.astype(BF16)
        return carry

    lax.fori_loop(0, 8, make_pick, 0)

    def picked(rows, o):
        pick = picks[pl.ds(pl.multiple_of(o * 256, 256), 256), :]
        return lax.dot_general(
            rows, pick, (((1,), (1,)), ((), ())), preferred_element_type=F32
        ).astype(BF16)

    def weight_copy(k, h):
        peer = (owner + k) % 8
        return pltpu.make_async_remote_copy(
            src_ref=weight_send.at[peer, pl.ds(h * 160, 160), :],
            dst_ref=weight_recv.at[owner, pl.ds(h * 160, 160), :],
            send_sem=ws_send.at[h * 8 + k],
            recv_sem=ws_recv.at[h * 8 + k],
            device_id=(dp, peer),
            device_id_type=MESH,
        )

    def target_copy(k):
        peer = (owner + k) % 8
        return pltpu.make_async_remote_copy(
            src_ref=target_send.at[peer],
            dst_ref=target_recv.at[owner],
            send_sem=ts_send.at[k],
            recv_sem=ts_recv.at[k],
            device_id=(dp, peer),
            device_id_type=MESH,
        )

    pl.semaphore_wait(barrier, 11)
    for h in range(2):
        for k in (4, 3, 5, 2, 6, 1, 7):
            peer = (owner + k) % 8
            weight_send[peer, pl.ds(h * 160, 160), :] = picked(kept_rows[h * 160 : h * 160 + 160, :], peer)
            weight_copy(k, h).start()
    weight_recv[owner] = picked(kept_rows[...], owner)

    own = ff_ref[pl.ds(pl.multiple_of(owner * 8, 8), 8), :]
    source = blocks_of(own, 1536, 8)
    source_hits = jnp.concatenate([jnp.where(source == s, 1.0, 0.0) for s in range(8)], axis=0)
    source_ranks = ranks_of(source_hits, 8) * source_hits
    arrives = source * SLOT_COLS
    for s in range(8):
        arrives += source_ranks[8 * s : 8 * s + 8, :].astype(jnp.int32)
    places[192:200, :] = arrives

    def make_unpack(s, carry):
        slots = lax.broadcasted_iota(jnp.int32, (256, 128), 0) + s * 256
        for r in range(8):
            hot = jnp.where(places[192 + r : 193 + r, :] == slots, 1.0, 0.0)
            unpack[pl.ds(pl.multiple_of(s * 256, 256), 256), r * 128 : r * 128 + 128] = hot.astype(BF16)
        return carry

    lax.fori_loop(0, 8, make_unpack, 0)

    old = gain_ref[...]
    first = old.astype(BF16)
    second = (old - first.astype(F32)).astype(BF16)
    third = (old - first.astype(F32) - second.astype(F32)).astype(BF16)
    gains = jnp.concatenate([first.astype(F32), second.astype(F32), third.astype(F32)], axis=0).astype(BF16)
    for r in range(32):
        line = chan_ref[r : r + 1, :]
        high = blocks_of(line, 128, 48)
        low = line - high * 128
        hot = jnp.where(lax.broadcasted_iota(jnp.int32, (128, 128), 0) == low, 1.0, 0.0).astype(BF16)
        wide = jnp.dot(gains, hot, preferred_element_type=F32)
        wide = (wide[0:48, :] + wide[48:96, :]) + wide[96:144, :]
        chosen = lax.broadcasted_iota(jnp.int32, (48, 128), 0) == high
        gain[:, r * 128 : r * 128 + 128] = jnp.sum(jnp.where(chosen, wide, 0.0), axis=0, keepdims=True)
    load_tokens.wait()

    def norm(r, carry):
        rows = pl.ds(pl.multiple_of(r * 16, 16), 16)
        values = packed_x[rows, pl.ds(0, 4096)].astype(F32)
        center = jnp.mean(values, axis=1, keepdims=True)
        spread = jnp.mean((values - center) ** 2, axis=1, keepdims=True)
        normed[rows, :] = ((values - center) * lax.rsqrt(spread + 1e-05) * gain[...]).astype(BF16)
        return carry

    def slot_row(ao, bo, h):
        aa, bb = (a + ao) % 4, (b + bo) % 4
        return pl.multiple_of((bb * 4 + aa) * SLOT_ROWS + h * 160, 32)

    ag_started = []

    def ag_copy(ring, step, ao, bo, h):
        far = (ao if ring == 0 else bo) != 0
        role = (4 + h) if far else ((0 if step == 1 else 2) + h)
        index = role if ring == 0 else 6 + ao * 6 + role
        rows = pl.ds(slot_row(ao, bo, h), 160)
        return pltpu.make_async_remote_copy(
            src_ref=weights.at[rows, :],
            dst_ref=weights.at[rows, :],
            send_sem=ag_send.at[len(ag_started)],
            recv_sem=ag_recv.at[index],
            device_id=device(step, 0) if ring == 0 else device(0, step),
            device_id_type=MESH,
        )

    def ag_start(ring, step, ao, bo, h):
        copy = ag_copy(ring, step, ao, bo, h)
        copy.start()
        ag_started.append(copy)

    def ag_wait(ring, ao, bo, h):
        offset = ao if ring == 0 else bo
        role = {3: 0, 1: 2, 2: 4}[offset] + h
        index = role if ring == 0 else 6 + ao * 6 + role
        rows = pl.ds(slot_row(ao, bo, h), 160)
        pltpu.make_async_remote_copy(
            src_ref=weights.at[rows, :],
            dst_ref=weights.at[rows, :],
            send_sem=ag_send.at[0],
            recv_sem=ag_recv.at[index],
            device_id=device(1, 0),
            device_id_type=MESH,
        ).wait_recv()

    lax.fori_loop(0, 32, norm, 0)
    load_teacher.wait()
    target_recv[owner] = picked(teacher[...], owner)
    for k in (4, 3, 5, 2, 6, 1, 7):
        peer = (owner + k) % 8
        target_send[peer] = picked(teacher[...], peer)
    for h in range(2):
        for k in range(1, 8):
            source = (owner - k + 8) % 8
            pltpu.make_async_remote_copy(
                src_ref=weight_recv.at[source, pl.ds(h * 160, 160), :],
                dst_ref=weight_recv.at[source, pl.ds(h * 160, 160), :],
                send_sem=ws_send.at[h * 8 + k],
                recv_sem=ws_recv.at[h * 8 + k],
                device_id=(dp, (owner + k) % 8),
                device_id_type=MESH,
            ).wait_recv()
        total = jnp.zeros((160, 1024), F32)
        for s in range(8):
            total += jnp.dot(
                weight_recv[s, h * 160 : h * 160 + 160, :],
                unpack[s * 256 : s * 256 + 256, :],
                preferred_element_type=F32,
            )
        weights[pl.ds(slot_row(0, 0, h), 160), :] = total.astype(BF16)
        for ring in (0, 1):
            for step in (1, 3):
                ag_start(ring, step, 0, 0, h)
    for k in (4, 3, 5, 2, 6, 1, 7):
        target_copy(k).start()

    def permute(c, carry):
        start = pl.multiple_of(c * 256, 256)
        slots = lax.broadcasted_iota(jnp.int32, (256, 128), 0) + start
        total = jnp.zeros((512, 256), F32)
        for part in range(4):
            hot = jnp.concatenate(
                [
                    jnp.where(places[r : r + 1, :] == slots, 1.0, 0.0).astype(BF16)
                    for r in range(part * 8, part * 8 + 8)
                ],
                axis=1,
            )
            total += lax.dot_general(
                normed[:, part * 1024 : part * 1024 + 1024], hot, (((1,), (1,)), ((), ())), preferred_element_type=F32
            )
        packed_x[:, pl.ds(start, 256)] = total.astype(BF16)
        return carry

    def fill(first, last):
        def one(q, carry):
            return permute((b * 5 + q) % 20, carry)

        lax.fori_loop(first, last, one, 0)

    def multiply_group(bo, first):
        depth = pl.ds(pl.multiple_of(((b + bo) % 4) * 1280, 256), 1280)

        @pl.loop(0, 4)
        def _(n):
            cols = pl.ds(pl.multiple_of(n * 256, 256), 256)
            part = jnp.dot(packed_x[:, depth], weights[depth, cols], preferred_element_type=F32)
            pre[:, cols] = part if first else pre[:, cols] + part

    def relay(ring, ao, bo, h):
        ag_wait(ring, ao, bo, h)
        far = ao if ring == 0 else bo
        if far == 3 and h == 0:
            ag_start(ring, 1, ao, bo, h)
        if far == 1 and h == 1:
            ag_start(ring, 3, ao, bo, h)
        if ring == 0:
            ag_start(1, 1, ao, 0, h)
            ag_start(1, 3, ao, 0, h)

    relay(0, 3, 0, 0)
    relay(0, 1, 0, 0)
    relay(1, 0, 3, 0)
    fill(0, 2)
    relay(0, 1, 0, 1)
    relay(0, 3, 0, 1)
    relay(1, 0, 1, 1)
    fill(2, 4)
    relay(0, 2, 0, 0)
    fill(4, 5)
    relay(0, 2, 0, 1)
    relay(1, 3, 3, 0)
    fill(5, 6)
    relay(1, 3, 1, 1)
    fill(6, 7)
    relay(1, 1, 3, 0)
    fill(7, 8)
    relay(1, 1, 1, 1)
    fill(8, 9)
    relay(1, 2, 3, 0)
    fill(9, 10)
    relay(1, 2, 1, 1)
    fill(10, 20)
    multiply_group(0, True)

    @pl.loop(0, 16)
    def _(s):
        aa, bb = s // 4, s % 4
        cols = pl.ds(pl.multiple_of((bb * 4 + aa + core * 3 * (aa - bb)) * 256, 256), 256)
        normed_t[pl.ds(pl.multiple_of(s * 256, 256), 256), :] = normed[:, cols].T

    for k in range(1, 8):
        source = (owner - k + 8) % 8
        pltpu.make_async_remote_copy(
            src_ref=target_recv.at[source],
            dst_ref=target_recv.at[source],
            send_sem=ts_send.at[k],
            recv_sem=ts_recv.at[k],
            device_id=(dp, (owner + k) % 8),
            device_id_type=MESH,
        ).wait_recv()

    @pl.loop(0, 4)
    def _(n):
        cols = pl.ds(pl.multiple_of(n * 256, 256), 256)
        total = jnp.zeros((512, 256), F32)
        for s in range(8):
            total += jnp.dot(target_recv[s], unpack[s * 256 : s * 256 + 256, cols], preferred_element_type=F32)
        target[:, cols] = total.astype(BF16)

    for ao in range(4):
        ag_wait(1, ao, 3, 1)
        ag_wait(1, ao, 1, 0)
    multiply_group(3, False)
    multiply_group(1, False)
    for ao in range(4):
        ag_wait(1, ao, 2, 0)
        ag_wait(1, ao, 2, 1)
    multiply_group(2, False)

    @pl.loop(0, 32)
    def _(r):
        rows = pl.ds(pl.multiple_of(r * 16, 16), 16)
        active = jnp.maximum(pre[rows, :], 0.0)
        delta[rows, :] = (2.0 * active * (active * active - target[rows, :].astype(F32)) * scale).astype(BF16)

    for copy in ag_started:
        copy.wait_send()
    for k in range(1, 8):
        for h in range(2):
            weight_copy(k, h).wait_send()
        target_copy(k).wait_send()

    rs_started = []

    def grad_row(ao, bo, h):
        aa, bb = (a + ao) % 4, (b + bo) % 4
        return pl.multiple_of((aa * 4 + bb) * 256 + h * 128, 128)

    def rs_start(ring, step, ao, bo, h, role):
        index = role if ring == 0 else 6 + ao * 6 + role
        place = ring_a.at[pl.ds(role * 128, 128), :] if ring == 0 else ring_b.at[pl.ds((ao * 6 + role) * 128, 128), :]
        copy = pltpu.make_async_remote_copy(
            src_ref=weights.at[pl.ds(grad_row(ao, bo, h), 128), :],
            dst_ref=place,
            send_sem=rs_send.at[len(rs_started)],
            recv_sem=rs_recv.at[index],
            device_id=device(step, 0) if ring == 0 else device(0, step),
            device_id_type=MESH,
        )
        copy.start()
        rs_started.append(copy)

    def rs_take(ring, ao, role):
        index = role if ring == 0 else 6 + ao * 6 + role
        place = ring_a.at[pl.ds(role * 128, 128), :] if ring == 0 else ring_b.at[pl.ds((ao * 6 + role) * 128, 128), :]
        pltpu.make_async_remote_copy(
            src_ref=place,
            dst_ref=place,
            send_sem=rs_send.at[0],
            recv_sem=rs_recv.at[index],
            device_id=device(1, 0),
            device_id_type=MESH,
        ).wait_recv()
        return place

    def add_into(ao, bo, h, places_in, final=False):
        base = grad_row(ao, bo, h)

        @pl.loop(0, 8)
        def _(r):
            total = weights[pl.ds(base + r * 16, 16), :].astype(F32)
            for place in places_in:
                total += place[pl.ds(pl.multiple_of(r * 16, 16), 16), :].astype(F32)
            if final:
                out_ref[pl.ds(pl.multiple_of(h * 128 + r * 16, 16), 16), :] = total
            else:
                weights[pl.ds(base + r * 16, 16), :] = total.astype(BF16)

    def products(ao):
        rows = pl.ds(pl.multiple_of(((a + ao) % 4) * 1024, 1024), 1024)

        @pl.loop(0, 4)
        def _(n):
            cols = pl.ds(pl.multiple_of(n * 256, 256), 256)
            weights[rows, cols] = jnp.dot(
                normed_t[rows, :], delta[:, cols], preferred_element_type=F32
            ).astype(BF16)

    def spread_b(ao):
        rs_start(1, 1, ao, 2, 0, 0)
        rs_start(1, 3, ao, 2, 1, 1)
        rs_start(1, 1, ao, 1, 1, 3)
        rs_start(1, 3, ao, 3, 0, 4)

    def relay_b(ao):
        add_into(ao, 1, 0, [rs_take(1, ao, 0)])
        rs_start(1, 1, ao, 1, 0, 2)
        add_into(ao, 3, 1, [rs_take(1, ao, 1)])
        rs_start(1, 3, ao, 3, 1, 5)

    def gather_b(ao):
        for h in range(2):
            add_into(ao, 0, h, [rs_take(1, ao, 2 + h), rs_take(1, ao, 4 + h)])

    products(2)
    spread_b(2)
    products(1)
    spread_b(1)
    relay_b(2)
    products(3)
    spread_b(3)
    relay_b(1)
    products(0)
    spread_b(0)
    relay_b(3)
    gather_b(2)
    rs_start(0, 1, 2, 0, 0, 0)
    rs_start(0, 3, 2, 0, 1, 1)
    relay_b(0)
    gather_b(1)
    rs_start(0, 1, 1, 0, 1, 3)
    add_into(1, 0, 0, [rs_take(0, 0, 0)])
    rs_start(0, 1, 1, 0, 0, 2)
    gather_b(3)
    rs_start(0, 3, 3, 0, 0, 4)
    add_into(3, 0, 1, [rs_take(0, 0, 1)])
    rs_start(0, 3, 3, 0, 1, 5)
    for h in range(2):
        add_into(
            0, 0, h,
            [rs_take(1, 0, 2 + h), rs_take(1, 0, 4 + h), rs_take(0, 0, 2 + h), rs_take(0, 0, 4 + h)],
            final=True,
        )
    for copy in rs_started:
        copy.wait_send()


def per_device(tokens_in, teacher_hidden, up_old, gain_old, keep_chan, keep_ff):
    scale = 1.0 / math.sqrt(tokens_in.shape[0] * lax.axis_size("dp"))
    anywhere = pl.BlockSpec(memory_space=pl.ANY)
    vmem = pl.BlockSpec(memory_space=pltpu.VMEM)
    dma = pltpu.SemaphoreType.DMA

    def body(*refs):
        kernel(scale, *refs)

    return pl.pallas_call(
        body,
        out_shape=jax.ShapeDtypeStruct((256, 1024), F32),
        in_specs=[anywhere, anywhere, anywhere, vmem, vmem, vmem],
        out_specs=vmem,
        scratch_shapes=[
            pltpu.VMEM((512, 4096), BF16),
            pltpu.VMEM((4096, 512), BF16),
            pltpu.VMEM((512, 5120), BF16),
            pltpu.VMEM((5120, 1024), BF16),
            pltpu.VMEM((512, 1536), BF16),
            pltpu.VMEM((384, 1536), BF16),
            pltpu.VMEM((SLOT_ROWS, 1536), BF16),
            pltpu.VMEM((8, SLOT_ROWS, SLOT_COLS), BF16),
            pltpu.VMEM((8, SLOT_ROWS, SLOT_COLS), BF16),
            pltpu.VMEM((8, 512, SLOT_COLS), BF16),
            pltpu.VMEM((8, 512, SLOT_COLS), BF16),
            pltpu.VMEM((2048, 1024), BF16),
            pltpu.VMEM((2048, 1536), BF16),
            pltpu.VMEM((512, 1024), F32),
            pltpu.VMEM((512, 1024), BF16),
            pltpu.VMEM((512, 1024), BF16),
            pltpu.VMEM((24 * 128, 1024), BF16),
            pltpu.VMEM((6 * 128, 1024), BF16),
            pltpu.VMEM((1, 4096), F32),
            pltpu.VMEM((200, 128), jnp.int32),
            dma((3,)),
            dma((16,)),
            dma((16,)),
            dma((8,)),
            dma((8,)),
            dma((30,)),
            dma((30,)),
            dma((30,)),
            dma((30,)),
        ],
        compiler_params=pltpu.CompilerParams(
            collective_id=0, has_side_effects=True, vmem_limit_bytes=62 * 1024 * 1024
        ),
        cost_estimate=pl.CostEstimate(flops=40_000_000_000, bytes_accessed=10_000_000, transcendentals=0),
    )(
        tokens_in, teacher_hidden, up_old,
        gain_old.reshape(48, 128), keep_chan.reshape(32, 128), keep_ff.reshape(64, 128),
    )


def solution(mesh):
    return jax.shard_map(
        per_device,
        mesh=mesh,
        in_specs=(P("dp", None), P("dp", "tensor"), P("dp", "tensor"), P(), P(), P()),
        out_specs=P("dp", "tensor"),
        check_vma=False,
    )
```

```python
import math

import jax
import jax.numpy as jnp
from jax import lax
from jax.experimental import pallas as pl
from jax.experimental.pallas import tpu as pltpu
from jax.sharding import PartitionSpec as P

MESH = pl.DeviceIdType.MESH
SLOT_ROWS = 320
SLOT_COLS = 256
BF16 = jnp.bfloat16
F32 = jnp.float32


def strict(shape, dim, group):
    rows = lax.broadcasted_iota(jnp.int32, shape, 0)
    cols = lax.broadcasted_iota(jnp.int32, shape, 1)
    ahead = rows < cols if dim == 1 else cols < rows
    same = rows // group == cols // group
    return jnp.where(ahead & same, 1.0, 0.0).astype(BF16)


def ranks_of(hits, group):
    parts = hits.astype(BF16)
    within = jnp.dot(parts, strict((128, 128), 1, 128), preferred_element_type=F32)
    above = jnp.dot(strict((hits.shape[0],) * 2, 0, group), parts, preferred_element_type=F32)
    return within + jnp.sum(above, axis=1, keepdims=True)


def blocks_of(index, width, count):
    block = jnp.zeros_like(index)
    for edge in range(1, count):
        block += jnp.where(index >= edge * width, 1, 0)
    return block


def kernel(
    scale,
    tokens_hbm, teacher_hbm, up_hbm, gain_ref, chan_ref, ff_ref,
    out_ref,
    normed, normed_t, packed_x, weights, teacher, up, kept_rows, weight_send, weight_recv,
    target_send, target_recv, unpack, picks, pre, delta, target, ring_b, ring_a, gain, places,
    local_sems, ws_send, ws_recv, ts_send, ts_recv, ag_send, ag_recv, rs_send, rs_recv,
):
    dp = lax.axis_index("dp")
    owner = lax.axis_index("tensor")
    core = owner % 2
    z, x = dp // 4, dp % 4
    a = x + core * (z - x)
    b = z + core * (x - z)

    def dp_of(ao, bo):
        aa, bb = (a + ao) % 4, (b + bo) % 4
        return bb * 4 + aa + core * 3 * (aa - bb)

    def device(ao, bo):
        return (dp_of(ao, bo), owner)

    load_up = pltpu.make_async_copy(up_hbm, up, local_sems.at[0])
    load_teacher = pltpu.make_async_copy(teacher_hbm, teacher, local_sems.at[1])
    load_tokens = pltpu.make_async_copy(tokens_hbm, packed_x.at[:, pl.ds(0, 4096)], local_sems.at[2])
    load_up.start()
    load_teacher.start()
    load_tokens.start()
    barrier = pltpu.get_barrier_semaphore()
    for ao, bo in ((1, 0), (3, 0), (0, 1), (0, 3)):
        pl.semaphore_signal(barrier, inc=1, device_id=device(ao, bo), device_id_type=MESH)
    for k in range(1, 8):
        pl.semaphore_signal(barrier, inc=1, device_id=(dp, (owner + k) % 8), device_id_type=MESH)

    chan = chan_ref[...]
    block = blocks_of(chan, 384, 16)
    block_hits = jnp.concatenate([jnp.where(block == s, 1.0, 0.0) for s in range(16)], axis=0)
    block_ranks = ranks_of(block_hits, 32) * block_hits
    rank = block_ranks[0:32, :]
    for s in range(1, 16):
        rank += block_ranks[32 * s : 32 * s + 32, :]
    rank = rank.astype(jnp.int32)
    group = blocks_of(block, 4, 4)
    order = block + core * 3 * (block - group * 5)
    places[0:32, :] = order * SLOT_ROWS + rank
    places[32:64, :] = jnp.where(block == dp, rank, -1)

    slots = lax.broadcasted_iota(jnp.int32, (SLOT_ROWS, 128), 0)
    found = jnp.zeros((SLOT_ROWS, 128), jnp.int32)
    for r in range(32):
        found += jnp.where(places[32 + r : 33 + r, :] == slots, chan_ref[r : r + 1, :] - dp * 384 + 1, 0)
    row = jnp.sum(found.astype(F32), axis=1, keepdims=True).astype(jnp.int32) - 1
    hot = jnp.where(lax.broadcasted_iota(jnp.int32, (SLOT_ROWS, 384), 1) == row, 1.0, 0.0).astype(BF16)
    load_up.wait()
    kept_rows[...] = jnp.dot(hot, up[...], preferred_element_type=F32).astype(BF16)

    places[64:128, :] = ff_ref[...] - owner * 1536
    local = places[64:128, :]
    mine = (local >= 0) & (local < 1536)
    slot = ranks_of(jnp.where(mine, 1.0, 0.0), 8).astype(jnp.int32)
    places[128:192, :] = jnp.where(mine, slot, -1)

    def make_pick(o, carry):
        slots = lax.broadcasted_iota(jnp.int32, (SLOT_COLS, 128), 0)
        found = jnp.zeros((SLOT_COLS, 128), jnp.int32)
        for r in range(8):
            found += jnp.where(
                places[pl.ds(128 + o * 8 + r, 1), :] == slots, places[pl.ds(64 + o * 8 + r, 1), :] + 1, 0
            )
        column = jnp.sum(found.astype(F32), axis=1, keepdims=True).astype(jnp.int32) - 1
        hot = jnp.where(lax.broadcasted_iota(jnp.int32, (SLOT_COLS, 1536), 1) == column, 1.0, 0.0)
        picks[pl.ds(pl.multiple_of(o * 256, 256), 256), :] = hot.astype(BF16)
        return carry

    lax.fori_loop(0, 8, make_pick, 0)

    def picked(rows, o):
        pick = picks[pl.ds(pl.multiple_of(o * 256, 256), 256), :]
        return lax.dot_general(
            rows, pick, (((1,), (1,)), ((), ())), preferred_element_type=F32
        ).astype(BF16)

    def weight_copy(k, h):
        peer = (owner + k) % 8
        return pltpu.make_async_remote_copy(
            src_ref=weight_send.at[peer, pl.ds(h * 160, 160), :],
            dst_ref=weight_recv.at[owner, pl.ds(h * 160, 160), :],
            send_sem=ws_send.at[h * 8 + k],
            recv_sem=ws_recv.at[h * 8 + k],
            device_id=(dp, peer),
            device_id_type=MESH,
        )

    def target_copy(k):
        peer = (owner + k) % 8
        return pltpu.make_async_remote_copy(
            src_ref=target_send.at[peer],
            dst_ref=target_recv.at[owner],
            send_sem=ts_send.at[k],
            recv_sem=ts_recv.at[k],
            device_id=(dp, peer),
            device_id_type=MESH,
        )

    pl.semaphore_wait(barrier, 11)
    for k in (4, 3, 5, 2, 6, 1, 7):
        peer = (owner + k) % 8
        weight_send[peer] = picked(kept_rows[...], peer)
        weight_copy(k, 0).start()
    for k in (4, 3, 5, 2, 6, 1, 7):
        weight_copy(k, 1).start()
    weight_send[owner] = picked(kept_rows[...], owner)

    own = ff_ref[pl.ds(pl.multiple_of(owner * 8, 8), 8), :]
    source = blocks_of(own, 1536, 8)
    source_hits = jnp.concatenate([jnp.where(source == s, 1.0, 0.0) for s in range(8)], axis=0)
    source_ranks = ranks_of(source_hits, 8) * source_hits
    arrives = source * SLOT_COLS
    for s in range(8):
        arrives += source_ranks[8 * s : 8 * s + 8, :].astype(jnp.int32)
    places[192:200, :] = arrives

    def make_unpack(s, carry):
        slots = lax.broadcasted_iota(jnp.int32, (256, 128), 0) + s * 256
        for r in range(8):
            hot = jnp.where(places[192 + r : 193 + r, :] == slots, 1.0, 0.0)
            unpack[pl.ds(pl.multiple_of(s * 256, 256), 256), r * 128 : r * 128 + 128] = hot.astype(BF16)
        return carry

    lax.fori_loop(0, 8, make_unpack, 0)

    old = gain_ref[...]
    first = old.astype(BF16)
    second = (old - first.astype(F32)).astype(BF16)
    third = (old - first.astype(F32) - second.astype(F32)).astype(BF16)
    gains = jnp.concatenate([first.astype(F32), second.astype(F32), third.astype(F32)], axis=0).astype(BF16)
    for r in range(32):
        line = chan_ref[r : r + 1, :]
        high = blocks_of(line, 128, 48)
        low = line - high * 128
        hot = jnp.where(lax.broadcasted_iota(jnp.int32, (128, 128), 0) == low, 1.0, 0.0).astype(BF16)
        wide = jnp.dot(gains, hot, preferred_element_type=F32)
        wide = (wide[0:48, :] + wide[48:96, :]) + wide[96:144, :]
        chosen = lax.broadcasted_iota(jnp.int32, (48, 128), 0) == high
        gain[:, r * 128 : r * 128 + 128] = jnp.sum(jnp.where(chosen, wide, 0.0), axis=0, keepdims=True)
    load_tokens.wait()

    def norm(r, carry):
        rows = pl.ds(pl.multiple_of(r * 16, 16), 16)
        values = packed_x[rows, pl.ds(0, 4096)].astype(F32)
        center = jnp.mean(values, axis=1, keepdims=True)
        spread = jnp.mean((values - center) ** 2, axis=1, keepdims=True)
        normed[rows, :] = ((values - center) * lax.rsqrt(spread + 1e-05) * gain[...]).astype(BF16)
        return carry

    def slot_row(ao, bo, h):
        aa, bb = (a + ao) % 4, (b + bo) % 4
        return pl.multiple_of((bb * 4 + aa) * SLOT_ROWS + h * 160, 32)

    ag_started = []

    def ag_copy(ring, step, ao, bo, h):
        far = (ao if ring == 0 else bo) != 0
        role = (4 + h) if far else ((0 if step == 1 else 2) + h)
        index = role if ring == 0 else 6 + ao * 6 + role
        rows = pl.ds(slot_row(ao, bo, h), 160)
        return pltpu.make_async_remote_copy(
            src_ref=weights.at[rows, :],
            dst_ref=weights.at[rows, :],
            send_sem=ag_send.at[len(ag_started)],
            recv_sem=ag_recv.at[index],
            device_id=device(step, 0) if ring == 0 else device(0, step),
            device_id_type=MESH,
        )

    def ag_start(ring, step, ao, bo, h):
        copy = ag_copy(ring, step, ao, bo, h)
        copy.start()
        ag_started.append(copy)

    def ag_wait(ring, ao, bo, h):
        offset = ao if ring == 0 else bo
        role = {3: 0, 1: 2, 2: 4}[offset] + h
        index = role if ring == 0 else 6 + ao * 6 + role
        rows = pl.ds(slot_row(ao, bo, h), 160)
        pltpu.make_async_remote_copy(
            src_ref=weights.at[rows, :],
            dst_ref=weights.at[rows, :],
            send_sem=ag_send.at[0],
            recv_sem=ag_recv.at[index],
            device_id=device(1, 0),
            device_id_type=MESH,
        ).wait_recv()

    lax.fori_loop(0, 32, norm, 0)
    load_teacher.wait()
    target_recv[owner] = picked(teacher[...], owner)
    for k in (4, 3, 5, 2, 6, 1, 7):
        peer = (owner + k) % 8
        target_send[peer] = picked(teacher[...], peer)
    for h in range(2):
        half = pl.ds(h * 160, 160)
        for k in (0, 4, 3, 5, 2, 6, 1, 7):
            source = (owner - k + 8) % 8
            table = unpack[pl.ds(pl.multiple_of(source * 256, 256), 256), :]
            if k == 0:
                pre[half, :] = jnp.dot(weight_send[owner, half, :], table, preferred_element_type=F32)
                continue
            pltpu.make_async_remote_copy(
                src_ref=weight_recv.at[source, half, :],
                dst_ref=weight_recv.at[source, half, :],
                send_sem=ws_send.at[h * 8 + k],
                recv_sem=ws_recv.at[h * 8 + k],
                device_id=(dp, (owner + k) % 8),
                device_id_type=MESH,
            ).wait_recv()
            pre[half, :] += jnp.dot(weight_recv[source, half, :], table, preferred_element_type=F32)
        weights[pl.ds(slot_row(0, 0, h), 160), :] = pre[half, :].astype(BF16)
        for ring in (0, 1):
            for step in (1, 3):
                ag_start(ring, step, 0, 0, h)
    for k in (4, 3, 5, 2, 6, 1, 7):
        target_copy(k).start()

    def permute(c, carry):
        start = pl.multiple_of(c * 256, 256)
        slots = lax.broadcasted_iota(jnp.int32, (256, 128), 0) + start
        total = jnp.zeros((512, 256), F32)
        for part in range(4):
            hot = jnp.concatenate(
                [
                    jnp.where(places[r : r + 1, :] == slots, 1.0, 0.0).astype(BF16)
                    for r in range(part * 8, part * 8 + 8)
                ],
                axis=1,
            )
            total += lax.dot_general(
                normed[:, part * 1024 : part * 1024 + 1024], hot, (((1,), (1,)), ((), ())), preferred_element_type=F32
            )
        packed_x[:, pl.ds(start, 256)] = total.astype(BF16)
        return carry

    def fill(first, last):
        def one(q, carry):
            return permute((b * 5 + q) % 20, carry)

        lax.fori_loop(first, last, one, 0)

    def multiply_group(bo, first):
        depth = pl.ds(pl.multiple_of(((b + bo) % 4) * 1280, 256), 1280)

        @pl.loop(0, 4)
        def _(n):
            cols = pl.ds(pl.multiple_of(n * 256, 256), 256)
            part = jnp.dot(packed_x[:, depth], weights[depth, cols], preferred_element_type=F32)
            pre[:, cols] = part if first else pre[:, cols] + part

    def relay(ring, ao, bo, h):
        ag_wait(ring, ao, bo, h)
        far = ao if ring == 0 else bo
        if far == 3 and h == 0:
            ag_start(ring, 1, ao, bo, h)
        if far == 1 and h == 1:
            ag_start(ring, 3, ao, bo, h)
        if ring == 0:
            ag_start(1, 1, ao, 0, h)
            ag_start(1, 3, ao, 0, h)

    fill(0, 4)
    relay(0, 3, 0, 0)
    relay(0, 1, 0, 0)
    relay(1, 0, 3, 0)
    fill(4, 8)
    relay(0, 1, 0, 1)
    relay(0, 3, 0, 1)
    relay(1, 0, 1, 1)
    fill(8, 11)
    relay(0, 2, 0, 0)
    fill(11, 13)
    relay(0, 2, 0, 1)
    relay(1, 3, 3, 0)
    fill(13, 15)
    relay(1, 3, 1, 1)
    relay(1, 1, 3, 0)
    fill(15, 17)
    relay(1, 1, 1, 1)
    fill(17, 20)
    relay(1, 2, 3, 0)
    multiply_group(0, True)
    relay(1, 2, 1, 1)

    @pl.loop(0, 16)
    def _(s):
        aa, bb = s // 4, s % 4
        cols = pl.ds(pl.multiple_of((bb * 4 + aa + core * 3 * (aa - bb)) * 256, 256), 256)
        normed_t[pl.ds(pl.multiple_of(s * 256, 256), 256), :] = normed[:, cols].T

    for k in range(1, 8):
        source = (owner - k + 8) % 8
        pltpu.make_async_remote_copy(
            src_ref=target_recv.at[source],
            dst_ref=target_recv.at[source],
            send_sem=ts_send.at[k],
            recv_sem=ts_recv.at[k],
            device_id=(dp, (owner + k) % 8),
            device_id_type=MESH,
        ).wait_recv()

    @pl.loop(0, 4)
    def _(n):
        cols = pl.ds(pl.multiple_of(n * 256, 256), 256)
        total = jnp.zeros((512, 256), F32)
        for s in range(8):
            total += jnp.dot(target_recv[s], unpack[s * 256 : s * 256 + 256, cols], preferred_element_type=F32)
        target[:, cols] = total.astype(BF16)

    for ao in range(4):
        ag_wait(1, ao, 3, 1)
        ag_wait(1, ao, 1, 0)
    multiply_group(3, False)
    multiply_group(1, False)
    for ao in range(4):
        ag_wait(1, ao, 2, 0)
        ag_wait(1, ao, 2, 1)
    multiply_group(2, False)

    @pl.loop(0, 32)
    def _(r):
        rows = pl.ds(pl.multiple_of(r * 16, 16), 16)
        active = jnp.maximum(pre[rows, :], 0.0)
        delta[rows, :] = (2.0 * active * (active * active - target[rows, :].astype(F32)) * scale).astype(BF16)

    for copy in ag_started:
        copy.wait_send()
    for k in range(1, 8):
        for h in range(2):
            weight_copy(k, h).wait_send()
        target_copy(k).wait_send()

    rs_started = []

    def grad_row(ao, bo, h):
        aa, bb = (a + ao) % 4, (b + bo) % 4
        return pl.multiple_of((aa * 4 + bb) * 256 + h * 128, 128)

    def rs_start(ring, step, ao, bo, h, role):
        index = role if ring == 0 else 6 + ao * 6 + role
        place = ring_a.at[pl.ds(role * 128, 128), :] if ring == 0 else ring_b.at[pl.ds((ao * 6 + role) * 128, 128), :]
        copy = pltpu.make_async_remote_copy(
            src_ref=weights.at[pl.ds(grad_row(ao, bo, h), 128), :],
            dst_ref=place,
            send_sem=rs_send.at[len(rs_started)],
            recv_sem=rs_recv.at[index],
            device_id=device(step, 0) if ring == 0 else device(0, step),
            device_id_type=MESH,
        )
        copy.start()
        rs_started.append(copy)

    def rs_take(ring, ao, role):
        index = role if ring == 0 else 6 + ao * 6 + role
        place = ring_a.at[pl.ds(role * 128, 128), :] if ring == 0 else ring_b.at[pl.ds((ao * 6 + role) * 128, 128), :]
        pltpu.make_async_remote_copy(
            src_ref=place,
            dst_ref=place,
            send_sem=rs_send.at[0],
            recv_sem=rs_recv.at[index],
            device_id=device(1, 0),
            device_id_type=MESH,
        ).wait_recv()
        return place

    def add_into(ao, bo, h, places_in, final=False):
        base = grad_row(ao, bo, h)

        @pl.loop(0, 8)
        def _(r):
            total = weights[pl.ds(base + r * 16, 16), :].astype(F32)
            for place in places_in:
                total += place[pl.ds(pl.multiple_of(r * 16, 16), 16), :].astype(F32)
            if final:
                out_ref[pl.ds(pl.multiple_of(h * 128 + r * 16, 16), 16), :] = total
            else:
                weights[pl.ds(base + r * 16, 16), :] = total.astype(BF16)

    def products(ao):
        rows = pl.ds(pl.multiple_of(((a + ao) % 4) * 1024, 1024), 1024)

        @pl.loop(0, 4)
        def _(n):
            cols = pl.ds(pl.multiple_of(n * 256, 256), 256)
            weights[rows, cols] = jnp.dot(
                normed_t[rows, :], delta[:, cols], preferred_element_type=F32
            ).astype(BF16)

    def spread_b(ao):
        rs_start(1, 1, ao, 2, 0, 0)
        rs_start(1, 3, ao, 2, 1, 1)
        rs_start(1, 1, ao, 1, 1, 3)
        rs_start(1, 3, ao, 3, 0, 4)

    def relay_b(ao):
        add_into(ao, 1, 0, [rs_take(1, ao, 0)])
        rs_start(1, 1, ao, 1, 0, 2)
        add_into(ao, 3, 1, [rs_take(1, ao, 1)])
        rs_start(1, 3, ao, 3, 1, 5)

    def gather_b(ao):
        for h in range(2):
            add_into(ao, 0, h, [rs_take(1, ao, 2 + h), rs_take(1, ao, 4 + h)])

    products(2)
    spread_b(2)
    products(1)
    spread_b(1)
    relay_b(2)
    products(3)
    spread_b(3)
    relay_b(1)
    products(0)
    spread_b(0)
    relay_b(3)
    gather_b(2)
    rs_start(0, 1, 2, 0, 0, 0)
    rs_start(0, 3, 2, 0, 1, 1)
    relay_b(0)
    gather_b(1)
    rs_start(0, 1, 1, 0, 1, 3)
    add_into(1, 0, 0, [rs_take(0, 0, 0)])
    rs_start(0, 1, 1, 0, 0, 2)
    gather_b(3)
    rs_start(0, 3, 3, 0, 0, 4)
    add_into(3, 0, 1, [rs_take(0, 0, 1)])
    rs_start(0, 3, 3, 0, 1, 5)
    for h in range(2):
        add_into(
            0, 0, h,
            [rs_take(1, 0, 2 + h), rs_take(1, 0, 4 + h), rs_take(0, 0, 2 + h), rs_take(0, 0, 4 + h)],
            final=True,
        )
    for copy in rs_started:
        copy.wait_send()


def per_device(tokens_in, teacher_hidden, up_old, gain_old, keep_chan, keep_ff):
    scale = 1.0 / math.sqrt(tokens_in.shape[0] * lax.axis_size("dp"))
    anywhere = pl.BlockSpec(memory_space=pl.ANY)
    vmem = pl.BlockSpec(memory_space=pltpu.VMEM)
    dma = pltpu.SemaphoreType.DMA

    def body(*refs):
        kernel(scale, *refs)

    return pl.pallas_call(
        body,
        out_shape=jax.ShapeDtypeStruct((256, 1024), F32),
        in_specs=[anywhere, anywhere, anywhere, vmem, vmem, vmem],
        out_specs=vmem,
        scratch_shapes=[
            pltpu.VMEM((512, 4096), BF16),
            pltpu.VMEM((4096, 512), BF16),
            pltpu.VMEM((512, 5120), BF16),
            pltpu.VMEM((5120, 1024), BF16),
            pltpu.VMEM((512, 1536), BF16),
            pltpu.VMEM((384, 1536), BF16),
            pltpu.VMEM((SLOT_ROWS, 1536), BF16),
            pltpu.VMEM((8, SLOT_ROWS, SLOT_COLS), BF16),
            pltpu.VMEM((8, SLOT_ROWS, SLOT_COLS), BF16),
            pltpu.VMEM((8, 512, SLOT_COLS), BF16),
            pltpu.VMEM((8, 512, SLOT_COLS), BF16),
            pltpu.VMEM((2048, 1024), BF16),
            pltpu.VMEM((2048, 1536), BF16),
            pltpu.VMEM((512, 1024), F32),
            pltpu.VMEM((512, 1024), BF16),
            pltpu.VMEM((512, 1024), BF16),
            pltpu.VMEM((24 * 128, 1024), BF16),
            pltpu.VMEM((6 * 128, 1024), BF16),
            pltpu.VMEM((1, 4096), F32),
            pltpu.VMEM((200, 128), jnp.int32),
            dma((3,)),
            dma((16,)),
            dma((16,)),
            dma((8,)),
            dma((8,)),
            dma((30,)),
            dma((30,)),
            dma((30,)),
            dma((30,)),
        ],
        compiler_params=pltpu.CompilerParams(
            collective_id=0, has_side_effects=True, vmem_limit_bytes=62 * 1024 * 1024
        ),
        cost_estimate=pl.CostEstimate(flops=40_000_000_000, bytes_accessed=10_000_000, transcendentals=0),
    )(
        tokens_in, teacher_hidden, up_old,
        gain_old.reshape(48, 128), keep_chan.reshape(32, 128), keep_ff.reshape(64, 128),
    )


def solution(mesh):
    return jax.shard_map(
        per_device,
        mesh=mesh,
        in_specs=(P("dp", None), P("dp", "tensor"), P("dp", "tensor"), P(), P(), P()),
        out_specs=P("dp", "tensor"),
        check_vma=False,
    )
```

```python
import math

import jax
import jax.numpy as jnp
from jax import lax
from jax.experimental import pallas as pl
from jax.experimental.pallas import tpu as pltpu
from jax.sharding import PartitionSpec as P

MESH = pl.DeviceIdType.MESH
SLOT_ROWS = 320
SLOT_COLS = 256
BF16 = jnp.bfloat16
F32 = jnp.float32


def strict(shape, dim, group):
    rows = lax.broadcasted_iota(jnp.int32, shape, 0)
    cols = lax.broadcasted_iota(jnp.int32, shape, 1)
    ahead = rows < cols if dim == 1 else cols < rows
    same = rows // group == cols // group
    return jnp.where(ahead & same, 1.0, 0.0).astype(BF16)


def ranks_of(hits, group):
    parts = hits.astype(BF16)
    within = jnp.dot(parts, strict((128, 128), 1, 128), preferred_element_type=F32)
    above = jnp.dot(strict((hits.shape[0],) * 2, 0, group), parts, preferred_element_type=F32)
    return within + jnp.sum(above, axis=1, keepdims=True)


def blocks_of(index, width, count):
    block = jnp.zeros_like(index)
    for edge in range(1, count):
        block += jnp.where(index >= edge * width, 1, 0)
    return block


def kernel(
    scale,
    tokens_hbm, teacher_hbm, up_hbm, gain_ref, chan_ref, ff_ref,
    out_ref,
    normed, normed_t, packed_x, weights, teacher, up, kept_rows, weight_send, weight_recv,
    target_send, target_recv, unpack, picks, pre, delta, target, ring_b, ring_a, gain, places,
    local_sems, ws_send, ws_recv, ts_send, ts_recv, ag_send, ag_recv, rs_send, rs_recv, px_send, px_recv,
):
    dp = lax.axis_index("dp")
    owner = lax.axis_index("tensor")
    core = owner % 2
    z, x = dp // 4, dp % 4
    a = x + core * (z - x)
    b = z + core * (x - z)

    def dp_of(ao, bo):
        aa, bb = (a + ao) % 4, (b + bo) % 4
        return bb * 4 + aa + core * 3 * (aa - bb)

    def device(ao, bo):
        return (dp_of(ao, bo), owner)

    load_up = pltpu.make_async_copy(up_hbm, up, local_sems.at[0])
    load_teacher = pltpu.make_async_copy(teacher_hbm, teacher, local_sems.at[1])
    load_tokens = pltpu.make_async_copy(tokens_hbm, normed, local_sems.at[2])
    load_up.start()
    load_teacher.start()
    load_tokens.start()
    barrier = pltpu.get_barrier_semaphore()
    for ao, bo in ((1, 0), (3, 0), (0, 1), (0, 3)):
        pl.semaphore_signal(barrier, inc=1, device_id=device(ao, bo), device_id_type=MESH)
    for k in range(1, 8):
        pl.semaphore_signal(barrier, inc=1, device_id=(dp, (owner + k) % 8), device_id_type=MESH)

    chan = chan_ref[...]
    block = blocks_of(chan, 384, 16)
    block_hits = jnp.concatenate([jnp.where(block == s, 1.0, 0.0) for s in range(16)], axis=0)
    block_ranks = ranks_of(block_hits, 32) * block_hits
    rank = block_ranks[0:32, :]
    for s in range(1, 16):
        rank += block_ranks[32 * s : 32 * s + 32, :]
    rank = rank.astype(jnp.int32)
    places[0:32, :] = block * SLOT_ROWS + rank
    places[32:64, :] = jnp.where(block == dp, rank, -1)

    slots = lax.broadcasted_iota(jnp.int32, (SLOT_ROWS, 128), 0)
    found = jnp.zeros((SLOT_ROWS, 128), jnp.int32)
    for r in range(32):
        found += jnp.where(places[32 + r : 33 + r, :] == slots, chan_ref[r : r + 1, :] - dp * 384 + 1, 0)
    row = jnp.sum(found.astype(F32), axis=1, keepdims=True).astype(jnp.int32) - 1
    hot = jnp.where(lax.broadcasted_iota(jnp.int32, (SLOT_ROWS, 384), 1) == row, 1.0, 0.0).astype(BF16)
    load_up.wait()
    kept_rows[...] = jnp.dot(hot, up[...], preferred_element_type=F32).astype(BF16)

    places[64:128, :] = ff_ref[...] - owner * 1536
    local = places[64:128, :]
    mine = (local >= 0) & (local < 1536)
    slot = ranks_of(jnp.where(mine, 1.0, 0.0), 8).astype(jnp.int32)
    places[128:192, :] = jnp.where(mine, slot, -1)

    def make_pick(o, carry):
        slots = lax.broadcasted_iota(jnp.int32, (SLOT_COLS, 128), 0)
        found = jnp.zeros((SLOT_COLS, 128), jnp.int32)
        for r in range(8):
            found += jnp.where(
                places[pl.ds(128 + o * 8 + r, 1), :] == slots, places[pl.ds(64 + o * 8 + r, 1), :] + 1, 0
            )
        column = jnp.sum(found.astype(F32), axis=1, keepdims=True).astype(jnp.int32) - 1
        hot = jnp.where(lax.broadcasted_iota(jnp.int32, (SLOT_COLS, 1536), 1) == column, 1.0, 0.0)
        picks[pl.ds(pl.multiple_of(o * 256, 256), 256), :] = hot.astype(BF16)
        return carry

    lax.fori_loop(0, 8, make_pick, 0)

    def picked(rows, o):
        pick = picks[pl.ds(pl.multiple_of(o * 256, 256), 256), :]
        return lax.dot_general(
            rows, pick, (((1,), (1,)), ((), ())), preferred_element_type=F32
        ).astype(BF16)

    def weight_copy(k, h):
        peer = (owner + k) % 8
        return pltpu.make_async_remote_copy(
            src_ref=weight_send.at[peer, pl.ds(h * 160, 160), :],
            dst_ref=weight_recv.at[owner, pl.ds(h * 160, 160), :],
            send_sem=ws_send.at[h * 8 + k],
            recv_sem=ws_recv.at[h * 8 + k],
            device_id=(dp, peer),
            device_id_type=MESH,
        )

    def target_copy(k):
        peer = (owner + k) % 8
        return pltpu.make_async_remote_copy(
            src_ref=target_send.at[peer],
            dst_ref=target_recv.at[owner],
            send_sem=ts_send.at[k],
            recv_sem=ts_recv.at[k],
            device_id=(dp, peer),
            device_id_type=MESH,
        )

    pl.semaphore_wait(barrier, 11)
    for k in (4, 3, 5, 2, 6, 1, 7):
        peer = (owner + k) % 8
        weight_send[peer] = picked(kept_rows[...], peer)
        weight_copy(k, 0).start()
    for k in (4, 3, 5, 2, 6, 1, 7):
        weight_copy(k, 1).start()
    weight_send[owner] = picked(kept_rows[...], owner)

    own = ff_ref[pl.ds(pl.multiple_of(owner * 8, 8), 8), :]
    source = blocks_of(own, 1536, 8)
    source_hits = jnp.concatenate([jnp.where(source == s, 1.0, 0.0) for s in range(8)], axis=0)
    source_ranks = ranks_of(source_hits, 8) * source_hits
    arrives = source * SLOT_COLS
    for s in range(8):
        arrives += source_ranks[8 * s : 8 * s + 8, :].astype(jnp.int32)
    places[192:200, :] = arrives

    def make_unpack(s, carry):
        slots = lax.broadcasted_iota(jnp.int32, (256, 128), 0) + s * 256
        for r in range(8):
            hot = jnp.where(places[192 + r : 193 + r, :] == slots, 1.0, 0.0)
            unpack[pl.ds(pl.multiple_of(s * 256, 256), 256), r * 128 : r * 128 + 128] = hot.astype(BF16)
        return carry

    lax.fori_loop(0, 8, make_unpack, 0)

    old = gain_ref[...]
    first = old.astype(BF16)
    second = (old - first.astype(F32)).astype(BF16)
    third = (old - first.astype(F32) - second.astype(F32)).astype(BF16)
    gains = jnp.concatenate([first.astype(F32), second.astype(F32), third.astype(F32)], axis=0).astype(BF16)
    for r in range(32):
        line = chan_ref[r : r + 1, :]
        high = blocks_of(line, 128, 48)
        low = line - high * 128
        hot = jnp.where(lax.broadcasted_iota(jnp.int32, (128, 128), 0) == low, 1.0, 0.0).astype(BF16)
        wide = jnp.dot(gains, hot, preferred_element_type=F32)
        wide = (wide[0:48, :] + wide[48:96, :]) + wide[96:144, :]
        chosen = lax.broadcasted_iota(jnp.int32, (48, 128), 0) == high
        gain[:, r * 128 : r * 128 + 128] = jnp.sum(jnp.where(chosen, wide, 0.0), axis=0, keepdims=True)
    def norm(r, carry):
        rows = pl.ds(pl.multiple_of(r * 32, 32), 32)
        values = normed[rows, :].astype(F32)
        center = jnp.mean(values, axis=1, keepdims=True)
        spread = jnp.mean((values - center) ** 2, axis=1, keepdims=True)
        normed[rows, :] = ((values - center) * lax.rsqrt(spread + 1e-05) * gain[...]).astype(BF16)
        return carry

    def slot_row(ao, bo, h):
        return pl.multiple_of(dp_of(ao, bo) * SLOT_ROWS + h * 160, 32)

    ag_started = []

    def ag_copy(ring, step, ao, bo, h):
        far = (ao if ring == 0 else bo) != 0
        role = (4 + h) if far else ((0 if step == 1 else 2) + h)
        index = role if ring == 0 else 6 + ao * 6 + role
        rows = pl.ds(slot_row(ao, bo, h), 160)
        return pltpu.make_async_remote_copy(
            src_ref=weights.at[rows, :],
            dst_ref=weights.at[rows, :],
            send_sem=ag_send.at[len(ag_started)],
            recv_sem=ag_recv.at[index],
            device_id=device(step, 0) if ring == 0 else device(0, step),
            device_id_type=MESH,
        )

    def ag_start(ring, step, ao, bo, h):
        copy = ag_copy(ring, step, ao, bo, h)
        copy.start()
        ag_started.append(copy)

    def ag_wait(ring, ao, bo, h):
        offset = ao if ring == 0 else bo
        role = {3: 0, 1: 2, 2: 4}[offset] + h
        index = role if ring == 0 else 6 + ao * 6 + role
        rows = pl.ds(slot_row(ao, bo, h), 160)
        pltpu.make_async_remote_copy(
            src_ref=weights.at[rows, :],
            dst_ref=weights.at[rows, :],
            send_sem=ag_send.at[0],
            recv_sem=ag_recv.at[index],
            device_id=device(1, 0),
            device_id_type=MESH,
        ).wait_recv()

    load_teacher.wait()
    target_recv[owner] = picked(teacher[...], owner)
    for k in (4, 3, 5, 2, 6, 1, 7):
        peer = (owner + k) % 8
        target_send[peer] = picked(teacher[...], peer)
    load_tokens.wait()
    for h in range(2):
        half = pl.ds(h * 160, 160)
        for k in (0, 4, 3, 5, 2, 6, 1, 7):
            source = (owner - k + 8) % 8
            table = unpack[pl.ds(pl.multiple_of(source * 256, 256), 256), :]
            if k == 0:
                pre[half, :] = jnp.dot(weight_send[owner, half, :], table, preferred_element_type=F32)
                continue
            pltpu.make_async_remote_copy(
                src_ref=weight_recv.at[source, half, :],
                dst_ref=weight_recv.at[source, half, :],
                send_sem=ws_send.at[h * 8 + k],
                recv_sem=ws_recv.at[h * 8 + k],
                device_id=(dp, (owner + k) % 8),
                device_id_type=MESH,
            ).wait_recv()
            pre[half, :] += jnp.dot(weight_recv[source, half, :], table, preferred_element_type=F32)
        weights[pl.ds(slot_row(0, 0, h), 160), :] = pre[half, :].astype(BF16)
        for ring in (0, 1):
            for step in (1, 3):
                ag_start(ring, step, 0, 0, h)
        lax.fori_loop(h * 8, h * 8 + 8, norm, 0)
    for k in (4, 3, 5, 2, 6, 1, 7):
        target_copy(k).start()

    def chunk_copy(index, turn):
        return pltpu.make_async_remote_copy(
            src_ref=packed_x.at[index],
            dst_ref=packed_x.at[index],
            send_sem=px_send.at[turn],
            recv_sem=px_recv.at[turn],
            device_id=(dp, owner + 1 - 2 * core),
            device_id_type=MESH,
        )

    def permute(turn, carry):
        index = (z * 5 + 2 * turn + core) % 20
        slots = lax.broadcasted_iota(jnp.int32, (256, 128), 0) + index * 256
        total = jnp.zeros((512, 256), F32)
        for part in range(4):
            hot = jnp.concatenate(
                [
                    jnp.where(places[r : r + 1, :] == slots, 1.0, 0.0).astype(BF16)
                    for r in range(part * 8, part * 8 + 8)
                ],
                axis=1,
            )
            total += lax.dot_general(
                normed[:, part * 1024 : part * 1024 + 1024], hot, (((1,), (1,)), ((), ())), preferred_element_type=F32
            )
        packed_x[index] = total.astype(BF16)
        chunk_copy(index, turn).start()
        return carry

    def fill(first, last):
        lax.fori_loop(first, last, permute, 0)

    def take_chunks(first, last):
        @pl.loop(first, last)
        def _(turn):
            chunk_copy((z * 5 + 2 * turn + 1 - core) % 20, turn).wait_recv()

    def multiply_group(zo, first):
        base = ((z + zo) % 4) * 5

        @pl.loop(0, 2)
        def _(n):
            cols = pl.ds(pl.multiple_of(n * 512, 512), 512)
            part = jnp.zeros((512, 512), F32) if first else pre[:, cols]
            for c in range(5):
                depth = pl.ds(pl.multiple_of((base + c) * 256, 256), 256)
                part += jnp.dot(packed_x[base + c], weights[depth, cols], preferred_element_type=F32)
            pre[:, cols] = part

    def relay(ring, ao, bo, h):
        ag_wait(ring, ao, bo, h)
        far = ao if ring == 0 else bo
        if far == 3 and h == 0:
            ag_start(ring, 1, ao, bo, h)
        if far == 1 and h == 1:
            ag_start(ring, 3, ao, bo, h)
        if ring == 0:
            ag_start(1, 1, ao, 0, h)
            ag_start(1, 3, ao, 0, h)

    relay(0, 3, 0, 0)
    relay(0, 1, 0, 0)
    relay(1, 0, 3, 0)
    fill(0, 2)
    relay(0, 1, 0, 1)
    relay(0, 3, 0, 1)
    relay(1, 0, 1, 1)
    fill(2, 4)
    relay(0, 2, 0, 0)
    fill(4, 6)
    relay(0, 2, 0, 1)
    relay(1, 3, 3, 0)
    fill(6, 7)
    relay(1, 3, 1, 1)
    relay(1, 1, 3, 0)
    fill(7, 8)
    relay(1, 1, 1, 1)
    fill(8, 10)
    relay(1, 2, 3, 0)

    @pl.loop(0, 16)
    def _(s):
        aa, bb = s // 4, s % 4
        cols = pl.ds(pl.multiple_of((bb * 4 + aa + core * 3 * (aa - bb)) * 256, 256), 256)
        normed_t[pl.ds(pl.multiple_of(s * 256, 256), 256), :] = normed[:, cols].T

    relay(1, 2, 1, 1)

    for k in range(1, 8):
        source = (owner - k + 8) % 8
        pltpu.make_async_remote_copy(
            src_ref=target_recv.at[source],
            dst_ref=target_recv.at[source],
            send_sem=ts_send.at[k],
            recv_sem=ts_recv.at[k],
            device_id=(dp, (owner + k) % 8),
            device_id_type=MESH,
        ).wait_recv()

    @pl.loop(0, 4)
    def _(n):
        cols = pl.ds(pl.multiple_of(n * 256, 256), 256)
        total = jnp.zeros((512, 256), F32)
        for s in range(8):
            total += jnp.dot(target_recv[s], unpack[s * 256 : s * 256 + 256, cols], preferred_element_type=F32)
        target[:, cols] = total.astype(BF16)

    take_chunks(0, 10)
    for bo, h in ((3, 1), (1, 0), (2, 0), (2, 1)):
        ag_wait(1, 0, bo, h)
    multiply_group(0, True)
    for ao in (3, 1, 2):
        ag_wait(1, ao, 3, 1)
    for h in range(2):
        ag_wait(1, 3, 2, h)
    ag_wait(1, 3, 1, 0)
    multiply_group(3, False)
    for ao in (1, 2):
        ag_wait(1, ao, 1, 0)
    for h in range(2):
        ag_wait(1, 1, 2, h)
    multiply_group(1, False)
    for h in range(2):
        ag_wait(1, 2, 2, h)
    multiply_group(2, False)

    @pl.loop(0, 32)
    def _(r):
        rows = pl.ds(pl.multiple_of(r * 16, 16), 16)
        active = jnp.maximum(pre[rows, :], 0.0)
        delta[rows, :] = (2.0 * active * (active * active - target[rows, :].astype(F32)) * scale).astype(BF16)

    for copy in ag_started:
        copy.wait_send()
    for k in range(1, 8):
        for h in range(2):
            weight_copy(k, h).wait_send()
        target_copy(k).wait_send()

    @pl.loop(0, 10)
    def _(turn):
        chunk_copy((z * 5 + 2 * turn + core) % 20, turn).wait_send()

    rs_started = []

    def grad_row(ao, bo, h):
        aa, bb = (a + ao) % 4, (b + bo) % 4
        return pl.multiple_of((aa * 4 + bb) * 256 + h * 128, 128)

    def rs_start(ring, step, ao, bo, h, role):
        index = role if ring == 0 else 6 + ao * 6 + role
        place = ring_a.at[pl.ds(role * 128, 128), :] if ring == 0 else ring_b.at[pl.ds((ao * 6 + role) * 128, 128), :]
        copy = pltpu.make_async_remote_copy(
            src_ref=weights.at[pl.ds(grad_row(ao, bo, h), 128), :],
            dst_ref=place,
            send_sem=rs_send.at[len(rs_started)],
            recv_sem=rs_recv.at[index],
            device_id=device(step, 0) if ring == 0 else device(0, step),
            device_id_type=MESH,
        )
        copy.start()
        rs_started.append(copy)

    def rs_take(ring, ao, role):
        index = role if ring == 0 else 6 + ao * 6 + role
        place = ring_a.at[pl.ds(role * 128, 128), :] if ring == 0 else ring_b.at[pl.ds((ao * 6 + role) * 128, 128), :]
        pltpu.make_async_remote_copy(
            src_ref=place,
            dst_ref=place,
            send_sem=rs_send.at[0],
            recv_sem=rs_recv.at[index],
            device_id=device(1, 0),
            device_id_type=MESH,
        ).wait_recv()
        return place

    def add_into(ao, bo, h, places_in, final=False):
        base = grad_row(ao, bo, h)

        @pl.loop(0, 8)
        def _(r):
            total = weights[pl.ds(base + r * 16, 16), :].astype(F32)
            for place in places_in:
                total += place[pl.ds(pl.multiple_of(r * 16, 16), 16), :].astype(F32)
            if final:
                out_ref[pl.ds(pl.multiple_of(h * 128 + r * 16, 16), 16), :] = total
            else:
                weights[pl.ds(base + r * 16, 16), :] = total.astype(BF16)

    def products(ao):
        rows = pl.ds(pl.multiple_of(((a + ao) % 4) * 1024, 1024), 1024)

        @pl.loop(0, 4)
        def _(n):
            cols = pl.ds(pl.multiple_of(n * 256, 256), 256)
            weights[rows, cols] = jnp.dot(
                normed_t[rows, :], delta[:, cols], preferred_element_type=F32
            ).astype(BF16)

    def spread_b(ao):
        rs_start(1, 1, ao, 2, 0, 0)
        rs_start(1, 3, ao, 2, 1, 1)
        rs_start(1, 1, ao, 1, 1, 3)
        rs_start(1, 3, ao, 3, 0, 4)

    def relay_b(ao):
        add_into(ao, 1, 0, [rs_take(1, ao, 0)])
        rs_start(1, 1, ao, 1, 0, 2)
        add_into(ao, 3, 1, [rs_take(1, ao, 1)])
        rs_start(1, 3, ao, 3, 1, 5)

    def gather_b(ao):
        for h in range(2):
            add_into(ao, 0, h, [rs_take(1, ao, 2 + h), rs_take(1, ao, 4 + h)])

    products(2)
    spread_b(2)
    products(1)
    spread_b(1)
    relay_b(2)
    products(3)
    spread_b(3)
    relay_b(1)
    products(0)
    spread_b(0)
    relay_b(3)
    gather_b(2)
    rs_start(0, 1, 2, 0, 0, 0)
    rs_start(0, 3, 2, 0, 1, 1)
    relay_b(0)
    gather_b(1)
    rs_start(0, 1, 1, 0, 1, 3)
    add_into(1, 0, 0, [rs_take(0, 0, 0)])
    rs_start(0, 1, 1, 0, 0, 2)
    gather_b(3)
    rs_start(0, 3, 3, 0, 0, 4)
    add_into(3, 0, 1, [rs_take(0, 0, 1)])
    rs_start(0, 3, 3, 0, 1, 5)
    for h in range(2):
        add_into(
            0, 0, h,
            [rs_take(1, 0, 2 + h), rs_take(1, 0, 4 + h), rs_take(0, 0, 2 + h), rs_take(0, 0, 4 + h)],
            final=True,
        )
    for copy in rs_started:
        copy.wait_send()


def per_device(tokens_in, teacher_hidden, up_old, gain_old, keep_chan, keep_ff):
    scale = 1.0 / math.sqrt(tokens_in.shape[0] * lax.axis_size("dp"))
    anywhere = pl.BlockSpec(memory_space=pl.ANY)
    vmem = pl.BlockSpec(memory_space=pltpu.VMEM)
    dma = pltpu.SemaphoreType.DMA

    def body(*refs):
        kernel(scale, *refs)

    return pl.pallas_call(
        body,
        out_shape=jax.ShapeDtypeStruct((256, 1024), F32),
        in_specs=[anywhere, anywhere, anywhere, vmem, vmem, vmem],
        out_specs=vmem,
        scratch_shapes=[
            pltpu.VMEM((512, 4096), BF16),
            pltpu.VMEM((4096, 512), BF16),
            pltpu.VMEM((20, 512, 256), BF16),
            pltpu.VMEM((5120, 1024), BF16),
            pltpu.VMEM((512, 1536), BF16),
            pltpu.VMEM((384, 1536), BF16),
            pltpu.VMEM((SLOT_ROWS, 1536), BF16),
            pltpu.VMEM((8, SLOT_ROWS, SLOT_COLS), BF16),
            pltpu.VMEM((8, SLOT_ROWS, SLOT_COLS), BF16),
            pltpu.VMEM((8, 512, SLOT_COLS), BF16),
            pltpu.VMEM((8, 512, SLOT_COLS), BF16),
            pltpu.VMEM((2048, 1024), BF16),
            pltpu.VMEM((2048, 1536), BF16),
            pltpu.VMEM((512, 1024), F32),
            pltpu.VMEM((512, 1024), BF16),
            pltpu.VMEM((512, 1024), BF16),
            pltpu.VMEM((24 * 128, 1024), BF16),
            pltpu.VMEM((6 * 128, 1024), BF16),
            pltpu.VMEM((1, 4096), F32),
            pltpu.VMEM((200, 128), jnp.int32),
            dma((3,)),
            dma((16,)),
            dma((16,)),
            dma((8,)),
            dma((8,)),
            dma((30,)),
            dma((30,)),
            dma((30,)),
            dma((30,)),
            dma((10,)),
            dma((10,)),
        ],
        compiler_params=pltpu.CompilerParams(
            collective_id=0, has_side_effects=True, vmem_limit_bytes=62 * 1024 * 1024
        ),
        cost_estimate=pl.CostEstimate(flops=40_000_000_000, bytes_accessed=10_000_000, transcendentals=0),
    )(
        tokens_in, teacher_hidden, up_old,
        gain_old.reshape(48, 128), keep_chan.reshape(32, 128), keep_ff.reshape(64, 128),
    )


def solution(mesh):
    return jax.shard_map(
        per_device,
        mesh=mesh,
        in_specs=(P("dp", None), P("dp", "tensor"), P("dp", "tensor"), P(), P(), P()),
        out_specs=P("dp", "tensor"),
        check_vma=False,
    )
```

```python
import math

import jax
import jax.numpy as jnp
from jax import lax
from jax.experimental import pallas as pl
from jax.experimental.pallas import tpu as pltpu
from jax.sharding import PartitionSpec as P

MESH = pl.DeviceIdType.MESH
SLOT_ROWS = 320
SLOT_COLS = 256
BF16 = jnp.bfloat16
F32 = jnp.float32


def strict(shape, dim, group):
    rows = lax.broadcasted_iota(jnp.int32, shape, 0)
    cols = lax.broadcasted_iota(jnp.int32, shape, 1)
    ahead = rows < cols if dim == 1 else cols < rows
    same = rows // group == cols // group
    return jnp.where(ahead & same, 1.0, 0.0).astype(BF16)


def ranks_of(hits, group):
    parts = hits.astype(BF16)
    within = jnp.dot(parts, strict((128, 128), 1, 128), preferred_element_type=F32)
    above = jnp.dot(strict((hits.shape[0],) * 2, 0, group), parts, preferred_element_type=F32)
    return within + jnp.sum(above, axis=1, keepdims=True)


def blocks_of(index, width, count):
    block = jnp.zeros_like(index)
    for edge in range(1, count):
        block += jnp.where(index >= edge * width, 1, 0)
    return block


def kernel(
    scale,
    tokens_hbm, teacher_hbm, up_hbm, gain_ref, chan_ref, ff_ref,
    out_ref,
    normed, normed_t, packed_x, weights, teacher, up, kept_rows, weight_send, weight_recv,
    target_send, target_recv, unpack, picks, pre, delta, target, ring_b, ring_a, gain, places,
    local_sems, ws_send, ws_recv, ts_send, ts_recv, ag_send, ag_recv, rs_send, rs_recv, px_send, px_recv,
):
    dp = lax.axis_index("dp")
    owner = lax.axis_index("tensor")
    core = owner % 2
    z, x = dp // 4, dp % 4
    a = x + core * (z - x)
    b = z + core * (x - z)

    def dp_of(ao, bo):
        aa, bb = (a + ao) % 4, (b + bo) % 4
        return bb * 4 + aa + core * 3 * (aa - bb)

    def device(ao, bo):
        return (dp_of(ao, bo), owner)

    load_up = pltpu.make_async_copy(up_hbm, up, local_sems.at[0])
    load_teacher = pltpu.make_async_copy(teacher_hbm, teacher, local_sems.at[1])
    load_tokens = pltpu.make_async_copy(tokens_hbm, normed, local_sems.at[2])
    load_up.start()
    load_teacher.start()
    load_tokens.start()
    barrier = pltpu.get_barrier_semaphore()
    for ao, bo in ((1, 0), (3, 0), (0, 1), (0, 3)):
        pl.semaphore_signal(barrier, inc=1, device_id=device(ao, bo), device_id_type=MESH)
    for k in range(1, 8):
        pl.semaphore_signal(barrier, inc=1, device_id=(dp, (owner + k) % 8), device_id_type=MESH)

    chan = chan_ref[...]
    block = blocks_of(chan, 384, 16)
    block_hits = jnp.concatenate([jnp.where(block == s, 1.0, 0.0) for s in range(16)], axis=0)
    block_ranks = ranks_of(block_hits, 32) * block_hits
    rank = block_ranks[0:32, :]
    for s in range(1, 16):
        rank += block_ranks[32 * s : 32 * s + 32, :]
    rank = rank.astype(jnp.int32)
    places[0:32, :] = block * SLOT_ROWS + rank
    places[32:64, :] = jnp.where(block == dp, rank, -1)

    slots = lax.broadcasted_iota(jnp.int32, (SLOT_ROWS, 128), 0)
    found = jnp.zeros((SLOT_ROWS, 128), jnp.int32)
    for r in range(32):
        found += jnp.where(places[32 + r : 33 + r, :] == slots, chan_ref[r : r + 1, :] - dp * 384 + 1, 0)
    row = jnp.sum(found.astype(F32), axis=1, keepdims=True).astype(jnp.int32) - 1
    hot = jnp.where(lax.broadcasted_iota(jnp.int32, (SLOT_ROWS, 384), 1) == row, 1.0, 0.0).astype(BF16)
    load_up.wait()
    kept_rows[...] = jnp.dot(hot, up[...], preferred_element_type=F32).astype(BF16)

    places[64:128, :] = ff_ref[...] - owner * 1536
    local = places[64:128, :]
    mine = (local >= 0) & (local < 1536)
    slot = ranks_of(jnp.where(mine, 1.0, 0.0), 8).astype(jnp.int32)
    places[128:192, :] = jnp.where(mine, slot, -1)

    def make_pick(o, carry):
        slots = lax.broadcasted_iota(jnp.int32, (SLOT_COLS, 128), 0)
        found = jnp.zeros((SLOT_COLS, 128), jnp.int32)
        for r in range(8):
            found += jnp.where(
                places[pl.ds(128 + o * 8 + r, 1), :] == slots, places[pl.ds(64 + o * 8 + r, 1), :] + 1, 0
            )
        column = jnp.sum(found.astype(F32), axis=1, keepdims=True).astype(jnp.int32) - 1
        hot = jnp.where(lax.broadcasted_iota(jnp.int32, (SLOT_COLS, 1536), 1) == column, 1.0, 0.0)
        picks[pl.ds(pl.multiple_of(o * 256, 256), 256), :] = hot.astype(BF16)
        return carry

    def picked(rows, o):
        pick = picks[pl.ds(pl.multiple_of(o * 256, 256), 256), :]
        return lax.dot_general(
            rows, pick, (((1,), (1,)), ((), ())), preferred_element_type=F32
        ).astype(BF16)

    def weight_copy(k, h):
        peer = (owner + k) % 8
        return pltpu.make_async_remote_copy(
            src_ref=weight_send.at[peer, pl.ds(h * 160, 160), :],
            dst_ref=weight_recv.at[owner, pl.ds(h * 160, 160), :],
            send_sem=ws_send.at[h * 8 + k],
            recv_sem=ws_recv.at[h * 8 + k],
            device_id=(dp, peer),
            device_id_type=MESH,
        )

    def target_copy(k):
        peer = (owner + k) % 8
        return pltpu.make_async_remote_copy(
            src_ref=target_send.at[peer],
            dst_ref=target_recv.at[owner],
            send_sem=ts_send.at[k],
            recv_sem=ts_recv.at[k],
            device_id=(dp, peer),
            device_id_type=MESH,
        )

    pl.semaphore_wait(barrier, 11)

    def pack(i, carry):
        k = 4 + (i + 1) // 2 * (1 - 2 * (i % 2))
        peer = (owner + k) % 8
        make_pick(peer, carry)
        weight_send[peer] = picked(kept_rows[...], peer)
        weight_copy(k, 0).start()
        return carry

    lax.fori_loop(0, 7, pack, 0)
    for k in (4, 3, 5, 2, 6, 1, 7):
        weight_copy(k, 1).start()
    make_pick(owner, 0)
    weight_send[owner] = picked(kept_rows[...], owner)

    own = ff_ref[pl.ds(pl.multiple_of(owner * 8, 8), 8), :]
    source = blocks_of(own, 1536, 8)
    source_hits = jnp.concatenate([jnp.where(source == s, 1.0, 0.0) for s in range(8)], axis=0)
    source_ranks = ranks_of(source_hits, 8) * source_hits
    arrives = source * SLOT_COLS
    for s in range(8):
        arrives += source_ranks[8 * s : 8 * s + 8, :].astype(jnp.int32)
    places[192:200, :] = arrives

    def make_unpack(s, carry):
        slots = lax.broadcasted_iota(jnp.int32, (256, 128), 0) + s * 256
        for r in range(8):
            hot = jnp.where(places[192 + r : 193 + r, :] == slots, 1.0, 0.0)
            unpack[pl.ds(pl.multiple_of(s * 256, 256), 256), r * 128 : r * 128 + 128] = hot.astype(BF16)
        return carry

    lax.fori_loop(0, 8, make_unpack, 0)

    old = gain_ref[...]
    first = old.astype(BF16)
    second = (old - first.astype(F32)).astype(BF16)
    third = (old - first.astype(F32) - second.astype(F32)).astype(BF16)
    gains = jnp.concatenate([first.astype(F32), second.astype(F32), third.astype(F32)], axis=0).astype(BF16)
    for r in range(32):
        line = chan_ref[r : r + 1, :]
        high = blocks_of(line, 128, 48)
        low = line - high * 128
        hot = jnp.where(lax.broadcasted_iota(jnp.int32, (128, 128), 0) == low, 1.0, 0.0).astype(BF16)
        wide = jnp.dot(gains, hot, preferred_element_type=F32)
        wide = (wide[0:48, :] + wide[48:96, :]) + wide[96:144, :]
        chosen = lax.broadcasted_iota(jnp.int32, (48, 128), 0) == high
        gain[:, r * 128 : r * 128 + 128] = jnp.sum(jnp.where(chosen, wide, 0.0), axis=0, keepdims=True)
    def norm(r, carry):
        rows = pl.ds(pl.multiple_of(r * 32, 32), 32)
        values = normed[rows, :].astype(F32)
        center = jnp.mean(values, axis=1, keepdims=True)
        spread = jnp.mean((values - center) ** 2, axis=1, keepdims=True)
        normed[rows, :] = ((values - center) * lax.rsqrt(spread + 1e-05) * gain[...]).astype(BF16)
        return carry

    def slot_row(ao, bo, h):
        return pl.multiple_of(dp_of(ao, bo) * SLOT_ROWS + h * 160, 32)

    ag_started = []

    def ag_copy(ring, step, ao, bo, h):
        far = (ao if ring == 0 else bo) != 0
        role = (4 + h) if far else ((0 if step == 1 else 2) + h)
        index = role if ring == 0 else 6 + ao * 6 + role
        rows = pl.ds(slot_row(ao, bo, h), 160)
        return pltpu.make_async_remote_copy(
            src_ref=weights.at[rows, :],
            dst_ref=weights.at[rows, :],
            send_sem=ag_send.at[len(ag_started)],
            recv_sem=ag_recv.at[index],
            device_id=device(step, 0) if ring == 0 else device(0, step),
            device_id_type=MESH,
        )

    def ag_start(ring, step, ao, bo, h):
        copy = ag_copy(ring, step, ao, bo, h)
        copy.start()
        ag_started.append(copy)

    def ag_wait(ring, ao, bo, h):
        offset = ao if ring == 0 else bo
        role = {3: 0, 1: 2, 2: 4}[offset] + h
        index = role if ring == 0 else 6 + ao * 6 + role
        rows = pl.ds(slot_row(ao, bo, h), 160)
        pltpu.make_async_remote_copy(
            src_ref=weights.at[rows, :],
            dst_ref=weights.at[rows, :],
            send_sem=ag_send.at[0],
            recv_sem=ag_recv.at[index],
            device_id=device(1, 0),
            device_id_type=MESH,
        ).wait_recv()

    load_teacher.wait()
    target_recv[owner] = picked(teacher[...], owner)
    for k in (4, 3, 5, 2, 6, 1, 7):
        peer = (owner + k) % 8
        target_send[peer] = picked(teacher[...], peer)
    load_tokens.wait()
    for h in range(2):
        half = pl.ds(h * 160, 160)
        for k in (0, 4, 3, 5, 2, 6, 1, 7):
            source = (owner - k + 8) % 8
            table = unpack[pl.ds(pl.multiple_of(source * 256, 256), 256), :]
            if k == 0:
                pre[half, :] = jnp.dot(weight_send[owner, half, :], table, preferred_element_type=F32)
                continue
            pltpu.make_async_remote_copy(
                src_ref=weight_recv.at[source, half, :],
                dst_ref=weight_recv.at[source, half, :],
                send_sem=ws_send.at[h * 8 + k],
                recv_sem=ws_recv.at[h * 8 + k],
                device_id=(dp, (owner + k) % 8),
                device_id_type=MESH,
            ).wait_recv()
            pre[half, :] += jnp.dot(weight_recv[source, half, :], table, preferred_element_type=F32)
        weights[pl.ds(slot_row(0, 0, h), 160), :] = pre[half, :].astype(BF16)
        for ring in (0, 1):
            for step in (1, 3):
                ag_start(ring, step, 0, 0, h)
        lax.fori_loop(h * 8, h * 8 + 8, norm, 0)
    for k in (4, 3, 5, 2, 6, 1, 7):
        target_copy(k).start()

    def chunk_copy(index, turn):
        return pltpu.make_async_remote_copy(
            src_ref=packed_x.at[index],
            dst_ref=packed_x.at[index],
            send_sem=px_send.at[turn],
            recv_sem=px_recv.at[turn],
            device_id=(dp, owner + 1 - 2 * core),
            device_id_type=MESH,
        )

    def permute(turn, carry):
        index = (z * 5 + 2 * turn + core) % 20
        slots = lax.broadcasted_iota(jnp.int32, (256, 128), 0) + index * 256
        total = jnp.zeros((512, 256), F32)
        for part in range(4):
            hot = jnp.concatenate(
                [
                    jnp.where(places[r : r + 1, :] == slots, 1.0, 0.0).astype(BF16)
                    for r in range(part * 8, part * 8 + 8)
                ],
                axis=1,
            )
            total += lax.dot_general(
                normed[:, part * 1024 : part * 1024 + 1024], hot, (((1,), (1,)), ((), ())), preferred_element_type=F32
            )
        packed_x[index] = total.astype(BF16)
        chunk_copy(index, turn).start()
        return carry

    def fill(first, last):
        lax.fori_loop(first, last, permute, 0)

    def take_chunks(first, last):
        @pl.loop(first, last)
        def _(turn):
            chunk_copy((z * 5 + 2 * turn + 1 - core) % 20, turn).wait_recv()

    def multiply_group(zo, first):
        base = ((z + zo) % 4) * 5

        @pl.loop(0, 2)
        def _(n):
            cols = pl.ds(pl.multiple_of(n * 512, 512), 512)
            part = jnp.zeros((512, 512), F32) if first else pre[:, cols]
            for c in range(5):
                depth = pl.ds(pl.multiple_of((base + c) * 256, 256), 256)
                part += jnp.dot(packed_x[base + c], weights[depth, cols], preferred_element_type=F32)
            pre[:, cols] = part

    def relay(ring, ao, bo, h):
        ag_wait(ring, ao, bo, h)
        far = ao if ring == 0 else bo
        if far == 3 and h == 0:
            ag_start(ring, 1, ao, bo, h)
        if far == 1 and h == 1:
            ag_start(ring, 3, ao, bo, h)
        if ring == 0:
            ag_start(1, 1, ao, 0, h)
            ag_start(1, 3, ao, 0, h)

    relay(0, 3, 0, 0)
    relay(0, 1, 0, 0)
    relay(1, 0, 3, 0)
    fill(0, 2)
    relay(0, 1, 0, 1)
    relay(0, 3, 0, 1)
    relay(1, 0, 1, 1)
    fill(2, 4)
    relay(0, 2, 0, 0)
    fill(4, 6)
    relay(0, 2, 0, 1)
    relay(1, 3, 3, 0)
    fill(6, 7)
    relay(1, 3, 1, 1)
    relay(1, 1, 3, 0)
    fill(7, 8)
    relay(1, 1, 1, 1)
    fill(8, 10)
    relay(1, 2, 3, 0)

    @pl.loop(0, 16)
    def _(s):
        aa, bb = s // 4, s % 4
        cols = pl.ds(pl.multiple_of((bb * 4 + aa + core * 3 * (aa - bb)) * 256, 256), 256)
        normed_t[pl.ds(pl.multiple_of(s * 256, 256), 256), :] = normed[:, cols].T

    relay(1, 2, 1, 1)

    for k in range(1, 8):
        source = (owner - k + 8) % 8
        pltpu.make_async_remote_copy(
            src_ref=target_recv.at[source],
            dst_ref=target_recv.at[source],
            send_sem=ts_send.at[k],
            recv_sem=ts_recv.at[k],
            device_id=(dp, (owner + k) % 8),
            device_id_type=MESH,
        ).wait_recv()

    @pl.loop(0, 4)
    def _(n):
        cols = pl.ds(pl.multiple_of(n * 256, 256), 256)
        total = jnp.zeros((512, 256), F32)
        for s in range(8):
            total += jnp.dot(target_recv[s], unpack[s * 256 : s * 256 + 256, cols], preferred_element_type=F32)
        target[:, cols] = total.astype(BF16)

    take_chunks(0, 10)
    for bo, h in ((3, 1), (1, 0), (2, 0), (2, 1)):
        ag_wait(1, 0, bo, h)
    multiply_group(0, True)
    for ao in (3, 1, 2):
        ag_wait(1, ao, 3, 1)
    for h in range(2):
        ag_wait(1, 3, 2, h)
    ag_wait(1, 3, 1, 0)
    multiply_group(3, False)
    for ao in (1, 2):
        ag_wait(1, ao, 1, 0)
    for h in range(2):
        ag_wait(1, 1, 2, h)
    multiply_group(1, False)
    for h in range(2):
        ag_wait(1, 2, 2, h)
    multiply_group(2, False)

    @pl.loop(0, 32)
    def _(r):
        rows = pl.ds(pl.multiple_of(r * 16, 16), 16)
        active = jnp.maximum(pre[rows, :], 0.0)
        delta[rows, :] = (2.0 * active * (active * active - target[rows, :].astype(F32)) * scale).astype(BF16)

    for copy in ag_started:
        copy.wait_send()
    for k in range(1, 8):
        for h in range(2):
            weight_copy(k, h).wait_send()
        target_copy(k).wait_send()

    @pl.loop(0, 10)
    def _(turn):
        chunk_copy((z * 5 + 2 * turn + core) % 20, turn).wait_send()

    rs_started = []

    def grad_row(ao, bo, h):
        aa, bb = (a + ao) % 4, (b + bo) % 4
        return pl.multiple_of((aa * 4 + bb) * 256 + h * 128, 128)

    def rs_start(ring, step, ao, bo, h, role):
        index = role if ring == 0 else 6 + ao * 6 + role
        place = ring_a.at[pl.ds(role * 128, 128), :] if ring == 0 else ring_b.at[pl.ds((ao * 6 + role) * 128, 128), :]
        copy = pltpu.make_async_remote_copy(
            src_ref=weights.at[pl.ds(grad_row(ao, bo, h), 128), :],
            dst_ref=place,
            send_sem=rs_send.at[len(rs_started)],
            recv_sem=rs_recv.at[index],
            device_id=device(step, 0) if ring == 0 else device(0, step),
            device_id_type=MESH,
        )
        copy.start()
        rs_started.append(copy)

    def rs_take(ring, ao, role):
        index = role if ring == 0 else 6 + ao * 6 + role
        place = ring_a.at[pl.ds(role * 128, 128), :] if ring == 0 else ring_b.at[pl.ds((ao * 6 + role) * 128, 128), :]
        pltpu.make_async_remote_copy(
            src_ref=place,
            dst_ref=place,
            send_sem=rs_send.at[0],
            recv_sem=rs_recv.at[index],
            device_id=device(1, 0),
            device_id_type=MESH,
        ).wait_recv()
        return place

    def add_into(ao, bo, h, places_in, final=False):
        base = grad_row(ao, bo, h)

        @pl.loop(0, 8)
        def _(r):
            total = weights[pl.ds(base + r * 16, 16), :].astype(F32)
            for place in places_in:
                total += place[pl.ds(pl.multiple_of(r * 16, 16), 16), :].astype(F32)
            if final:
                out_ref[pl.ds(pl.multiple_of(h * 128 + r * 16, 16), 16), :] = total
            else:
                weights[pl.ds(base + r * 16, 16), :] = total.astype(BF16)

    def products(ao, bo, count):
        first = ((a + ao) % 4) * 4 + (b + bo) % 4 if count == 1 else ((a + ao) % 4) * 4
        rows = pl.ds(pl.multiple_of(first * 256, 256), 256 * count)

        @pl.loop(0, 4)
        def _(n):
            cols = pl.ds(pl.multiple_of(n * 256, 256), 256)
            weights[rows, cols] = jnp.dot(
                normed_t[rows, :], delta[:, cols], preferred_element_type=F32
            ).astype(BF16)

    def spread_b(ao, only=None):
        if only in (None, 2):
            rs_start(1, 1, ao, 2, 0, 0)
            rs_start(1, 3, ao, 2, 1, 1)
        if only in (None, 1):
            rs_start(1, 1, ao, 1, 1, 3)
        if only in (None, 3):
            rs_start(1, 3, ao, 3, 0, 4)

    def relay_b(ao):
        add_into(ao, 1, 0, [rs_take(1, ao, 0)])
        rs_start(1, 1, ao, 1, 0, 2)
        add_into(ao, 3, 1, [rs_take(1, ao, 1)])
        rs_start(1, 3, ao, 3, 1, 5)

    def gather_b(ao):
        for h in range(2):
            add_into(ao, 0, h, [rs_take(1, ao, 2 + h), rs_take(1, ao, 4 + h)])

    for bo in (2, 1, 3):
        products(2, bo, 1)
        spread_b(2, bo)
    products(1, 0, 4)
    spread_b(1)
    products(3, 0, 4)
    spread_b(3)
    relay_b(2)
    relay_b(1)
    relay_b(3)
    products(0, 0, 4)
    spread_b(0)
    products(2, 0, 1)
    gather_b(2)
    rs_start(0, 1, 2, 0, 0, 0)
    rs_start(0, 3, 2, 0, 1, 1)
    gather_b(1)
    rs_start(0, 1, 1, 0, 1, 3)
    gather_b(3)
    rs_start(0, 3, 3, 0, 0, 4)
    add_into(1, 0, 0, [rs_take(0, 0, 0)])
    rs_start(0, 1, 1, 0, 0, 2)
    add_into(3, 0, 1, [rs_take(0, 0, 1)])
    rs_start(0, 3, 3, 0, 1, 5)
    relay_b(0)
    for h in range(2):
        add_into(
            0, 0, h,
            [rs_take(1, 0, 2 + h), rs_take(1, 0, 4 + h), rs_take(0, 0, 2 + h), rs_take(0, 0, 4 + h)],
            final=True,
        )
    for copy in rs_started:
        copy.wait_send()


def per_device(tokens_in, teacher_hidden, up_old, gain_old, keep_chan, keep_ff):
    scale = 1.0 / math.sqrt(tokens_in.shape[0] * lax.axis_size("dp"))
    anywhere = pl.BlockSpec(memory_space=pl.ANY)
    vmem = pl.BlockSpec(memory_space=pltpu.VMEM)
    dma = pltpu.SemaphoreType.DMA

    def body(*refs):
        kernel(scale, *refs)

    return pl.pallas_call(
        body,
        out_shape=jax.ShapeDtypeStruct((256, 1024), F32),
        in_specs=[anywhere, anywhere, anywhere, vmem, vmem, vmem],
        out_specs=vmem,
        scratch_shapes=[
            pltpu.VMEM((512, 4096), BF16),
            pltpu.VMEM((4096, 512), BF16),
            pltpu.VMEM((20, 512, 256), BF16),
            pltpu.VMEM((5120, 1024), BF16),
            pltpu.VMEM((512, 1536), BF16),
            pltpu.VMEM((384, 1536), BF16),
            pltpu.VMEM((SLOT_ROWS, 1536), BF16),
            pltpu.VMEM((8, SLOT_ROWS, SLOT_COLS), BF16),
            pltpu.VMEM((8, SLOT_ROWS, SLOT_COLS), BF16),
            pltpu.VMEM((8, 512, SLOT_COLS), BF16),
            pltpu.VMEM((8, 512, SLOT_COLS), BF16),
            pltpu.VMEM((2048, 1024), BF16),
            pltpu.VMEM((2048, 1536), BF16),
            pltpu.VMEM((512, 1024), F32),
            pltpu.VMEM((512, 1024), BF16),
            pltpu.VMEM((512, 1024), BF16),
            pltpu.VMEM((24 * 128, 1024), BF16),
            pltpu.VMEM((6 * 128, 1024), BF16),
            pltpu.VMEM((1, 4096), F32),
            pltpu.VMEM((200, 128), jnp.int32),
            dma((3,)),
            dma((16,)),
            dma((16,)),
            dma((8,)),
            dma((8,)),
            dma((30,)),
            dma((30,)),
            dma((30,)),
            dma((30,)),
            dma((10,)),
            dma((10,)),
        ],
        compiler_params=pltpu.CompilerParams(
            collective_id=0, has_side_effects=True, vmem_limit_bytes=62 * 1024 * 1024
        ),
        cost_estimate=pl.CostEstimate(flops=40_000_000_000, bytes_accessed=10_000_000, transcendentals=0),
    )(
        tokens_in, teacher_hidden, up_old,
        gain_old.reshape(48, 128), keep_chan.reshape(32, 128), keep_ff.reshape(64, 128),
    )


def solution(mesh):
    return jax.shard_map(
        per_device,
        mesh=mesh,
        in_specs=(P("dp", None), P("dp", "tensor"), P("dp", "tensor"), P(), P(), P()),
        out_specs=P("dp", "tensor"),
        check_vma=False,
    )
```

```python
import math

import jax
import jax.numpy as jnp
from jax import lax
from jax.experimental import pallas as pl
from jax.experimental.pallas import tpu as pltpu
from jax.sharding import PartitionSpec as P

MESH = pl.DeviceIdType.MESH
SLOT_ROWS = 320
SLOT_COLS = 256
PIECES = 4
SLOT_PIECE = SLOT_ROWS // PIECES
GRAD_PIECE = 256 // PIECES
BF16 = jnp.bfloat16
F32 = jnp.float32


def strict(shape, dim, group):
    rows = lax.broadcasted_iota(jnp.int32, shape, 0)
    cols = lax.broadcasted_iota(jnp.int32, shape, 1)
    ahead = rows < cols if dim == 1 else cols < rows
    same = rows // group == cols // group
    return jnp.where(ahead & same, 1.0, 0.0).astype(BF16)


def ranks_of(hits, group):
    parts = hits.astype(BF16)
    within = jnp.dot(parts, strict((128, 128), 1, 128), preferred_element_type=F32)
    above = jnp.dot(strict((hits.shape[0],) * 2, 0, group), parts, preferred_element_type=F32)
    return within + jnp.sum(above, axis=1, keepdims=True)


def blocks_of(index, width, count):
    block = jnp.zeros_like(index)
    for edge in range(1, count):
        block += jnp.where(index >= edge * width, 1, 0)
    return block


def kernel(
    scale,
    tokens_hbm, teacher_hbm, up_hbm, gain_ref, chan_ref, ff_ref,
    out_ref,
    normed, normed_t, packed_x, weights, teacher, up, kept_rows, weight_send, weight_recv,
    target_send, target_recv, unpack, picks, pre, delta, target, ring_b, ring_a, gain, places,
    local_sems, ws_send, ws_recv, ts_send, ts_recv, ag_send, ag_recv, rs_send, rs_recv, px_send, px_recv,
):
    dp = lax.axis_index("dp")
    owner = lax.axis_index("tensor")
    core = owner % 2
    z, x = dp // 4, dp % 4
    a = x + core * (z - x)
    b = z + core * (x - z)

    def dp_of(ao, bo):
        aa, bb = (a + ao) % 4, (b + bo) % 4
        return bb * 4 + aa + core * 3 * (aa - bb)

    def device(ao, bo):
        return (dp_of(ao, bo), owner)

    load_up = pltpu.make_async_copy(up_hbm, up, local_sems.at[0])
    load_teacher = pltpu.make_async_copy(teacher_hbm, teacher, local_sems.at[1])
    load_tokens = pltpu.make_async_copy(tokens_hbm, normed, local_sems.at[2])
    load_up.start()
    load_teacher.start()
    load_tokens.start()
    barrier = pltpu.get_barrier_semaphore()
    for ao, bo in ((1, 0), (3, 0), (0, 1), (0, 3)):
        pl.semaphore_signal(barrier, inc=1, device_id=device(ao, bo), device_id_type=MESH)
    for k in range(1, 8):
        pl.semaphore_signal(barrier, inc=1, device_id=(dp, (owner + k) % 8), device_id_type=MESH)

    chan = chan_ref[...]
    block = blocks_of(chan, 384, 16)
    block_hits = jnp.concatenate([jnp.where(block == s, 1.0, 0.0) for s in range(16)], axis=0)
    block_ranks = ranks_of(block_hits, 32) * block_hits
    rank = block_ranks[0:32, :]
    for s in range(1, 16):
        rank += block_ranks[32 * s : 32 * s + 32, :]
    rank = rank.astype(jnp.int32)
    places[0:32, :] = block * SLOT_ROWS + rank
    places[32:64, :] = jnp.where(block == dp, rank, -1)

    slots = lax.broadcasted_iota(jnp.int32, (SLOT_ROWS, 128), 0)
    found = jnp.zeros((SLOT_ROWS, 128), jnp.int32)
    for r in range(32):
        found += jnp.where(places[32 + r : 33 + r, :] == slots, chan_ref[r : r + 1, :] - dp * 384 + 1, 0)
    row = jnp.sum(found.astype(F32), axis=1, keepdims=True).astype(jnp.int32) - 1
    hot = jnp.where(lax.broadcasted_iota(jnp.int32, (SLOT_ROWS, 384), 1) == row, 1.0, 0.0).astype(BF16)
    load_up.wait()
    kept_rows[...] = jnp.dot(hot, up[...], preferred_element_type=F32).astype(BF16)

    places[64:128, :] = ff_ref[...] - owner * 1536
    local = places[64:128, :]
    mine = (local >= 0) & (local < 1536)
    slot = ranks_of(jnp.where(mine, 1.0, 0.0), 8).astype(jnp.int32)
    places[128:192, :] = jnp.where(mine, slot, -1)

    def make_pick(o, carry):
        slots = lax.broadcasted_iota(jnp.int32, (SLOT_COLS, 128), 0)
        found = jnp.zeros((SLOT_COLS, 128), jnp.int32)
        for r in range(8):
            found += jnp.where(
                places[pl.ds(128 + o * 8 + r, 1), :] == slots, places[pl.ds(64 + o * 8 + r, 1), :] + 1, 0
            )
        column = jnp.sum(found.astype(F32), axis=1, keepdims=True).astype(jnp.int32) - 1
        hot = jnp.where(lax.broadcasted_iota(jnp.int32, (SLOT_COLS, 1536), 1) == column, 1.0, 0.0)
        picks[pl.ds(pl.multiple_of(o * 256, 256), 256), :] = hot.astype(BF16)
        return carry

    def picked(rows, o):
        pick = picks[pl.ds(pl.multiple_of(o * 256, 256), 256), :]
        return lax.dot_general(
            rows, pick, (((1,), (1,)), ((), ())), preferred_element_type=F32
        ).astype(BF16)

    def weight_copy(k, h):
        peer = (owner + k) % 8
        return pltpu.make_async_remote_copy(
            src_ref=weight_send.at[peer, pl.ds(h * SLOT_PIECE, SLOT_PIECE), :],
            dst_ref=weight_recv.at[owner, pl.ds(h * SLOT_PIECE, SLOT_PIECE), :],
            send_sem=ws_send.at[h * 8 + k],
            recv_sem=ws_recv.at[h * 8 + k],
            device_id=(dp, peer),
            device_id_type=MESH,
        )

    def target_copy(k):
        peer = (owner + k) % 8
        return pltpu.make_async_remote_copy(
            src_ref=target_send.at[peer],
            dst_ref=target_recv.at[owner],
            send_sem=ts_send.at[k],
            recv_sem=ts_recv.at[k],
            device_id=(dp, peer),
            device_id_type=MESH,
        )

    pl.semaphore_wait(barrier, 11)

    def pack(i, carry):
        k = 4 + (i + 1) // 2 * (1 - 2 * (i % 2))
        peer = (owner + k) % 8
        make_pick(peer, carry)
        weight_send[peer] = picked(kept_rows[...], peer)
        weight_copy(k, 0).start()
        return carry

    lax.fori_loop(0, 7, pack, 0)
    for h in range(1, PIECES):
        for k in (4, 3, 5, 2, 6, 1, 7):
            weight_copy(k, h).start()
    make_pick(owner, 0)
    weight_send[owner] = picked(kept_rows[...], owner)

    own = ff_ref[pl.ds(pl.multiple_of(owner * 8, 8), 8), :]
    source = blocks_of(own, 1536, 8)
    source_hits = jnp.concatenate([jnp.where(source == s, 1.0, 0.0) for s in range(8)], axis=0)
    source_ranks = ranks_of(source_hits, 8) * source_hits
    arrives = source * SLOT_COLS
    for s in range(8):
        arrives += source_ranks[8 * s : 8 * s + 8, :].astype(jnp.int32)
    places[192:200, :] = arrives

    def make_unpack(s, carry):
        slots = lax.broadcasted_iota(jnp.int32, (256, 128), 0) + s * 256
        for r in range(8):
            hot = jnp.where(places[192 + r : 193 + r, :] == slots, 1.0, 0.0)
            unpack[pl.ds(pl.multiple_of(s * 256, 256), 256), r * 128 : r * 128 + 128] = hot.astype(BF16)
        return carry

    lax.fori_loop(0, 8, make_unpack, 0)

    old = gain_ref[...]
    first = old.astype(BF16)
    second = (old - first.astype(F32)).astype(BF16)
    third = (old - first.astype(F32) - second.astype(F32)).astype(BF16)
    gains = jnp.concatenate([first.astype(F32), second.astype(F32), third.astype(F32)], axis=0).astype(BF16)
    for r in range(32):
        line = chan_ref[r : r + 1, :]
        high = blocks_of(line, 128, 48)
        low = line - high * 128
        hot = jnp.where(lax.broadcasted_iota(jnp.int32, (128, 128), 0) == low, 1.0, 0.0).astype(BF16)
        wide = jnp.dot(gains, hot, preferred_element_type=F32)
        wide = (wide[0:48, :] + wide[48:96, :]) + wide[96:144, :]
        chosen = lax.broadcasted_iota(jnp.int32, (48, 128), 0) == high
        gain[:, r * 128 : r * 128 + 128] = jnp.sum(jnp.where(chosen, wide, 0.0), axis=0, keepdims=True)
    def norm(r, carry):
        rows = pl.ds(pl.multiple_of(r * 32, 32), 32)
        values = normed[rows, :].astype(F32)
        center = jnp.mean(values, axis=1, keepdims=True)
        spread = jnp.mean((values - center) ** 2, axis=1, keepdims=True)
        normed[rows, :] = ((values - center) * lax.rsqrt(spread + 1e-05) * gain[...]).astype(BF16)
        return carry

    def slot_row(ao, bo, h):
        return pl.multiple_of(dp_of(ao, bo) * SLOT_ROWS + h * SLOT_PIECE, 16)

    ag_started = []

    def ag_copy(ring, step, ao, bo, h):
        far = (ao if ring == 0 else bo) != 0
        role = (2 * PIECES if far else 0 if step == 1 else PIECES) + h
        index = role if ring == 0 else 3 * PIECES * (1 + ao) + role
        rows = pl.ds(slot_row(ao, bo, h), SLOT_PIECE)
        return pltpu.make_async_remote_copy(
            src_ref=weights.at[rows, :],
            dst_ref=weights.at[rows, :],
            send_sem=ag_send.at[len(ag_started)],
            recv_sem=ag_recv.at[index],
            device_id=device(step, 0) if ring == 0 else device(0, step),
            device_id_type=MESH,
        )

    def ag_start(ring, step, ao, bo, h):
        copy = ag_copy(ring, step, ao, bo, h)
        copy.start()
        ag_started.append(copy)

    def ag_wait(ring, ao, bo, h):
        offset = ao if ring == 0 else bo
        role = {3: 0, 1: 1, 2: 2}[offset] * PIECES + h
        index = role if ring == 0 else 3 * PIECES * (1 + ao) + role
        rows = pl.ds(slot_row(ao, bo, h), SLOT_PIECE)
        pltpu.make_async_remote_copy(
            src_ref=weights.at[rows, :],
            dst_ref=weights.at[rows, :],
            send_sem=ag_send.at[0],
            recv_sem=ag_recv.at[index],
            device_id=device(1, 0),
            device_id_type=MESH,
        ).wait_recv()

    load_teacher.wait()
    target_recv[owner] = picked(teacher[...], owner)
    for k in (4, 3, 5, 2, 6, 1, 7):
        peer = (owner + k) % 8
        target_send[peer] = picked(teacher[...], peer)
    load_tokens.wait()
    def own_piece(h):
        half = pl.ds(h * SLOT_PIECE, SLOT_PIECE)
        for k in (0, 4, 3, 5, 2, 6, 1, 7):
            source = (owner - k + 8) % 8
            table = unpack[pl.ds(pl.multiple_of(source * 256, 256), 256), :]
            if k == 0:
                pre[half, :] = jnp.dot(weight_send[owner, half, :], table, preferred_element_type=F32)
                continue
            pltpu.make_async_remote_copy(
                src_ref=weight_recv.at[source, half, :],
                dst_ref=weight_recv.at[source, half, :],
                send_sem=ws_send.at[h * 8 + k],
                recv_sem=ws_recv.at[h * 8 + k],
                device_id=(dp, (owner + k) % 8),
                device_id_type=MESH,
            ).wait_recv()
            pre[half, :] += jnp.dot(weight_recv[source, half, :], table, preferred_element_type=F32)
        weights[pl.ds(slot_row(0, 0, h), SLOT_PIECE), :] = pre[half, :].astype(BF16)
        for ring in (0, 1):
            for step in (1, 3):
                ag_start(ring, step, 0, 0, h)

    def chunk_copy(index, turn):
        return pltpu.make_async_remote_copy(
            src_ref=packed_x.at[index],
            dst_ref=packed_x.at[index],
            send_sem=px_send.at[turn],
            recv_sem=px_recv.at[turn],
            device_id=(dp, owner + 1 - 2 * core),
            device_id_type=MESH,
        )

    def permute(turn, carry):
        index = (z * 5 + 2 * turn + core) % 20
        slots = lax.broadcasted_iota(jnp.int32, (256, 128), 0) + index * 256
        total = jnp.zeros((512, 256), F32)
        for part in range(4):
            hot = jnp.concatenate(
                [
                    jnp.where(places[r : r + 1, :] == slots, 1.0, 0.0).astype(BF16)
                    for r in range(part * 8, part * 8 + 8)
                ],
                axis=1,
            )
            total += lax.dot_general(
                normed[:, part * 1024 : part * 1024 + 1024], hot, (((1,), (1,)), ((), ())), preferred_element_type=F32
            )
        packed_x[index] = total.astype(BF16)
        chunk_copy(index, turn).start()
        return carry

    def fill(first, last):
        lax.fori_loop(first, last, permute, 0)

    def take_chunks(first, last):
        @pl.loop(first, last)
        def _(turn):
            chunk_copy((z * 5 + 2 * turn + 1 - core) % 20, turn).wait_recv()

    def multiply_group(zo, first):
        base = ((z + zo) % 4) * 5

        @pl.loop(0, 2)
        def _(n):
            cols = pl.ds(pl.multiple_of(n * 512, 512), 512)
            part = jnp.zeros((512, 512), F32) if first else pre[:, cols]
            for c in range(5):
                depth = pl.ds(pl.multiple_of((base + c) * 256, 256), 256)
                part += jnp.dot(packed_x[base + c], weights[depth, cols], preferred_element_type=F32)
            pre[:, cols] = part

    def relay(ring, ao, bo, h):
        ag_wait(ring, ao, bo, h)
        far = ao if ring == 0 else bo
        if far == 3 and h < PIECES // 2:
            ag_start(ring, 1, ao, bo, h)
        if far == 1 and h >= PIECES // 2:
            ag_start(ring, 3, ao, bo, h)
        if ring == 0:
            ag_start(1, 1, ao, 0, h)
            ag_start(1, 3, ao, 0, h)

    def first_relays(h):
        near = 3 if h < PIECES // 2 else 1
        relay(0, near, 0, h)
        relay(0, 4 - near, 0, h)
        relay(1, 0, near, h)

    own_piece(0)
    lax.fori_loop(0, 4, norm, 0)
    own_piece(1)
    first_relays(0)
    lax.fori_loop(4, 8, norm, 0)
    own_piece(2)
    first_relays(1)
    lax.fori_loop(8, 12, norm, 0)
    own_piece(3)
    for k in (4, 3, 5, 2, 6, 1, 7):
        target_copy(k).start()
    first_relays(2)
    lax.fori_loop(12, 16, norm, 0)
    first_relays(3)
    fill(0, 1)
    relay(0, 2, 0, 0)
    relay(0, 2, 0, 1)
    fill(1, 2)
    relay(1, 3, 3, 0)
    relay(1, 1, 3, 0)
    fill(2, 3)
    relay(0, 2, 0, 2)
    relay(0, 2, 0, 3)
    fill(3, 4)
    relay(1, 3, 3, 1)
    relay(1, 1, 3, 1)
    fill(4, 5)
    relay(1, 3, 1, 2)
    relay(1, 1, 1, 2)
    fill(5, 6)
    relay(1, 3, 1, 3)
    relay(1, 1, 1, 3)
    fill(6, 8)
    relay(1, 2, 3, 0)
    fill(8, 9)
    relay(1, 2, 3, 1)
    fill(9, 10)
    relay(1, 2, 1, 2)

    @pl.loop(0, 16)
    def _(s):
        aa, bb = s // 4, s % 4
        cols = pl.ds(pl.multiple_of((bb * 4 + aa + core * 3 * (aa - bb)) * 256, 256), 256)
        normed_t[pl.ds(pl.multiple_of(s * 256, 256), 256), :] = normed[:, cols].T

    relay(1, 2, 1, 3)

    for k in range(1, 8):
        source = (owner - k + 8) % 8
        pltpu.make_async_remote_copy(
            src_ref=target_recv.at[source],
            dst_ref=target_recv.at[source],
            send_sem=ts_send.at[k],
            recv_sem=ts_recv.at[k],
            device_id=(dp, (owner + k) % 8),
            device_id_type=MESH,
        ).wait_recv()

    @pl.loop(0, 4)
    def _(n):
        cols = pl.ds(pl.multiple_of(n * 256, 256), 256)
        total = jnp.zeros((512, 256), F32)
        for s in range(8):
            total += jnp.dot(target_recv[s], unpack[s * 256 : s * 256 + 256, cols], preferred_element_type=F32)
        target[:, cols] = total.astype(BF16)

    take_chunks(0, 10)
    lower, upper = range(PIECES // 2), range(PIECES // 2, PIECES)

    def group_waits(ao):
        for h in upper:
            ag_wait(1, ao, 3, h)
        for h in lower:
            ag_wait(1, ao, 1, h)
        for h in range(PIECES):
            ag_wait(1, ao, 2, h)

    group_waits(0)
    multiply_group(0, True)
    group_waits(3)
    for ao in (1, 2):
        for h in upper:
            ag_wait(1, ao, 3, h)
    multiply_group(3, False)
    for ao in (1, 2):
        for h in lower:
            ag_wait(1, ao, 1, h)
    for h in range(PIECES):
        ag_wait(1, 1, 2, h)
    multiply_group(1, False)
    for h in range(PIECES):
        ag_wait(1, 2, 2, h)
    multiply_group(2, False)

    @pl.loop(0, 32)
    def _(r):
        rows = pl.ds(pl.multiple_of(r * 16, 16), 16)
        active = jnp.maximum(pre[rows, :], 0.0)
        delta[rows, :] = (2.0 * active * (active * active - target[rows, :].astype(F32)) * scale).astype(BF16)

    for copy in ag_started:
        copy.wait_send()
    for k in range(1, 8):
        for h in range(PIECES):
            weight_copy(k, h).wait_send()
        target_copy(k).wait_send()

    @pl.loop(0, 10)
    def _(turn):
        chunk_copy((z * 5 + 2 * turn + core) % 20, turn).wait_send()

    rs_started = []

    def grad_row(ao, bo, h):
        aa, bb = (a + ao) % 4, (b + bo) % 4
        return pl.multiple_of((aa * 4 + bb) * 256 + h * GRAD_PIECE, GRAD_PIECE)

    def landing(ring, ao, role):
        index = role if ring == 0 else 3 * PIECES * (1 + ao) + role
        place = ring_a if ring == 0 else ring_b
        start = (role if ring == 0 else ao * 3 * PIECES + role) * GRAD_PIECE
        return place.at[pl.ds(start, GRAD_PIECE), :], index

    def rs_start(ring, step, ao, bo, h, role):
        place, index = landing(ring, ao, role)
        copy = pltpu.make_async_remote_copy(
            src_ref=weights.at[pl.ds(grad_row(ao, bo, h), GRAD_PIECE), :],
            dst_ref=place,
            send_sem=rs_send.at[len(rs_started)],
            recv_sem=rs_recv.at[index],
            device_id=device(step, 0) if ring == 0 else device(0, step),
            device_id_type=MESH,
        )
        copy.start()
        rs_started.append(copy)

    def rs_take(ring, ao, role):
        place, index = landing(ring, ao, role)
        pltpu.make_async_remote_copy(
            src_ref=place,
            dst_ref=place,
            send_sem=rs_send.at[0],
            recv_sem=rs_recv.at[index],
            device_id=device(1, 0),
            device_id_type=MESH,
        ).wait_recv()
        return place

    def add_into(ao, bo, h, places_in, final=False):
        base = grad_row(ao, bo, h)

        @pl.loop(0, GRAD_PIECE // 16)
        def _(r):
            total = weights[pl.ds(base + r * 16, 16), :].astype(F32)
            for place in places_in:
                total += place[pl.ds(pl.multiple_of(r * 16, 16), 16), :].astype(F32)
            if final:
                out_ref[pl.ds(pl.multiple_of(h * GRAD_PIECE + r * 16, 16), 16), :] = total
            else:
                weights[pl.ds(base + r * 16, 16), :] = total.astype(BF16)

    def products(ao, bo, count):
        first = ((a + ao) % 4) * 4 + (b + bo) % 4 if count == 1 else ((a + ao) % 4) * 4
        rows = pl.ds(pl.multiple_of(first * 256, 256), 256 * count)

        @pl.loop(0, 4)
        def _(n):
            cols = pl.ds(pl.multiple_of(n * 256, 256), 256)
            weights[rows, cols] = jnp.dot(
                normed_t[rows, :], delta[:, cols], preferred_element_type=F32
            ).astype(BF16)

    left, right = PIECES, 2 * PIECES

    def spread_b(ao, only=None):
        if only in (None, 2):
            for h in lower:
                rs_start(1, 1, ao, 2, h, h)
            for h in upper:
                rs_start(1, 3, ao, 2, h, h)
        if only in (None, 1):
            for h in upper:
                rs_start(1, 1, ao, 1, h, left + h)
        if only in (None, 3):
            for h in lower:
                rs_start(1, 3, ao, 3, h, right + h)

    def relay_b(ao):
        for low, high in zip(lower, upper):
            add_into(ao, 1, low, [rs_take(1, ao, low)])
            rs_start(1, 1, ao, 1, low, left + low)
            add_into(ao, 3, high, [rs_take(1, ao, high)])
            rs_start(1, 3, ao, 3, high, right + high)

    def gather_b(ao, h):
        add_into(ao, 0, h, [rs_take(1, ao, left + h), rs_take(1, ao, right + h)])

    for bo in (2, 1, 3):
        products(2, bo, 1)
        spread_b(2, bo)
    products(1, 0, 4)
    spread_b(1)
    products(3, 0, 4)
    spread_b(3)
    relay_b(2)
    relay_b(1)
    relay_b(3)
    products(0, 0, 4)
    spread_b(0)
    products(2, 0, 1)
    for h in range(PIECES):
        gather_b(2, h)
        rs_start(0, 1 if h in lower else 3, 2, 0, h, h)
    for h in upper:
        gather_b(1, h)
        rs_start(0, 1, 1, 0, h, left + h)
    for h in lower:
        gather_b(3, h)
        rs_start(0, 3, 3, 0, h, right + h)
    for h in lower:
        gather_b(1, h)
        add_into(1, 0, h, [rs_take(0, 0, h)])
        rs_start(0, 1, 1, 0, h, left + h)
    for h in upper:
        gather_b(3, h)
        add_into(3, 0, h, [rs_take(0, 0, h)])
        rs_start(0, 3, 3, 0, h, right + h)
    relay_b(0)
    for h in range(PIECES):
        places_in = [rs_take(ring, 0, side + h) for ring in (1, 0) for side in (left, right)]
        add_into(0, 0, h, places_in, final=True)
    for copy in rs_started:
        copy.wait_send()


def per_device(tokens_in, teacher_hidden, up_old, gain_old, keep_chan, keep_ff):
    scale = 1.0 / math.sqrt(tokens_in.shape[0] * lax.axis_size("dp"))
    anywhere = pl.BlockSpec(memory_space=pl.ANY)
    vmem = pl.BlockSpec(memory_space=pltpu.VMEM)
    dma = pltpu.SemaphoreType.DMA

    def body(*refs):
        kernel(scale, *refs)

    return pl.pallas_call(
        body,
        out_shape=jax.ShapeDtypeStruct((256, 1024), F32),
        in_specs=[anywhere, anywhere, anywhere, vmem, vmem, vmem],
        out_specs=vmem,
        scratch_shapes=[
            pltpu.VMEM((512, 4096), BF16),
            pltpu.VMEM((4096, 512), BF16),
            pltpu.VMEM((20, 512, 256), BF16),
            pltpu.VMEM((5120, 1024), BF16),
            pltpu.VMEM((512, 1536), BF16),
            pltpu.VMEM((384, 1536), BF16),
            pltpu.VMEM((SLOT_ROWS, 1536), BF16),
            pltpu.VMEM((8, SLOT_ROWS, SLOT_COLS), BF16),
            pltpu.VMEM((8, SLOT_ROWS, SLOT_COLS), BF16),
            pltpu.VMEM((8, 512, SLOT_COLS), BF16),
            pltpu.VMEM((8, 512, SLOT_COLS), BF16),
            pltpu.VMEM((2048, 1024), BF16),
            pltpu.VMEM((2048, 1536), BF16),
            pltpu.VMEM((512, 1024), F32),
            pltpu.VMEM((512, 1024), BF16),
            pltpu.VMEM((512, 1024), BF16),
            pltpu.VMEM((24 * 128, 1024), BF16),
            pltpu.VMEM((6 * 128, 1024), BF16),
            pltpu.VMEM((1, 4096), F32),
            pltpu.VMEM((200, 128), jnp.int32),
            dma((3,)),
            dma((8 * PIECES,)),
            dma((8 * PIECES,)),
            dma((8,)),
            dma((8,)),
            dma((15 * PIECES,)),
            dma((15 * PIECES,)),
            dma((15 * PIECES,)),
            dma((15 * PIECES,)),
            dma((10,)),
            dma((10,)),
        ],
        compiler_params=pltpu.CompilerParams(
            collective_id=0, has_side_effects=True, vmem_limit_bytes=62 * 1024 * 1024
        ),
        cost_estimate=pl.CostEstimate(flops=40_000_000_000, bytes_accessed=10_000_000, transcendentals=0),
    )(
        tokens_in, teacher_hidden, up_old,
        gain_old.reshape(48, 128), keep_chan.reshape(32, 128), keep_ff.reshape(64, 128),
    )


def solution(mesh):
    return jax.shard_map(
        per_device,
        mesh=mesh,
        in_specs=(P("dp", None), P("dp", "tensor"), P("dp", "tensor"), P(), P(), P()),
        out_specs=P("dp", "tensor"),
        check_vma=False,
    )
```

```python
import math

import jax
import jax.numpy as jnp
from jax import lax
from jax.experimental import pallas as pl
from jax.experimental.pallas import tpu as pltpu
from jax.sharding import PartitionSpec as P

MESH = pl.DeviceIdType.MESH
SLOT_ROWS = 320
SLOT_COLS = 256
PIECES = 2
SLOT_PIECE = SLOT_ROWS // PIECES
GRAD_PIECE = 256 // PIECES
BF16 = jnp.bfloat16
F32 = jnp.float32


def strict(shape, dim, group):
    rows = lax.broadcasted_iota(jnp.int32, shape, 0)
    cols = lax.broadcasted_iota(jnp.int32, shape, 1)
    ahead = rows < cols if dim == 1 else cols < rows
    same = rows // group == cols // group
    return jnp.where(ahead & same, 1.0, 0.0).astype(BF16)


def ranks_of(hits, group):
    parts = hits.astype(BF16)
    within = jnp.dot(parts, strict((128, 128), 1, 128), preferred_element_type=F32)
    above = jnp.dot(strict((hits.shape[0],) * 2, 0, group), parts, preferred_element_type=F32)
    return within + jnp.sum(above, axis=1, keepdims=True)


def blocks_of(index, width, count):
    block = jnp.zeros_like(index)
    for edge in range(1, count):
        block += jnp.where(index >= edge * width, 1, 0)
    return block


def kernel(
    scale,
    tokens_hbm, teacher_hbm, up_hbm, gain_ref, chan_ref, ff_ref,
    out_ref,
    normed, normed_t, packed_x, weights, teacher, up, kept_rows, weight_send, weight_recv,
    target_send, target_recv, unpack, picks, pre, delta, target, ring_b, ring_a, gain, places,
    local_sems, ws_send, ws_recv, ts_send, ts_recv, ag_send, ag_recv, rs_send, rs_recv, px_send, px_recv,
    hops, hop_send, hop_recv, onward_send,
):
    dp = lax.axis_index("dp")
    owner = lax.axis_index("tensor")
    core = owner % 2
    z, x = dp // 4, dp % 4
    a = x + core * (z - x)
    b = z + core * (x - z)

    def dp_of(ao, bo):
        aa, bb = (a + ao) % 4, (b + bo) % 4
        return bb * 4 + aa + core * 3 * (aa - bb)

    def device(ao, bo):
        return (dp_of(ao, bo), owner)

    load_up = pltpu.make_async_copy(up_hbm, up, local_sems.at[0])
    load_teacher = pltpu.make_async_copy(teacher_hbm, teacher, local_sems.at[1])
    load_tokens = pltpu.make_async_copy(tokens_hbm, normed, local_sems.at[2])
    load_up.start()
    load_teacher.start()
    load_tokens.start()
    barrier = pltpu.get_barrier_semaphore()
    for ao, bo in ((1, 0), (3, 0), (0, 1), (0, 3)):
        pl.semaphore_signal(barrier, inc=1, device_id=device(ao, bo), device_id_type=MESH)
    for k in range(1, 8):
        pl.semaphore_signal(barrier, inc=1, device_id=(dp, (owner + k) % 8), device_id_type=MESH)

    chan = chan_ref[...]
    block = blocks_of(chan, 384, 16)
    block_hits = jnp.concatenate([jnp.where(block == s, 1.0, 0.0) for s in range(16)], axis=0)
    block_ranks = ranks_of(block_hits, 32) * block_hits
    rank = block_ranks[0:32, :]
    for s in range(1, 16):
        rank += block_ranks[32 * s : 32 * s + 32, :]
    rank = rank.astype(jnp.int32)
    places[0:32, :] = block * SLOT_ROWS + rank
    places[32:64, :] = jnp.where(block == dp, rank, -1)

    slots = lax.broadcasted_iota(jnp.int32, (SLOT_ROWS, 128), 0)
    found = jnp.zeros((SLOT_ROWS, 128), jnp.int32)
    for r in range(32):
        found += jnp.where(places[32 + r : 33 + r, :] == slots, chan_ref[r : r + 1, :] - dp * 384 + 1, 0)
    row = jnp.sum(found.astype(F32), axis=1, keepdims=True).astype(jnp.int32) - 1
    hot = jnp.where(lax.broadcasted_iota(jnp.int32, (SLOT_ROWS, 384), 1) == row, 1.0, 0.0).astype(BF16)
    load_up.wait()
    kept_rows[...] = jnp.dot(hot, up[...], preferred_element_type=F32).astype(BF16)

    places[64:128, :] = ff_ref[...] - owner * 1536
    local = places[64:128, :]
    mine = (local >= 0) & (local < 1536)
    slot = ranks_of(jnp.where(mine, 1.0, 0.0), 8).astype(jnp.int32)
    places[128:192, :] = jnp.where(mine, slot, -1)

    def make_pick(o, carry):
        slots = lax.broadcasted_iota(jnp.int32, (SLOT_COLS, 128), 0)
        found = jnp.zeros((SLOT_COLS, 128), jnp.int32)
        for r in range(8):
            found += jnp.where(
                places[pl.ds(128 + o * 8 + r, 1), :] == slots, places[pl.ds(64 + o * 8 + r, 1), :] + 1, 0
            )
        column = jnp.sum(found.astype(F32), axis=1, keepdims=True).astype(jnp.int32) - 1
        hot = jnp.where(lax.broadcasted_iota(jnp.int32, (SLOT_COLS, 1536), 1) == column, 1.0, 0.0)
        picks[pl.ds(pl.multiple_of(o * 256, 256), 256), :] = hot.astype(BF16)
        return carry

    def picked(rows, o):
        pick = picks[pl.ds(pl.multiple_of(o * 256, 256), 256), :]
        return lax.dot_general(
            rows, pick, (((1,), (1,)), ((), ())), preferred_element_type=F32
        ).astype(BF16)

    def weight_copy(k, h):
        peer = (owner + k) % 8
        return pltpu.make_async_remote_copy(
            src_ref=weight_send.at[peer, pl.ds(h * SLOT_PIECE, SLOT_PIECE), :],
            dst_ref=weight_recv.at[owner, pl.ds(h * SLOT_PIECE, SLOT_PIECE), :],
            send_sem=ws_send.at[h * 8 + k],
            recv_sem=ws_recv.at[h * 8 + k],
            device_id=(dp, peer),
            device_id_type=MESH,
        )

    def target_copy(k):
        peer = (owner + k) % 8
        return pltpu.make_async_remote_copy(
            src_ref=target_send.at[peer],
            dst_ref=target_recv.at[owner],
            send_sem=ts_send.at[k],
            recv_sem=ts_recv.at[k],
            device_id=(dp, peer),
            device_id_type=MESH,
        )

    pl.semaphore_wait(barrier, 11)

    near, beyond = 3 + 2 * core, 5 - 2 * core

    def hop_copy(way, j):
        peer = (owner + (4 if j == 0 else beyond)) % 8
        return pltpu.make_async_remote_copy(
            src_ref=weight_send.at[peer, pl.ds(way * SLOT_PIECE, SLOT_PIECE), :],
            dst_ref=hops.at[2 * way + j],
            send_sem=hop_send.at[2 * way + j],
            recv_sem=hop_recv.at[2 * way + j],
            device_id=(dp, (owner + (2 if way == 0 else 6)) % 8),
            device_id_type=MESH,
        )

    def onward_copy(way, j):
        origin = (owner + (6 if way == 0 else 2)) % 8
        k = 4 if j == 0 else beyond
        return pltpu.make_async_remote_copy(
            src_ref=hops.at[2 * way + j],
            dst_ref=weight_recv.at[origin, pl.ds(way * SLOT_PIECE, SLOT_PIECE), :],
            send_sem=onward_send.at[2 * way + j],
            recv_sem=ws_recv.at[way * 8 + k],
            device_id=(dp, (origin + k) % 8),
            device_id_type=MESH,
        )

    def pack(k):
        peer = (owner + k) % 8
        make_pick(peer, 0)
        weight_send[peer] = picked(kept_rows[...], peer)

    for j in range(2):
        pack(beyond if j == 1 else 4)
        for way in range(2):
            hop_copy(way, j).start()
    for k in (2, 6, near):
        pack(k)
        weight_copy(k, 0).start()
    for k in (1, 7):
        pack(k)
        weight_copy(k, 0).start()
    for k in (2, 6, near, 1, 7):
        weight_copy(k, 1).start()
    pack(0)

    own = ff_ref[pl.ds(pl.multiple_of(owner * 8, 8), 8), :]
    source = blocks_of(own, 1536, 8)
    source_hits = jnp.concatenate([jnp.where(source == s, 1.0, 0.0) for s in range(8)], axis=0)
    source_ranks = ranks_of(source_hits, 8) * source_hits
    arrives = source * SLOT_COLS
    for s in range(8):
        arrives += source_ranks[8 * s : 8 * s + 8, :].astype(jnp.int32)
    places[192:200, :] = arrives

    def make_unpack(s, carry):
        slots = lax.broadcasted_iota(jnp.int32, (256, 128), 0) + s * 256
        for r in range(8):
            hot = jnp.where(places[192 + r : 193 + r, :] == slots, 1.0, 0.0)
            unpack[pl.ds(pl.multiple_of(s * 256, 256), 256), r * 128 : r * 128 + 128] = hot.astype(BF16)
        return carry

    lax.fori_loop(0, 8, make_unpack, 0)

    old = gain_ref[...]
    first = old.astype(BF16)
    second = (old - first.astype(F32)).astype(BF16)
    third = (old - first.astype(F32) - second.astype(F32)).astype(BF16)
    gains = jnp.concatenate([first.astype(F32), second.astype(F32), third.astype(F32)], axis=0).astype(BF16)
    for r in range(32):
        line = chan_ref[r : r + 1, :]
        high = blocks_of(line, 128, 48)
        low = line - high * 128
        hot = jnp.where(lax.broadcasted_iota(jnp.int32, (128, 128), 0) == low, 1.0, 0.0).astype(BF16)
        wide = jnp.dot(gains, hot, preferred_element_type=F32)
        wide = (wide[0:48, :] + wide[48:96, :]) + wide[96:144, :]
        chosen = lax.broadcasted_iota(jnp.int32, (48, 128), 0) == high
        gain[:, r * 128 : r * 128 + 128] = jnp.sum(jnp.where(chosen, wide, 0.0), axis=0, keepdims=True)
    def norm(r, carry):
        rows = pl.ds(pl.multiple_of(r * 32, 32), 32)
        values = normed[rows, :].astype(F32)
        center = jnp.mean(values, axis=1, keepdims=True)
        spread = jnp.mean((values - center) ** 2, axis=1, keepdims=True)
        normed[rows, :] = ((values - center) * lax.rsqrt(spread + 1e-05) * gain[...]).astype(BF16)
        return carry

    def slot_row(ao, bo, h):
        return pl.multiple_of(dp_of(ao, bo) * SLOT_ROWS + h * SLOT_PIECE, 16)

    ag_started = []

    def ag_copy(ring, step, ao, bo, h):
        far = (ao if ring == 0 else bo) != 0
        role = (2 * PIECES if far else 0 if step == 1 else PIECES) + h
        index = role if ring == 0 else 3 * PIECES * (1 + ao) + role
        rows = pl.ds(slot_row(ao, bo, h), SLOT_PIECE)
        return pltpu.make_async_remote_copy(
            src_ref=weights.at[rows, :],
            dst_ref=weights.at[rows, :],
            send_sem=ag_send.at[len(ag_started)],
            recv_sem=ag_recv.at[index],
            device_id=device(step, 0) if ring == 0 else device(0, step),
            device_id_type=MESH,
        )

    def ag_start(ring, step, ao, bo, h):
        copy = ag_copy(ring, step, ao, bo, h)
        copy.start()
        ag_started.append(copy)

    def ag_wait(ring, ao, bo, h):
        offset = ao if ring == 0 else bo
        role = {3: 0, 1: 1, 2: 2}[offset] * PIECES + h
        index = role if ring == 0 else 3 * PIECES * (1 + ao) + role
        rows = pl.ds(slot_row(ao, bo, h), SLOT_PIECE)
        pltpu.make_async_remote_copy(
            src_ref=weights.at[rows, :],
            dst_ref=weights.at[rows, :],
            send_sem=ag_send.at[0],
            recv_sem=ag_recv.at[index],
            device_id=device(1, 0),
            device_id_type=MESH,
        ).wait_recv()

    for way in range(2):
        for j in range(2):
            hop_copy(way, j).wait_recv()
            onward_copy(way, j).start()
    load_teacher.wait()
    target_recv[owner] = picked(teacher[...], owner)
    for k in (4, 3, 5, 2, 6, 1, 7):
        peer = (owner + k) % 8
        target_send[peer] = picked(teacher[...], peer)
    load_tokens.wait()
    def own_piece(h):
        half = pl.ds(h * SLOT_PIECE, SLOT_PIECE)
        for k in (0, 1, 7, 2, 6, 3, 5, 4):
            source = (owner - k + 8) % 8
            table = unpack[pl.ds(pl.multiple_of(source * 256, 256), 256), :]
            if k == 0:
                pre[half, :] = jnp.dot(weight_send[owner, half, :], table, preferred_element_type=F32)
                continue
            pltpu.make_async_remote_copy(
                src_ref=weight_recv.at[source, half, :],
                dst_ref=weight_recv.at[source, half, :],
                send_sem=ws_send.at[h * 8 + k],
                recv_sem=ws_recv.at[h * 8 + k],
                device_id=(dp, (owner + k) % 8),
                device_id_type=MESH,
            ).wait_recv()
            pre[half, :] += jnp.dot(weight_recv[source, half, :], table, preferred_element_type=F32)
        weights[pl.ds(slot_row(0, 0, h), SLOT_PIECE), :] = pre[half, :].astype(BF16)
        for ring in (0, 1):
            for step in (1, 3):
                ag_start(ring, step, 0, 0, h)

    def chunk_copy(index, turn):
        return pltpu.make_async_remote_copy(
            src_ref=packed_x.at[index],
            dst_ref=packed_x.at[index],
            send_sem=px_send.at[turn],
            recv_sem=px_recv.at[turn],
            device_id=(dp, owner + 1 - 2 * core),
            device_id_type=MESH,
        )

    def permute(turn, carry):
        index = (z * 5 + 2 * turn + core) % 20
        slots = lax.broadcasted_iota(jnp.int32, (256, 128), 0) + index * 256
        total = jnp.zeros((512, 256), F32)
        for part in range(4):
            hot = jnp.concatenate(
                [
                    jnp.where(places[r : r + 1, :] == slots, 1.0, 0.0).astype(BF16)
                    for r in range(part * 8, part * 8 + 8)
                ],
                axis=1,
            )
            total += lax.dot_general(
                normed[:, part * 1024 : part * 1024 + 1024], hot, (((1,), (1,)), ((), ())), preferred_element_type=F32
            )
        packed_x[index] = total.astype(BF16)
        chunk_copy(index, turn).start()
        return carry

    def fill(first, last):
        lax.fori_loop(first, last, permute, 0)

    def take_chunks(first, last):
        @pl.loop(first, last)
        def _(turn):
            chunk_copy((z * 5 + 2 * turn + 1 - core) % 20, turn).wait_recv()

    def multiply_group(zo, first):
        base = ((z + zo) % 4) * 5

        @pl.loop(0, 2)
        def _(n):
            cols = pl.ds(pl.multiple_of(n * 512, 512), 512)
            part = jnp.zeros((512, 512), F32) if first else pre[:, cols]
            for c in range(5):
                depth = pl.ds(pl.multiple_of((base + c) * 256, 256), 256)
                part += jnp.dot(packed_x[base + c], weights[depth, cols], preferred_element_type=F32)
            pre[:, cols] = part

    def relay(ring, ao, bo, h):
        ag_wait(ring, ao, bo, h)
        far = ao if ring == 0 else bo
        if far == 3 and h < PIECES // 2:
            ag_start(ring, 1, ao, bo, h)
        if far == 1 and h >= PIECES // 2:
            ag_start(ring, 3, ao, bo, h)
        if ring == 0:
            ag_start(1, 1, ao, 0, h)
            ag_start(1, 3, ao, 0, h)

    def first_relays(h):
        side = 3 if h < PIECES // 2 else 1
        relay(0, side, 0, h)
        relay(0, 4 - side, 0, h)
        relay(1, 0, side, h)

    own_piece(0)
    lax.fori_loop(0, 8, norm, 0)
    first_relays(0)
    own_piece(1)
    for k in (4, 3, 5, 2, 6, 1, 7):
        target_copy(k).start()
    lax.fori_loop(8, 16, norm, 0)
    first_relays(1)
    fill(0, 1)
    relay(0, 2, 0, 0)
    fill(1, 2)
    relay(1, 3, 3, 0)
    relay(1, 1, 3, 0)
    fill(2, 3)
    relay(0, 2, 0, 1)
    fill(3, 4)
    relay(1, 3, 1, 1)
    relay(1, 1, 1, 1)
    fill(4, 7)
    relay(1, 2, 3, 0)
    fill(7, 9)

    @pl.loop(0, 16)
    def _(s):
        aa, bb = s // 4, s % 4
        cols = pl.ds(pl.multiple_of((bb * 4 + aa + core * 3 * (aa - bb)) * 256, 256), 256)
        normed_t[pl.ds(pl.multiple_of(s * 256, 256), 256), :] = normed[:, cols].T

    relay(1, 2, 1, 1)
    fill(9, 10)

    for k in range(1, 8):
        source = (owner - k + 8) % 8
        pltpu.make_async_remote_copy(
            src_ref=target_recv.at[source],
            dst_ref=target_recv.at[source],
            send_sem=ts_send.at[k],
            recv_sem=ts_recv.at[k],
            device_id=(dp, (owner + k) % 8),
            device_id_type=MESH,
        ).wait_recv()

    @pl.loop(0, 4)
    def _(n):
        cols = pl.ds(pl.multiple_of(n * 256, 256), 256)
        total = jnp.zeros((512, 256), F32)
        for s in range(8):
            total += jnp.dot(target_recv[s], unpack[s * 256 : s * 256 + 256, cols], preferred_element_type=F32)
        target[:, cols] = total.astype(BF16)

    take_chunks(0, 10)
    lower, upper = range(PIECES // 2), range(PIECES // 2, PIECES)

    def group_waits(ao):
        for h in upper:
            ag_wait(1, ao, 3, h)
        for h in lower:
            ag_wait(1, ao, 1, h)
        for h in range(PIECES):
            ag_wait(1, ao, 2, h)

    group_waits(0)
    multiply_group(0, True)
    group_waits(3)
    for ao in (1, 2):
        for h in upper:
            ag_wait(1, ao, 3, h)
    multiply_group(3, False)
    for ao in (1, 2):
        for h in lower:
            ag_wait(1, ao, 1, h)
    for h in range(PIECES):
        ag_wait(1, 1, 2, h)
    multiply_group(1, False)
    for h in range(PIECES):
        ag_wait(1, 2, 2, h)
    multiply_group(2, False)

    @pl.loop(0, 32)
    def _(r):
        rows = pl.ds(pl.multiple_of(r * 16, 16), 16)
        active = jnp.maximum(pre[rows, :], 0.0)
        delta[rows, :] = (2.0 * active * (active * active - target[rows, :].astype(F32)) * scale).astype(BF16)

    for copy in ag_started:
        copy.wait_send()
    for k in range(1, 8):
        target_copy(k).wait_send()
    for k in (2, 6, near, 1, 7):
        for h in range(PIECES):
            weight_copy(k, h).wait_send()
    for way in range(2):
        for j in range(2):
            hop_copy(way, j).wait_send()
            onward_copy(way, j).wait_send()

    @pl.loop(0, 10)
    def _(turn):
        chunk_copy((z * 5 + 2 * turn + core) % 20, turn).wait_send()

    rs_started = []

    def grad_row(ao, bo, h):
        aa, bb = (a + ao) % 4, (b + bo) % 4
        return pl.multiple_of((aa * 4 + bb) * 256 + h * GRAD_PIECE, GRAD_PIECE)

    def landing(ring, ao, role):
        index = role if ring == 0 else 3 * PIECES * (1 + ao) + role
        place = ring_a if ring == 0 else ring_b
        start = (role if ring == 0 else ao * 3 * PIECES + role) * GRAD_PIECE
        return place.at[pl.ds(start, GRAD_PIECE), :], index

    def rs_start(ring, step, ao, bo, h, role):
        place, index = landing(ring, ao, role)
        copy = pltpu.make_async_remote_copy(
            src_ref=weights.at[pl.ds(grad_row(ao, bo, h), GRAD_PIECE), :],
            dst_ref=place,
            send_sem=rs_send.at[len(rs_started)],
            recv_sem=rs_recv.at[index],
            device_id=device(step, 0) if ring == 0 else device(0, step),
            device_id_type=MESH,
        )
        copy.start()
        rs_started.append(copy)

    def rs_take(ring, ao, role):
        place, index = landing(ring, ao, role)
        pltpu.make_async_remote_copy(
            src_ref=place,
            dst_ref=place,
            send_sem=rs_send.at[0],
            recv_sem=rs_recv.at[index],
            device_id=device(1, 0),
            device_id_type=MESH,
        ).wait_recv()
        return place

    def add_into(ao, bo, h, places_in, final=False):
        base = grad_row(ao, bo, h)

        @pl.loop(0, GRAD_PIECE // 16)
        def _(r):
            total = weights[pl.ds(base + r * 16, 16), :].astype(F32)
            for place in places_in:
                total += place[pl.ds(pl.multiple_of(r * 16, 16), 16), :].astype(F32)
            if final:
                out_ref[pl.ds(pl.multiple_of(h * GRAD_PIECE + r * 16, 16), 16), :] = total
            else:
                weights[pl.ds(base + r * 16, 16), :] = total.astype(BF16)

    def products(ao, bo, count):
        first = ((a + ao) % 4) * 4 + (b + bo) % 4 if count == 1 else ((a + ao) % 4) * 4
        rows = pl.ds(pl.multiple_of(first * 256, 256), 256 * count)

        @pl.loop(0, 4)
        def _(n):
            cols = pl.ds(pl.multiple_of(n * 256, 256), 256)
            weights[rows, cols] = jnp.dot(
                normed_t[rows, :], delta[:, cols], preferred_element_type=F32
            ).astype(BF16)

    left, right = PIECES, 2 * PIECES

    def spread_b(ao, only=None):
        if only in (None, 2):
            for h in lower:
                rs_start(1, 1, ao, 2, h, h)
            for h in upper:
                rs_start(1, 3, ao, 2, h, h)
        if only in (None, 1):
            for h in upper:
                rs_start(1, 1, ao, 1, h, left + h)
        if only in (None, 3):
            for h in lower:
                rs_start(1, 3, ao, 3, h, right + h)

    def relay_b(ao):
        for low, high in zip(lower, upper):
            add_into(ao, 1, low, [rs_take(1, ao, low)])
            rs_start(1, 1, ao, 1, low, left + low)
            add_into(ao, 3, high, [rs_take(1, ao, high)])
            rs_start(1, 3, ao, 3, high, right + high)

    def gather_b(ao, h):
        add_into(ao, 0, h, [rs_take(1, ao, left + h), rs_take(1, ao, right + h)])

    for bo in (2, 1, 3):
        products(2, bo, 1)
        spread_b(2, bo)
    products(1, 0, 4)
    spread_b(1)
    products(3, 0, 4)
    spread_b(3)
    relay_b(2)
    relay_b(1)
    relay_b(3)
    products(0, 0, 4)
    spread_b(0)
    products(2, 0, 1)
    for h in range(PIECES):
        gather_b(2, h)
        rs_start(0, 1 if h in lower else 3, 2, 0, h, h)
    for h in upper:
        gather_b(1, h)
        rs_start(0, 1, 1, 0, h, left + h)
    for h in lower:
        gather_b(3, h)
        rs_start(0, 3, 3, 0, h, right + h)
    for h in lower:
        gather_b(1, h)
        add_into(1, 0, h, [rs_take(0, 0, h)])
        rs_start(0, 1, 1, 0, h, left + h)
    for h in upper:
        gather_b(3, h)
        add_into(3, 0, h, [rs_take(0, 0, h)])
        rs_start(0, 3, 3, 0, h, right + h)
    relay_b(0)
    for h in range(PIECES):
        places_in = [rs_take(ring, 0, side + h) for ring in (1, 0) for side in (left, right)]
        add_into(0, 0, h, places_in, final=True)
    for copy in rs_started:
        copy.wait_send()


def per_device(tokens_in, teacher_hidden, up_old, gain_old, keep_chan, keep_ff):
    scale = 1.0 / math.sqrt(tokens_in.shape[0] * lax.axis_size("dp"))
    anywhere = pl.BlockSpec(memory_space=pl.ANY)
    vmem = pl.BlockSpec(memory_space=pltpu.VMEM)
    dma = pltpu.SemaphoreType.DMA

    def body(*refs):
        kernel(scale, *refs)

    return pl.pallas_call(
        body,
        out_shape=jax.ShapeDtypeStruct((256, 1024), F32),
        in_specs=[anywhere, anywhere, anywhere, vmem, vmem, vmem],
        out_specs=vmem,
        scratch_shapes=[
            pltpu.VMEM((512, 4096), BF16),
            pltpu.VMEM((4096, 512), BF16),
            pltpu.VMEM((20, 512, 256), BF16),
            pltpu.VMEM((5120, 1024), BF16),
            pltpu.VMEM((512, 1536), BF16),
            pltpu.VMEM((384, 1536), BF16),
            pltpu.VMEM((SLOT_ROWS, 1536), BF16),
            pltpu.VMEM((8, SLOT_ROWS, SLOT_COLS), BF16),
            pltpu.VMEM((8, SLOT_ROWS, SLOT_COLS), BF16),
            pltpu.VMEM((8, 512, SLOT_COLS), BF16),
            pltpu.VMEM((8, 512, SLOT_COLS), BF16),
            pltpu.VMEM((2048, 1024), BF16),
            pltpu.VMEM((2048, 1536), BF16),
            pltpu.VMEM((512, 1024), F32),
            pltpu.VMEM((512, 1024), BF16),
            pltpu.VMEM((512, 1024), BF16),
            pltpu.VMEM((24 * 128, 1024), BF16),
            pltpu.VMEM((6 * 128, 1024), BF16),
            pltpu.VMEM((1, 4096), F32),
            pltpu.VMEM((200, 128), jnp.int32),
            dma((3,)),
            dma((8 * PIECES,)),
            dma((8 * PIECES,)),
            dma((8,)),
            dma((8,)),
            dma((15 * PIECES,)),
            dma((15 * PIECES,)),
            dma((15 * PIECES,)),
            dma((15 * PIECES,)),
            dma((10,)),
            dma((10,)),
            pltpu.VMEM((4, SLOT_PIECE, SLOT_COLS), BF16),
            dma((4,)),
            dma((4,)),
            dma((4,)),
        ],
        compiler_params=pltpu.CompilerParams(
            collective_id=0, has_side_effects=True, vmem_limit_bytes=62 * 1024 * 1024
        ),
        cost_estimate=pl.CostEstimate(flops=40_000_000_000, bytes_accessed=10_000_000, transcendentals=0),
    )(
        tokens_in, teacher_hidden, up_old,
        gain_old.reshape(48, 128), keep_chan.reshape(32, 128), keep_ff.reshape(64, 128),
    )


def solution(mesh):
    return jax.shard_map(
        per_device,
        mesh=mesh,
        in_specs=(P("dp", None), P("dp", "tensor"), P("dp", "tensor"), P(), P(), P()),
        out_specs=P("dp", "tensor"),
        check_vma=False,
    )
```

```python
import math

import jax
import jax.numpy as jnp
from jax import lax
from jax.experimental import pallas as pl
from jax.experimental.pallas import tpu as pltpu
from jax.sharding import PartitionSpec as P

MESH = pl.DeviceIdType.MESH
SLOT_ROWS = 320
SLOT_COLS = 256
BF16 = jnp.bfloat16
F32 = jnp.float32


def strict(shape, dim, group):
    rows = lax.broadcasted_iota(jnp.int32, shape, 0)
    cols = lax.broadcasted_iota(jnp.int32, shape, 1)
    ahead = rows < cols if dim == 1 else cols < rows
    same = rows // group == cols // group
    return jnp.where(ahead & same, 1.0, 0.0).astype(BF16)


def ranks_of(hits, group):
    parts = hits.astype(BF16)
    within = jnp.dot(parts, strict((128, 128), 1, 128), preferred_element_type=F32)
    above = jnp.dot(strict((hits.shape[0],) * 2, 0, group), parts, preferred_element_type=F32)
    return within + jnp.sum(above, axis=1, keepdims=True)


def blocks_of(index, width, count):
    block = jnp.zeros_like(index)
    for edge in range(1, count):
        block += jnp.where(index >= edge * width, 1, 0)
    return block


def kernel(
    scale,
    tokens_hbm, teacher_hbm, up_hbm, gain_ref, chan_ref, ff_ref,
    out_ref,
    normed, normed_t, packed_x, weights, teacher, up, kept_rows, weight_send, weight_recv,
    target_send, target_recv, unpack, picks, pre, delta, target, ring_b, ring_a, gain, places,
    local_sems, ws_send, ws_recv, ts_send, ts_recv, ag_send, ag_recv, rs_send, rs_recv, px_send, px_recv,
):
    dp = lax.axis_index("dp")
    owner = lax.axis_index("tensor")
    core = owner % 2
    z, x = dp // 4, dp % 4
    a = x + core * (z - x)
    b = z + core * (x - z)

    def dp_of(ao, bo):
        aa, bb = (a + ao) % 4, (b + bo) % 4
        return bb * 4 + aa + core * 3 * (aa - bb)

    def device(ao, bo):
        return (dp_of(ao, bo), owner)

    load_up = pltpu.make_async_copy(up_hbm, up, local_sems.at[0])
    load_teacher = pltpu.make_async_copy(teacher_hbm, teacher, local_sems.at[1])
    load_tokens = pltpu.make_async_copy(tokens_hbm, normed, local_sems.at[2])
    load_up.start()
    load_teacher.start()
    load_tokens.start()
    barrier = pltpu.get_barrier_semaphore()
    for ao, bo in ((1, 0), (3, 0), (0, 1), (0, 3)):
        pl.semaphore_signal(barrier, inc=1, device_id=device(ao, bo), device_id_type=MESH)
    for k in range(1, 8):
        pl.semaphore_signal(barrier, inc=1, device_id=(dp, (owner + k) % 8), device_id_type=MESH)

    chan = chan_ref[...]
    block = blocks_of(chan, 384, 16)
    block_hits = jnp.concatenate([jnp.where(block == s, 1.0, 0.0) for s in range(16)], axis=0)
    block_ranks = ranks_of(block_hits, 32) * block_hits
    rank = block_ranks[0:32, :]
    for s in range(1, 16):
        rank += block_ranks[32 * s : 32 * s + 32, :]
    rank = rank.astype(jnp.int32)
    places[0:32, :] = block * SLOT_ROWS + rank
    places[32:64, :] = jnp.where(block == dp, rank, -1)

    slots = lax.broadcasted_iota(jnp.int32, (SLOT_ROWS, 128), 0)
    found = jnp.zeros((SLOT_ROWS, 128), jnp.int32)
    for r in range(32):
        found += jnp.where(places[32 + r : 33 + r, :] == slots, chan_ref[r : r + 1, :] - dp * 384 + 1, 0)
    row = jnp.sum(found.astype(F32), axis=1, keepdims=True).astype(jnp.int32) - 1
    hot = jnp.where(lax.broadcasted_iota(jnp.int32, (SLOT_ROWS, 384), 1) == row, 1.0, 0.0).astype(BF16)
    load_up.wait()
    kept_rows[...] = jnp.dot(hot, up[...], preferred_element_type=F32).astype(BF16)

    places[64:128, :] = ff_ref[...] - owner * 1536
    local = places[64:128, :]
    mine = (local >= 0) & (local < 1536)
    slot = ranks_of(jnp.where(mine, 1.0, 0.0), 8).astype(jnp.int32)
    places[128:192, :] = jnp.where(mine, slot, -1)

    def make_pick(o, carry):
        slots = lax.broadcasted_iota(jnp.int32, (SLOT_COLS, 128), 0)
        found = jnp.zeros((SLOT_COLS, 128), jnp.int32)
        for r in range(8):
            found += jnp.where(
                places[pl.ds(128 + o * 8 + r, 1), :] == slots, places[pl.ds(64 + o * 8 + r, 1), :] + 1, 0
            )
        column = jnp.sum(found.astype(F32), axis=1, keepdims=True).astype(jnp.int32) - 1
        hot = jnp.where(lax.broadcasted_iota(jnp.int32, (SLOT_COLS, 1536), 1) == column, 1.0, 0.0)
        picks[pl.ds(pl.multiple_of(o * 256, 256), 256), :] = hot.astype(BF16)
        return carry

    def picked(rows, o):
        pick = picks[pl.ds(pl.multiple_of(o * 256, 256), 256), :]
        return lax.dot_general(
            rows, pick, (((1,), (1,)), ((), ())), preferred_element_type=F32
        ).astype(BF16)

    def weight_copy(k, h):
        peer = (owner + k) % 8
        return pltpu.make_async_remote_copy(
            src_ref=weight_send.at[peer, pl.ds(h * 160, 160), :],
            dst_ref=weight_recv.at[owner, pl.ds(h * 160, 160), :],
            send_sem=ws_send.at[h * 8 + k],
            recv_sem=ws_recv.at[h * 8 + k],
            device_id=(dp, peer),
            device_id_type=MESH,
        )

    def target_copy(k):
        peer = (owner + k) % 8
        return pltpu.make_async_remote_copy(
            src_ref=target_send.at[peer],
            dst_ref=target_recv.at[owner],
            send_sem=ts_send.at[k],
            recv_sem=ts_recv.at[k],
            device_id=(dp, peer),
            device_id_type=MESH,
        )

    pl.semaphore_wait(barrier, 11)

    def pack(i, carry):
        k = 4 + (i + 1) // 2 * (1 - 2 * (i % 2))
        peer = (owner + k) % 8
        make_pick(peer, carry)
        weight_send[peer] = picked(kept_rows[...], peer)
        weight_copy(k, 0).start()
        return carry

    lax.fori_loop(0, 7, pack, 0)
    make_pick(owner, 0)
    weight_send[owner] = picked(kept_rows[...], owner)

    own = ff_ref[pl.ds(pl.multiple_of(owner * 8, 8), 8), :]
    source = blocks_of(own, 1536, 8)
    source_hits = jnp.concatenate([jnp.where(source == s, 1.0, 0.0) for s in range(8)], axis=0)
    source_ranks = ranks_of(source_hits, 8) * source_hits
    arrives = source * SLOT_COLS
    for s in range(8):
        arrives += source_ranks[8 * s : 8 * s + 8, :].astype(jnp.int32)
    places[192:200, :] = arrives

    def make_unpack(s, carry):
        slots = lax.broadcasted_iota(jnp.int32, (256, 128), 0) + s * 256
        for r in range(8):
            hot = jnp.where(places[192 + r : 193 + r, :] == slots, 1.0, 0.0)
            unpack[pl.ds(pl.multiple_of(s * 256, 256), 256), r * 128 : r * 128 + 128] = hot.astype(BF16)
        return carry

    lax.fori_loop(0, 8, make_unpack, 0)

    old = gain_ref[...]
    first = old.astype(BF16)
    second = (old - first.astype(F32)).astype(BF16)
    third = (old - first.astype(F32) - second.astype(F32)).astype(BF16)
    gains = jnp.concatenate([first.astype(F32), second.astype(F32), third.astype(F32)], axis=0).astype(BF16)
    for r in range(32):
        line = chan_ref[r : r + 1, :]
        high = blocks_of(line, 128, 48)
        low = line - high * 128
        hot = jnp.where(lax.broadcasted_iota(jnp.int32, (128, 128), 0) == low, 1.0, 0.0).astype(BF16)
        wide = jnp.dot(gains, hot, preferred_element_type=F32)
        wide = (wide[0:48, :] + wide[48:96, :]) + wide[96:144, :]
        chosen = lax.broadcasted_iota(jnp.int32, (48, 128), 0) == high
        gain[:, r * 128 : r * 128 + 128] = jnp.sum(jnp.where(chosen, wide, 0.0), axis=0, keepdims=True)
    def norm(r, carry):
        rows = pl.ds(pl.multiple_of(r * 32, 32), 32)
        values = normed[rows, :].astype(F32)
        center = jnp.mean(values, axis=1, keepdims=True)
        spread = jnp.mean((values - center) ** 2, axis=1, keepdims=True)
        normed[rows, :] = ((values - center) * lax.rsqrt(spread + 1e-05) * gain[...]).astype(BF16)
        return carry

    def slot_row(ao, bo, h):
        return pl.multiple_of(dp_of(ao, bo) * SLOT_ROWS + h * 160, 32)

    ag_started = []

    def ag_copy(ring, step, ao, bo, h):
        far = (ao if ring == 0 else bo) != 0
        role = (4 + h) if far else ((0 if step == 1 else 2) + h)
        index = role if ring == 0 else 6 + ao * 6 + role
        rows = pl.ds(slot_row(ao, bo, h), 160)
        return pltpu.make_async_remote_copy(
            src_ref=weights.at[rows, :],
            dst_ref=weights.at[rows, :],
            send_sem=ag_send.at[len(ag_started)],
            recv_sem=ag_recv.at[index],
            device_id=device(step, 0) if ring == 0 else device(0, step),
            device_id_type=MESH,
        )

    def ag_start(ring, step, ao, bo, h):
        copy = ag_copy(ring, step, ao, bo, h)
        copy.start()
        ag_started.append(copy)

    def ag_wait(ring, ao, bo, h):
        offset = ao if ring == 0 else bo
        role = {3: 0, 1: 2, 2: 4}[offset] + h
        index = role if ring == 0 else 6 + ao * 6 + role
        rows = pl.ds(slot_row(ao, bo, h), 160)
        pltpu.make_async_remote_copy(
            src_ref=weights.at[rows, :],
            dst_ref=weights.at[rows, :],
            send_sem=ag_send.at[0],
            recv_sem=ag_recv.at[index],
            device_id=device(1, 0),
            device_id_type=MESH,
        ).wait_recv()

    for k in (4, 3, 5, 2, 6, 1, 7):
        weight_copy(k, 0).wait_send()
    for k in (4, 3, 5, 2, 6, 1, 7):
        weight_copy(k, 1).start()
    load_teacher.wait()
    target_recv[owner] = picked(teacher[...], owner)
    for k in (4, 3, 5, 2, 6, 1, 7):
        peer = (owner + k) % 8
        target_send[peer] = picked(teacher[...], peer)
    load_tokens.wait()
    for h in range(2):
        half = pl.ds(h * 160, 160)
        for k in (0, 4, 3, 5, 2, 6, 1, 7):
            source = (owner - k + 8) % 8
            table = unpack[pl.ds(pl.multiple_of(source * 256, 256), 256), :]
            if k == 0:
                pre[half, :] = jnp.dot(weight_send[owner, half, :], table, preferred_element_type=F32)
                continue
            pltpu.make_async_remote_copy(
                src_ref=weight_recv.at[source, half, :],
                dst_ref=weight_recv.at[source, half, :],
                send_sem=ws_send.at[h * 8 + k],
                recv_sem=ws_recv.at[h * 8 + k],
                device_id=(dp, (owner + k) % 8),
                device_id_type=MESH,
            ).wait_recv()
            pre[half, :] += jnp.dot(weight_recv[source, half, :], table, preferred_element_type=F32)
        weights[pl.ds(slot_row(0, 0, h), 160), :] = pre[half, :].astype(BF16)
        for ring in (0, 1):
            for step in (1, 3):
                ag_start(ring, step, 0, 0, h)
        lax.fori_loop(h * 8, h * 8 + 8, norm, 0)
    for k in (4, 3, 5, 2, 6, 1, 7):
        target_copy(k).start()

    def chunk_copy(index, turn):
        return pltpu.make_async_remote_copy(
            src_ref=packed_x.at[index],
            dst_ref=packed_x.at[index],
            send_sem=px_send.at[turn],
            recv_sem=px_recv.at[turn],
            device_id=(dp, owner + 1 - 2 * core),
            device_id_type=MESH,
        )

    def permute(turn, carry):
        index = (z * 5 + 2 * turn + core) % 20
        slots = lax.broadcasted_iota(jnp.int32, (256, 128), 0) + index * 256
        total = jnp.zeros((512, 256), F32)
        for part in range(4):
            hot = jnp.concatenate(
                [
                    jnp.where(places[r : r + 1, :] == slots, 1.0, 0.0).astype(BF16)
                    for r in range(part * 8, part * 8 + 8)
                ],
                axis=1,
            )
            total += lax.dot_general(
                normed[:, part * 1024 : part * 1024 + 1024], hot, (((1,), (1,)), ((), ())), preferred_element_type=F32
            )
        packed_x[index] = total.astype(BF16)
        chunk_copy(index, turn).start()
        return carry

    def fill(first, last):
        lax.fori_loop(first, last, permute, 0)

    def take_chunks(first, last):
        @pl.loop(first, last)
        def _(turn):
            chunk_copy((z * 5 + 2 * turn + 1 - core) % 20, turn).wait_recv()

    def multiply_group(zo, first, start=0, count=5):
        base = ((z + zo) % 4) * 5

        @pl.loop(0, 2)
        def _(n):
            cols = pl.ds(pl.multiple_of(n * 512, 512), 512)
            part = jnp.zeros((512, 512), F32) if first else pre[:, cols]
            for c in range(count):
                chunk = base + (start + c) % 5
                depth = pl.ds(pl.multiple_of(chunk * 256, 256), 256)
                part += jnp.dot(packed_x[chunk], weights[depth, cols], preferred_element_type=F32)
            pre[:, cols] = part

    def relay(ring, ao, bo, h):
        ag_wait(ring, ao, bo, h)
        far = ao if ring == 0 else bo
        if far == 3 and h == 0:
            ag_start(ring, 1, ao, bo, h)
        if far == 1 and h == 1:
            ag_start(ring, 3, ao, bo, h)
        if ring == 0:
            ag_start(1, 1, ao, 0, h)
            ag_start(1, 3, ao, 0, h)

    relay(0, 3, 0, 0)
    relay(0, 1, 0, 0)
    relay(1, 0, 3, 0)
    fill(0, 2)
    relay(0, 1, 0, 1)
    relay(0, 3, 0, 1)
    relay(1, 0, 1, 1)
    fill(2, 4)
    relay(0, 2, 0, 0)
    fill(4, 6)
    relay(0, 2, 0, 1)
    relay(1, 3, 3, 0)
    fill(6, 7)
    relay(1, 3, 1, 1)
    relay(1, 1, 3, 0)
    fill(7, 8)
    relay(1, 1, 1, 1)
    fill(8, 10)
    relay(1, 2, 3, 0)

    @pl.loop(0, 16)
    def _(s):
        aa, bb = s // 4, s % 4
        cols = pl.ds(pl.multiple_of((bb * 4 + aa + core * 3 * (aa - bb)) * 256, 256), 256)
        normed_t[pl.ds(pl.multiple_of(s * 256, 256), 256), :] = normed[:, cols].T

    relay(1, 2, 1, 1)

    for k in range(1, 8):
        source = (owner - k + 8) % 8
        pltpu.make_async_remote_copy(
            src_ref=target_recv.at[source],
            dst_ref=target_recv.at[source],
            send_sem=ts_send.at[k],
            recv_sem=ts_recv.at[k],
            device_id=(dp, (owner + k) % 8),
            device_id_type=MESH,
        ).wait_recv()

    @pl.loop(0, 4)
    def _(n):
        cols = pl.ds(pl.multiple_of(n * 256, 256), 256)
        total = jnp.zeros((512, 256), F32)
        for s in range(8):
            total += jnp.dot(target_recv[s], unpack[s * 256 : s * 256 + 256, cols], preferred_element_type=F32)
        target[:, cols] = total.astype(BF16)

    take_chunks(0, 10)
    for bo, h in ((3, 1), (1, 0), (2, 0), (2, 1)):
        ag_wait(1, 0, bo, h)
    multiply_group(0, True)
    for ao in (3, 1, 2):
        ag_wait(1, ao, 3, 1)
    for h in range(2):
        ag_wait(1, 3, 2, h)
    ag_wait(1, 3, 1, 0)
    multiply_group(3, False)
    for ao in (1, 2):
        ag_wait(1, ao, 1, 0)
    for h in range(2):
        ag_wait(1, 1, 2, h)
    multiply_group(1, False)
    late = (x + 2) % 4
    multiply_group(2, False, late + 2, 3)
    for h in range(2):
        ag_wait(1, 2, 2, h)
    multiply_group(2, False, late, 2)

    @pl.loop(0, 32)
    def _(r):
        rows = pl.ds(pl.multiple_of(r * 16, 16), 16)
        active = jnp.maximum(pre[rows, :], 0.0)
        delta[rows, :] = (2.0 * active * (active * active - target[rows, :].astype(F32)) * scale).astype(BF16)

    for copy in ag_started:
        copy.wait_send()
    for k in range(1, 8):
        weight_copy(k, 1).wait_send()
        target_copy(k).wait_send()

    @pl.loop(0, 10)
    def _(turn):
        chunk_copy((z * 5 + 2 * turn + core) % 20, turn).wait_send()

    rs_started = []

    def grad_row(ao, bo, h):
        aa, bb = (a + ao) % 4, (b + bo) % 4
        return pl.multiple_of((aa * 4 + bb) * 256 + h * 128, 128)

    def rs_start(ring, step, ao, bo, h, role):
        index = role if ring == 0 else 6 + ao * 6 + role
        place = ring_a.at[pl.ds(role * 128, 128), :] if ring == 0 else ring_b.at[pl.ds((ao * 6 + role) * 128, 128), :]
        copy = pltpu.make_async_remote_copy(
            src_ref=weights.at[pl.ds(grad_row(ao, bo, h), 128), :],
            dst_ref=place,
            send_sem=rs_send.at[len(rs_started)],
            recv_sem=rs_recv.at[index],
            device_id=device(step, 0) if ring == 0 else device(0, step),
            device_id_type=MESH,
        )
        copy.start()
        rs_started.append(copy)

    def rs_take(ring, ao, role):
        index = role if ring == 0 else 6 + ao * 6 + role
        place = ring_a.at[pl.ds(role * 128, 128), :] if ring == 0 else ring_b.at[pl.ds((ao * 6 + role) * 128, 128), :]
        pltpu.make_async_remote_copy(
            src_ref=place,
            dst_ref=place,
            send_sem=rs_send.at[0],
            recv_sem=rs_recv.at[index],
            device_id=device(1, 0),
            device_id_type=MESH,
        ).wait_recv()
        return place

    def add_into(ao, bo, h, places_in, final=False):
        base = grad_row(ao, bo, h)

        @pl.loop(0, 8)
        def _(r):
            total = weights[pl.ds(base + r * 16, 16), :].astype(F32)
            for place in places_in:
                total += place[pl.ds(pl.multiple_of(r * 16, 16), 16), :].astype(F32)
            if final:
                out_ref[pl.ds(pl.multiple_of(h * 128 + r * 16, 16), 16), :] = total
            else:
                weights[pl.ds(base + r * 16, 16), :] = total.astype(BF16)

    def products(ao, bo, count):
        first = ((a + ao) % 4) * 4 + (b + bo) % 4 if count == 1 else ((a + ao) % 4) * 4
        rows = pl.ds(pl.multiple_of(first * 256, 256), 256 * count)

        @pl.loop(0, 4)
        def _(n):
            cols = pl.ds(pl.multiple_of(n * 256, 256), 256)
            weights[rows, cols] = jnp.dot(
                normed_t[rows, :], delta[:, cols], preferred_element_type=F32
            ).astype(BF16)

    def spread_b(ao, only=None):
        if only in (None, 2):
            rs_start(1, 1, ao, 2, 0, 0)
            rs_start(1, 3, ao, 2, 1, 1)
        if only in (None, 1):
            rs_start(1, 1, ao, 1, 1, 3)
        if only in (None, 3):
            rs_start(1, 3, ao, 3, 0, 4)

    def relay_b(ao):
        add_into(ao, 1, 0, [rs_take(1, ao, 0)])
        rs_start(1, 1, ao, 1, 0, 2)
        add_into(ao, 3, 1, [rs_take(1, ao, 1)])
        rs_start(1, 3, ao, 3, 1, 5)

    def gather_b(ao):
        for h in range(2):
            add_into(ao, 0, h, [rs_take(1, ao, 2 + h), rs_take(1, ao, 4 + h)])

    for bo in (2, 1, 3):
        products(2, bo, 1)
        spread_b(2, bo)
    products(1, 0, 4)
    spread_b(1)
    relay_b(2)
    products(3, 0, 4)
    spread_b(3)
    relay_b(1)
    products(2, 0, 1)
    gather_b(2)
    rs_start(0, 1, 2, 0, 0, 0)
    rs_start(0, 3, 2, 0, 1, 1)
    products(0, 0, 4)
    relay_b(3)
    spread_b(0)
    gather_b(1)
    rs_start(0, 1, 1, 0, 1, 3)
    gather_b(3)
    rs_start(0, 3, 3, 0, 0, 4)
    add_into(1, 0, 0, [rs_take(0, 0, 0)])
    rs_start(0, 1, 1, 0, 0, 2)
    add_into(3, 0, 1, [rs_take(0, 0, 1)])
    rs_start(0, 3, 3, 0, 1, 5)
    relay_b(0)
    for h in range(2):
        add_into(
            0, 0, h,
            [rs_take(1, 0, 2 + h), rs_take(1, 0, 4 + h), rs_take(0, 0, 2 + h), rs_take(0, 0, 4 + h)],
            final=True,
        )
    for copy in rs_started:
        copy.wait_send()


def per_device(tokens_in, teacher_hidden, up_old, gain_old, keep_chan, keep_ff):
    scale = 1.0 / math.sqrt(tokens_in.shape[0] * lax.axis_size("dp"))
    anywhere = pl.BlockSpec(memory_space=pl.ANY)
    vmem = pl.BlockSpec(memory_space=pltpu.VMEM)
    dma = pltpu.SemaphoreType.DMA

    def body(*refs):
        kernel(scale, *refs)

    return pl.pallas_call(
        body,
        out_shape=jax.ShapeDtypeStruct((256, 1024), F32),
        in_specs=[anywhere, anywhere, anywhere, vmem, vmem, vmem],
        out_specs=vmem,
        scratch_shapes=[
            pltpu.VMEM((512, 4096), BF16),
            pltpu.VMEM((4096, 512), BF16),
            pltpu.VMEM((20, 512, 256), BF16),
            pltpu.VMEM((5120, 1024), BF16),
            pltpu.VMEM((512, 1536), BF16),
            pltpu.VMEM((384, 1536), BF16),
            pltpu.VMEM((SLOT_ROWS, 1536), BF16),
            pltpu.VMEM((8, SLOT_ROWS, SLOT_COLS), BF16),
            pltpu.VMEM((8, SLOT_ROWS, SLOT_COLS), BF16),
            pltpu.VMEM((8, 512, SLOT_COLS), BF16),
            pltpu.VMEM((8, 512, SLOT_COLS), BF16),
            pltpu.VMEM((2048, 1024), BF16),
            pltpu.VMEM((2048, 1536), BF16),
            pltpu.VMEM((512, 1024), F32),
            pltpu.VMEM((512, 1024), BF16),
            pltpu.VMEM((512, 1024), BF16),
            pltpu.VMEM((24 * 128, 1024), BF16),
            pltpu.VMEM((6 * 128, 1024), BF16),
            pltpu.VMEM((1, 4096), F32),
            pltpu.VMEM((200, 128), jnp.int32),
            dma((3,)),
            dma((16,)),
            dma((16,)),
            dma((8,)),
            dma((8,)),
            dma((30,)),
            dma((30,)),
            dma((30,)),
            dma((30,)),
            dma((10,)),
            dma((10,)),
        ],
        compiler_params=pltpu.CompilerParams(
            collective_id=0, has_side_effects=True, vmem_limit_bytes=62 * 1024 * 1024
        ),
        cost_estimate=pl.CostEstimate(flops=40_000_000_000, bytes_accessed=10_000_000, transcendentals=0),
    )(
        tokens_in, teacher_hidden, up_old,
        gain_old.reshape(48, 128), keep_chan.reshape(32, 128), keep_ff.reshape(64, 128),
    )


def solution(mesh):
    return jax.shard_map(
        per_device,
        mesh=mesh,
        in_specs=(P("dp", None), P("dp", "tensor"), P("dp", "tensor"), P(), P(), P()),
        out_specs=P("dp", "tensor"),
        check_vma=False,
    )
```

```python
import math

import jax
import jax.numpy as jnp
from jax import lax
from jax.experimental import pallas as pl
from jax.experimental.pallas import tpu as pltpu
from jax.sharding import PartitionSpec as P

MESH = pl.DeviceIdType.MESH
SLOT_ROWS = 320
SLOT_COLS = 256
BF16 = jnp.bfloat16
F32 = jnp.float32


def strict(shape, dim, group):
    rows = lax.broadcasted_iota(jnp.int32, shape, 0)
    cols = lax.broadcasted_iota(jnp.int32, shape, 1)
    ahead = rows < cols if dim == 1 else cols < rows
    same = rows // group == cols // group
    return jnp.where(ahead & same, 1.0, 0.0).astype(BF16)


def ranks_of(hits, group):
    parts = hits.astype(BF16)
    within = jnp.dot(parts, strict((128, 128), 1, 128), preferred_element_type=F32)
    above = jnp.dot(strict((hits.shape[0],) * 2, 0, group), parts, preferred_element_type=F32)
    return within + jnp.sum(above, axis=1, keepdims=True)


def blocks_of(index, width, count):
    block = jnp.zeros_like(index)
    for edge in range(1, count):
        block += jnp.where(index >= edge * width, 1, 0)
    return block


def kernel(
    scale,
    tokens_hbm, teacher_hbm, up_hbm, gain_ref, chan_ref, ff_ref,
    out_ref,
    normed, normed_t, packed_x, weights, teacher, up, kept_rows, weight_send, weight_recv,
    target_send, target_recv, unpack, picks, pre, delta, target, ring_b, ring_a, gain, places,
    local_sems, ws_send, ws_recv, ts_send, ts_recv, ag_send, ag_recv, rs_send, rs_recv, px_send, px_recv,
):
    dp = lax.axis_index("dp")
    owner = lax.axis_index("tensor")
    core = owner % 2
    z, x = dp // 4, dp % 4
    a = x + core * (z - x)
    b = z + core * (x - z)

    def dp_of(ao, bo):
        aa, bb = (a + ao) % 4, (b + bo) % 4
        return bb * 4 + aa + core * 3 * (aa - bb)

    def device(ao, bo):
        return (dp_of(ao, bo), owner)

    load_up = pltpu.make_async_copy(up_hbm, up, local_sems.at[0])
    load_teacher = pltpu.make_async_copy(teacher_hbm, teacher, local_sems.at[1])
    load_tokens = pltpu.make_async_copy(tokens_hbm, normed, local_sems.at[2])
    load_up.start()
    load_teacher.start()
    load_tokens.start()
    barrier = pltpu.get_barrier_semaphore()
    for ao, bo in ((1, 0), (3, 0), (0, 1), (0, 3)):
        pl.semaphore_signal(barrier, inc=1, device_id=device(ao, bo), device_id_type=MESH)
    for k in range(1, 8):
        pl.semaphore_signal(barrier, inc=1, device_id=(dp, (owner + k) % 8), device_id_type=MESH)

    chan = chan_ref[...]
    block = blocks_of(chan, 384, 16)
    block_hits = jnp.concatenate([jnp.where(block == s, 1.0, 0.0) for s in range(16)], axis=0)
    block_ranks = ranks_of(block_hits, 32) * block_hits
    rank = block_ranks[0:32, :]
    for s in range(1, 16):
        rank += block_ranks[32 * s : 32 * s + 32, :]
    rank = rank.astype(jnp.int32)
    places[0:32, :] = block * SLOT_ROWS + rank
    places[32:64, :] = jnp.where(block == dp, rank, -1)

    slots = lax.broadcasted_iota(jnp.int32, (SLOT_ROWS, 128), 0)
    found = jnp.zeros((SLOT_ROWS, 128), jnp.int32)
    for r in range(32):
        found += jnp.where(places[32 + r : 33 + r, :] == slots, chan_ref[r : r + 1, :] - dp * 384 + 1, 0)
    row = jnp.sum(found.astype(F32), axis=1, keepdims=True).astype(jnp.int32) - 1
    hot = jnp.where(lax.broadcasted_iota(jnp.int32, (SLOT_ROWS, 384), 1) == row, 1.0, 0.0).astype(BF16)
    load_up.wait()
    kept_rows[...] = jnp.dot(hot, up[...], preferred_element_type=F32).astype(BF16)

    places[64:128, :] = ff_ref[...] - owner * 1536
    local = places[64:128, :]
    mine = (local >= 0) & (local < 1536)
    slot = ranks_of(jnp.where(mine, 1.0, 0.0), 8).astype(jnp.int32)
    places[128:192, :] = jnp.where(mine, slot, -1)

    def make_pick(o, carry):
        slots = lax.broadcasted_iota(jnp.int32, (SLOT_COLS, 128), 0)
        found = jnp.zeros((SLOT_COLS, 128), jnp.int32)
        for r in range(8):
            found += jnp.where(
                places[pl.ds(128 + o * 8 + r, 1), :] == slots, places[pl.ds(64 + o * 8 + r, 1), :] + 1, 0
            )
        column = jnp.sum(found.astype(F32), axis=1, keepdims=True).astype(jnp.int32) - 1
        hot = jnp.where(lax.broadcasted_iota(jnp.int32, (SLOT_COLS, 1536), 1) == column, 1.0, 0.0)
        picks[pl.ds(pl.multiple_of(o * 256, 256), 256), :] = hot.astype(BF16)
        return carry

    def picked(rows, o):
        pick = picks[pl.ds(pl.multiple_of(o * 256, 256), 256), :]
        return lax.dot_general(
            rows, pick, (((1,), (1,)), ((), ())), preferred_element_type=F32
        ).astype(BF16)

    def weight_copy(k, h):
        peer = (owner + k) % 8
        return pltpu.make_async_remote_copy(
            src_ref=weight_send.at[peer, pl.ds(h * 160, 160), :],
            dst_ref=weight_recv.at[owner, pl.ds(h * 160, 160), :],
            send_sem=ws_send.at[h * 8 + k],
            recv_sem=ws_recv.at[h * 8 + k],
            device_id=(dp, peer),
            device_id_type=MESH,
        )

    def target_copy(k):
        peer = (owner + k) % 8
        return pltpu.make_async_remote_copy(
            src_ref=target_send.at[peer],
            dst_ref=target_recv.at[owner],
            send_sem=ts_send.at[k],
            recv_sem=ts_recv.at[k],
            device_id=(dp, peer),
            device_id_type=MESH,
        )

    pl.semaphore_wait(barrier, 11)

    def pack(i, carry):
        k = 4 + (i + 1) // 2 * (1 - 2 * (i % 2))
        peer = (owner + k) % 8
        make_pick(peer, carry)
        weight_send[peer] = picked(kept_rows[...], peer)
        weight_copy(k, 0).start()
        return carry

    lax.fori_loop(0, 7, pack, 0)
    make_pick(owner, 0)
    weight_send[owner] = picked(kept_rows[...], owner)

    own = ff_ref[pl.ds(pl.multiple_of(owner * 8, 8), 8), :]
    source = blocks_of(own, 1536, 8)
    source_hits = jnp.concatenate([jnp.where(source == s, 1.0, 0.0) for s in range(8)], axis=0)
    source_ranks = ranks_of(source_hits, 8) * source_hits
    arrives = source * SLOT_COLS
    for s in range(8):
        arrives += source_ranks[8 * s : 8 * s + 8, :].astype(jnp.int32)
    places[192:200, :] = arrives

    def make_unpack(s, carry):
        slots = lax.broadcasted_iota(jnp.int32, (256, 128), 0) + s * 256
        for r in range(8):
            hot = jnp.where(places[192 + r : 193 + r, :] == slots, 1.0, 0.0)
            unpack[pl.ds(pl.multiple_of(s * 256, 256), 256), r * 128 : r * 128 + 128] = hot.astype(BF16)
        return carry

    lax.fori_loop(0, 8, make_unpack, 0)

    old = gain_ref[...]
    first = old.astype(BF16)
    second = (old - first.astype(F32)).astype(BF16)
    third = (old - first.astype(F32) - second.astype(F32)).astype(BF16)
    gains = jnp.concatenate([first.astype(F32), second.astype(F32), third.astype(F32)], axis=0).astype(BF16)
    for r in range(32):
        line = chan_ref[r : r + 1, :]
        high = blocks_of(line, 128, 48)
        low = line - high * 128
        hot = jnp.where(lax.broadcasted_iota(jnp.int32, (128, 128), 0) == low, 1.0, 0.0).astype(BF16)
        wide = jnp.dot(gains, hot, preferred_element_type=F32)
        wide = (wide[0:48, :] + wide[48:96, :]) + wide[96:144, :]
        chosen = lax.broadcasted_iota(jnp.int32, (48, 128), 0) == high
        gain[:, r * 128 : r * 128 + 128] = jnp.sum(jnp.where(chosen, wide, 0.0), axis=0, keepdims=True)
    def norm(r, carry):
        rows = pl.ds(pl.multiple_of(r * 32, 32), 32)
        values = normed[rows, :].astype(F32)
        center = jnp.mean(values, axis=1, keepdims=True)
        spread = jnp.mean((values - center) ** 2, axis=1, keepdims=True)
        normed[rows, :] = ((values - center) * lax.rsqrt(spread + 1e-05) * gain[...]).astype(BF16)
        return carry

    def slot_row(ao, bo, h):
        return pl.multiple_of(dp_of(ao, bo) * SLOT_ROWS + h * 160, 32)

    ag_started = []

    def ag_copy(ring, step, ao, bo, h):
        far = (ao if ring == 0 else bo) != 0
        role = (4 + h) if far else ((0 if step == 1 else 2) + h)
        index = role if ring == 0 else 6 + ao * 6 + role
        rows = pl.ds(slot_row(ao, bo, h), 160)
        return pltpu.make_async_remote_copy(
            src_ref=weights.at[rows, :],
            dst_ref=weights.at[rows, :],
            send_sem=ag_send.at[len(ag_started)],
            recv_sem=ag_recv.at[index],
            device_id=device(step, 0) if ring == 0 else device(0, step),
            device_id_type=MESH,
        )

    def ag_start(ring, step, ao, bo, h):
        copy = ag_copy(ring, step, ao, bo, h)
        copy.start()
        ag_started.append(copy)

    def ag_wait(ring, ao, bo, h):
        offset = ao if ring == 0 else bo
        role = {3: 0, 1: 2, 2: 4}[offset] + h
        index = role if ring == 0 else 6 + ao * 6 + role
        rows = pl.ds(slot_row(ao, bo, h), 160)
        pltpu.make_async_remote_copy(
            src_ref=weights.at[rows, :],
            dst_ref=weights.at[rows, :],
            send_sem=ag_send.at[0],
            recv_sem=ag_recv.at[index],
            device_id=device(1, 0),
            device_id_type=MESH,
        ).wait_recv()

    for k in (4, 3, 5, 2, 6, 1, 7):
        weight_copy(k, 0).wait_send()
    for k in (4, 3, 5, 2, 6, 1, 7):
        weight_copy(k, 1).start()
    load_teacher.wait()
    target_recv[owner] = picked(teacher[...], owner)
    for k in (4, 3, 5, 2, 6, 1, 7):
        peer = (owner + k) % 8
        target_send[peer] = picked(teacher[...], peer)
    load_tokens.wait()
    for h in range(2):
        half = pl.ds(h * 160, 160)
        for k in (0, 4, 3, 5, 2, 6, 1, 7):
            source = (owner - k + 8) % 8
            table = unpack[pl.ds(pl.multiple_of(source * 256, 256), 256), :]
            if k == 0:
                pre[half, :] = jnp.dot(weight_send[owner, half, :], table, preferred_element_type=F32)
                continue
            pltpu.make_async_remote_copy(
                src_ref=weight_recv.at[source, half, :],
                dst_ref=weight_recv.at[source, half, :],
                send_sem=ws_send.at[h * 8 + k],
                recv_sem=ws_recv.at[h * 8 + k],
                device_id=(dp, (owner + k) % 8),
                device_id_type=MESH,
            ).wait_recv()
            pre[half, :] += jnp.dot(weight_recv[source, half, :], table, preferred_element_type=F32)
        weights[pl.ds(slot_row(0, 0, h), 160), :] = pre[half, :].astype(BF16)
        for ring in (0, 1):
            for step in (1, 3):
                ag_start(ring, step, 0, 0, h)
        lax.fori_loop(h * 8, h * 8 + 8, norm, 0)
    for k in (4, 3, 5, 2, 6, 1, 7):
        target_copy(k).start()

    def chunk_copy(index, turn):
        return pltpu.make_async_remote_copy(
            src_ref=packed_x.at[index],
            dst_ref=packed_x.at[index],
            send_sem=px_send.at[turn],
            recv_sem=px_recv.at[turn],
            device_id=(dp, owner + 1 - 2 * core),
            device_id_type=MESH,
        )

    def permute(turn, carry):
        index = (z * 5 + 2 * turn + core) % 20
        slots = lax.broadcasted_iota(jnp.int32, (256, 128), 0) + index * 256
        total = jnp.zeros((512, 256), F32)
        for part in range(4):
            hot = jnp.concatenate(
                [
                    jnp.where(places[r : r + 1, :] == slots, 1.0, 0.0).astype(BF16)
                    for r in range(part * 8, part * 8 + 8)
                ],
                axis=1,
            )
            total += lax.dot_general(
                normed[:, part * 1024 : part * 1024 + 1024], hot, (((1,), (1,)), ((), ())), preferred_element_type=F32
            )
        packed_x[index] = total.astype(BF16)
        chunk_copy(index, turn).start()
        return carry

    def fill(first, last):
        lax.fori_loop(first, last, permute, 0)

    def take_chunks(first, last):
        @pl.loop(first, last)
        def _(turn):
            chunk_copy((z * 5 + 2 * turn + 1 - core) % 20, turn).wait_recv()

    def multiply_group(zo, first, start=0, count=5):
        base = ((z + zo) % 4) * 5

        @pl.loop(0, 2)
        def _(n):
            cols = pl.ds(pl.multiple_of(n * 512, 512), 512)
            part = jnp.zeros((512, 512), F32) if first else pre[:, cols]
            for c in range(count):
                chunk = base + (start + c) % 5
                depth = pl.ds(pl.multiple_of(chunk * 256, 256), 256)
                part += jnp.dot(packed_x[chunk], weights[depth, cols], preferred_element_type=F32)
            pre[:, cols] = part

    def relay(ring, ao, bo, h):
        ag_wait(ring, ao, bo, h)
        far = ao if ring == 0 else bo
        if far == 3 and h == 0:
            ag_start(ring, 1, ao, bo, h)
        if far == 1 and h == 1:
            ag_start(ring, 3, ao, bo, h)
        if ring == 0:
            ag_start(1, 1, ao, 0, h)
            ag_start(1, 3, ao, 0, h)

    relay(0, 3, 0, 0)
    relay(0, 1, 0, 0)
    relay(1, 0, 3, 0)
    fill(0, 2)
    relay(0, 1, 0, 1)
    relay(0, 3, 0, 1)
    relay(1, 0, 1, 1)
    fill(2, 4)
    relay(0, 2, 0, 0)
    fill(4, 6)
    relay(0, 2, 0, 1)
    relay(1, 3, 3, 0)
    fill(6, 7)
    relay(1, 3, 1, 1)
    relay(1, 1, 3, 0)
    fill(7, 8)
    relay(1, 1, 1, 1)
    fill(8, 10)
    relay(1, 2, 3, 0)

    @pl.loop(0, 16)
    def _(s):
        aa, bb = s // 4, s % 4
        cols = pl.ds(pl.multiple_of((bb * 4 + aa + core * 3 * (aa - bb)) * 256, 256), 256)
        normed_t[pl.ds(pl.multiple_of(s * 256, 256), 256), :] = normed[:, cols].T

    relay(1, 2, 1, 1)

    for k in range(1, 8):
        source = (owner - k + 8) % 8
        pltpu.make_async_remote_copy(
            src_ref=target_recv.at[source],
            dst_ref=target_recv.at[source],
            send_sem=ts_send.at[k],
            recv_sem=ts_recv.at[k],
            device_id=(dp, (owner + k) % 8),
            device_id_type=MESH,
        ).wait_recv()

    @pl.loop(0, 4)
    def _(n):
        cols = pl.ds(pl.multiple_of(n * 256, 256), 256)
        total = jnp.zeros((512, 256), F32)
        for s in range(8):
            total += jnp.dot(target_recv[s], unpack[s * 256 : s * 256 + 256, cols], preferred_element_type=F32)
        target[:, cols] = total.astype(BF16)

    take_chunks(0, 10)
    for bo, h in ((3, 1), (1, 0), (2, 0), (2, 1)):
        ag_wait(1, 0, bo, h)
    multiply_group(0, True)
    for ao in (3, 1, 2):
        ag_wait(1, ao, 3, 1)
    for h in range(2):
        ag_wait(1, 3, 2, h)
    ag_wait(1, 3, 1, 0)
    multiply_group(3, False)
    for ao in (1, 2):
        ag_wait(1, ao, 1, 0)
    for h in range(2):
        ag_wait(1, 1, 2, h)
    multiply_group(1, False)
    late = (x + 2) % 4
    multiply_group(2, False, late + 2, 3)
    for copy in ag_started[:24]:
        copy.wait_send()
    for h in range(2):
        ag_wait(1, 2, 2, h)
    multiply_group(2, False, late, 2)

    @pl.loop(0, 32)
    def _(r):
        rows = pl.ds(pl.multiple_of(r * 16, 16), 16)
        active = jnp.maximum(pre[rows, :], 0.0)
        delta[rows, :] = (2.0 * active * (active * active - target[rows, :].astype(F32)) * scale).astype(BF16)

    for copy in ag_started[24:]:
        copy.wait_send()

    rs_started = []

    def grad_row(ao, bo, h):
        aa, bb = (a + ao) % 4, (b + bo) % 4
        return pl.multiple_of((aa * 4 + bb) * 256 + h * 128, 128)

    def rs_start(ring, step, ao, bo, h, role):
        index = role if ring == 0 else 6 + ao * 6 + role
        place = ring_a.at[pl.ds(role * 128, 128), :] if ring == 0 else ring_b.at[pl.ds((ao * 6 + role) * 128, 128), :]
        copy = pltpu.make_async_remote_copy(
            src_ref=weights.at[pl.ds(grad_row(ao, bo, h), 128), :],
            dst_ref=place,
            send_sem=rs_send.at[len(rs_started)],
            recv_sem=rs_recv.at[index],
            device_id=device(step, 0) if ring == 0 else device(0, step),
            device_id_type=MESH,
        )
        copy.start()
        rs_started.append(copy)

    def rs_take(ring, ao, role):
        index = role if ring == 0 else 6 + ao * 6 + role
        place = ring_a.at[pl.ds(role * 128, 128), :] if ring == 0 else ring_b.at[pl.ds((ao * 6 + role) * 128, 128), :]
        pltpu.make_async_remote_copy(
            src_ref=place,
            dst_ref=place,
            send_sem=rs_send.at[0],
            recv_sem=rs_recv.at[index],
            device_id=device(1, 0),
            device_id_type=MESH,
        ).wait_recv()
        return place

    def add_into(ao, bo, h, places_in, final=False):
        base = grad_row(ao, bo, h)

        @pl.loop(0, 8)
        def _(r):
            total = weights[pl.ds(base + r * 16, 16), :].astype(F32)
            for place in places_in:
                total += place[pl.ds(pl.multiple_of(r * 16, 16), 16), :].astype(F32)
            if final:
                out_ref[pl.ds(pl.multiple_of(h * 128 + r * 16, 16), 16), :] = total
            else:
                weights[pl.ds(base + r * 16, 16), :] = total.astype(BF16)

    def products(ao, bo, count):
        first = ((a + ao) % 4) * 4 + (b + bo) % 4 if count == 1 else ((a + ao) % 4) * 4
        rows = pl.ds(pl.multiple_of(first * 256, 256), 256 * count)

        @pl.loop(0, 4)
        def _(n):
            cols = pl.ds(pl.multiple_of(n * 256, 256), 256)
            weights[rows, cols] = jnp.dot(
                normed_t[rows, :], delta[:, cols], preferred_element_type=F32
            ).astype(BF16)

    def spread_b(ao, only=None):
        if only in (None, 2):
            rs_start(1, 1, ao, 2, 0, 0)
            rs_start(1, 3, ao, 2, 1, 1)
        if only in (None, 1):
            rs_start(1, 1, ao, 1, 1, 3)
        if only in (None, 3):
            rs_start(1, 3, ao, 3, 0, 4)

    def relay_b(ao):
        add_into(ao, 1, 0, [rs_take(1, ao, 0)])
        rs_start(1, 1, ao, 1, 0, 2)
        add_into(ao, 3, 1, [rs_take(1, ao, 1)])
        rs_start(1, 3, ao, 3, 1, 5)

    def gather_b(ao):
        for h in range(2):
            add_into(ao, 0, h, [rs_take(1, ao, 2 + h), rs_take(1, ao, 4 + h)])

    for bo in (2, 1, 3):
        products(2, bo, 1)
        spread_b(2, bo)
    products(1, 0, 4)
    spread_b(1)
    relay_b(2)
    products(3, 0, 4)
    spread_b(3)
    relay_b(1)
    products(2, 0, 1)
    gather_b(2)
    rs_start(0, 1, 2, 0, 0, 0)
    rs_start(0, 3, 2, 0, 1, 1)
    products(0, 0, 4)
    relay_b(3)
    spread_b(0)
    gather_b(1)
    rs_start(0, 1, 1, 0, 1, 3)
    gather_b(3)
    rs_start(0, 3, 3, 0, 0, 4)
    add_into(1, 0, 0, [rs_take(0, 0, 0)])
    rs_start(0, 1, 1, 0, 0, 2)
    add_into(3, 0, 1, [rs_take(0, 0, 1)])
    rs_start(0, 3, 3, 0, 1, 5)
    relay_b(0)
    for h in range(2):
        add_into(
            0, 0, h,
            [rs_take(1, 0, 2 + h), rs_take(1, 0, 4 + h), rs_take(0, 0, 2 + h), rs_take(0, 0, 4 + h)],
            final=True,
        )
    for copy in rs_started:
        copy.wait_send()
    for k in range(1, 8):
        weight_copy(k, 1).wait_send()
        target_copy(k).wait_send()

    @pl.loop(0, 10)
    def _(turn):
        chunk_copy((z * 5 + 2 * turn + core) % 20, turn).wait_send()


def per_device(tokens_in, teacher_hidden, up_old, gain_old, keep_chan, keep_ff):
    scale = 1.0 / math.sqrt(tokens_in.shape[0] * lax.axis_size("dp"))
    anywhere = pl.BlockSpec(memory_space=pl.ANY)
    vmem = pl.BlockSpec(memory_space=pltpu.VMEM)
    dma = pltpu.SemaphoreType.DMA

    def body(*refs):
        kernel(scale, *refs)

    return pl.pallas_call(
        body,
        out_shape=jax.ShapeDtypeStruct((256, 1024), F32),
        in_specs=[anywhere, anywhere, anywhere, vmem, vmem, vmem],
        out_specs=vmem,
        scratch_shapes=[
            pltpu.VMEM((512, 4096), BF16),
            pltpu.VMEM((4096, 512), BF16),
            pltpu.VMEM((20, 512, 256), BF16),
            pltpu.VMEM((5120, 1024), BF16),
            pltpu.VMEM((512, 1536), BF16),
            pltpu.VMEM((384, 1536), BF16),
            pltpu.VMEM((SLOT_ROWS, 1536), BF16),
            pltpu.VMEM((8, SLOT_ROWS, SLOT_COLS), BF16),
            pltpu.VMEM((8, SLOT_ROWS, SLOT_COLS), BF16),
            pltpu.VMEM((8, 512, SLOT_COLS), BF16),
            pltpu.VMEM((8, 512, SLOT_COLS), BF16),
            pltpu.VMEM((2048, 1024), BF16),
            pltpu.VMEM((2048, 1536), BF16),
            pltpu.VMEM((512, 1024), F32),
            pltpu.VMEM((512, 1024), BF16),
            pltpu.VMEM((512, 1024), BF16),
            pltpu.VMEM((24 * 128, 1024), BF16),
            pltpu.VMEM((6 * 128, 1024), BF16),
            pltpu.VMEM((1, 4096), F32),
            pltpu.VMEM((200, 128), jnp.int32),
            dma((3,)),
            dma((16,)),
            dma((16,)),
            dma((8,)),
            dma((8,)),
            dma((30,)),
            dma((30,)),
            dma((30,)),
            dma((30,)),
            dma((10,)),
            dma((10,)),
        ],
        compiler_params=pltpu.CompilerParams(
            collective_id=0, has_side_effects=True, vmem_limit_bytes=62 * 1024 * 1024
        ),
        cost_estimate=pl.CostEstimate(flops=40_000_000_000, bytes_accessed=10_000_000, transcendentals=0),
    )(
        tokens_in, teacher_hidden, up_old,
        gain_old.reshape(48, 128), keep_chan.reshape(32, 128), keep_ff.reshape(64, 128),
    )


def solution(mesh):
    return jax.shard_map(
        per_device,
        mesh=mesh,
        in_specs=(P("dp", None), P("dp", "tensor"), P("dp", "tensor"), P(), P(), P()),
        out_specs=P("dp", "tensor"),
        check_vma=False,
    )
```
